32 devices in a mesh: tok: 8 (over z, x), head: 4 (over y, core).
Axes of the slice: x: 2, y: 2, z: 4, core: 2. Of those that a mesh axis runs over, the one named last changes fastest.
Arguments:
- tokens_in: bfloat16 [5, 32, 14, 14, 384], P(None, ('tok', 'head')), may hold values from -6 to 6
- cotangent: bfloat16 [5, 32, 14, 14, 384], P(None, ('tok', 'head')), may hold values from -6 to 6
- route: int32 [5, 32, 4], P(None, 'tok'), may hold values from -1 to 15, as said below
- extent: int32 [5, 32, 2], P(None, 'tok'), may hold values from 7 to 14, as said below
- qkv_weight: float32 [3, 384, 384], P(None, 'tok', 'head'), may hold values from -0.15625 to 0.15625
- proj_weight: float32 [384, 384], P('head', 'tok'), may hold values from -0.875 to 0.875
- fc1_weight: float32 [384, 1536], P('tok', 'head'), may hold values from -0.15625 to 0.15625
- fc2_weight: float32 [1536, 384], P('head', 'tok'), may hold values from -0.21875 to 0.21875
- vectors: float32 [12, 384], replicated
- rel_table: float32 [169, 12], replicated, may hold values from -5 to 5
- qkv_first: float32 [3, 384, 384], P(None, 'tok', 'head'), may hold values from -6.1035156e-05 to 6.1035156e-05
- proj_first: float32 [384, 384], P('head', 'tok'), may hold values from -6.1035156e-05 to 6.1035156e-05
- fc1_first: float32 [384, 1536], P('tok', 'head'), may hold values from -6.1035156e-05 to 6.1035156e-05
- fc2_first: float32 [1536, 384], P('head', 'tok'), may hold values from -6.1035156e-05 to 6.1035156e-05
- vectors_first: float32 [12, 384], replicated, may hold values from -6.1035156e-05 to 6.1035156e-05
- table_first: float32 [169, 12], replicated, may hold values from -6.1035156e-05 to 6.1035156e-05
- qkv_second: float32 [3, 384, 384], P(None, 'tok', 'head'), may hold values from 7.064254e-13 to 1.1302807e-11
- proj_second: float32 [384, 384], P('head', 'tok'), may hold values from 7.064254e-13 to 1.1302807e-11
- fc1_second: float32 [384, 1536], P('tok', 'head'), may hold values from 7.064254e-13 to 1.1302807e-11
- fc2_second: float32 [1536, 384], P('head', 'tok'), may hold values from 7.064254e-13 to 1.1302807e-11
- vectors_second: float32 [12, 384], replicated, may hold values from 7.064254e-13 to 1.1302807e-11
- table_second: float32 [169, 12], replicated, may hold values from 7.064254e-13 to 1.1302807e-11
Outputs:
- block_out: bfloat16 [5, 32, 14, 14, 384], P(None, ('tok', 'head'))
- grad_in: bfloat16 [5, 32, 14, 14, 384], P(None, ('tok', 'head'))
- grad_norm: float32 [], replicated
- qkv_new: float32 [3, 384, 384], P(None, 'tok', 'head')
- qkv_first_new: float32 [3, 384, 384], P(None, 'tok', 'head')
- qkv_second_new: float32 [3, 384, 384], P(None, 'tok', 'head')
- proj_new: float32 [384, 384], P('head', 'tok')
- proj_first_new: float32 [384, 384], P('head', 'tok')
- proj_second_new: float32 [384, 384], P('head', 'tok')
- fc1_new: float32 [384, 1536], P('tok', 'head')
- fc1_first_new: float32 [384, 1536], P('tok', 'head')
- fc1_second_new: float32 [384, 1536], P('tok', 'head')
- fc2_new: float32 [1536, 384], P('head', 'tok')
- fc2_first_new: float32 [1536, 384], P('head', 'tok')
- fc2_second_new: float32 [1536, 384], P('head', 'tok')
- vectors_new: float32 [12, 384], replicated
- vectors_first_new: float32 [12, 384], replicated
- vectors_second_new: float32 [12, 384], replicated
- table_new: float32 [169, 12], replicated
- table_first_new: float32 [169, 12], replicated
- table_second_new: float32 [169, 12], replicated
The draws below stay inside these ranges and needn't reach their ends.
Inputs may be any that keep to these rules, and one draw needn't show every extreme that they name: `route`: for every window of the rolled partition (images in order, windows row by row): -1 exactly when the window holds no valid patch, otherwise destination * 2 + slot with destination an index along tok and slot below 2. Among the windows of the images that share an index along tok no value repeats, so a device receives at most 2 windows from one group, and in every micro-batch each group fills all 2 slots of some device. `extent`: valid patches of an image are the rows below its first entry and the columns below its second; the rest is padding.
All inputs are finite; a program needn't handle non-finite values.
Results may differ from the reference program's by a relative error of at most 0.012.
The reference program's roundings to bfloat16 on the way count: a program that leaves them out, or rounds other values in their place, can miss the bound.
Values may be sent and summed in bfloat16 or wider, within the bound.
No kernel may reach another device: no remote copies, remote signals or barrier semaphores. Data moves between devices by JAX's collectives and lax.ppermute only.
A program may use at most 256 MiB of HBM per device.

```python
import math
import jax
import jax.numpy as jnp
from jax import lax

C = 384
NH = 12
HD = 32
FF = 1536
WS = 7
SHIFT = 3
STEP = 10
MICRO = 5
GRID = 14
IMAGES = 32
GROUPS = 8
WPI = 4
GROUP_WIN = 16
CAP = 2
VEC_ROWS = 12
REL = 169
PATCHES = 31360
N_HEAD = 4


def image_extents(key):
    sizes = jax.random.randint(jax.random.fold_in(key, 17), (MICRO, IMAGES, 2), GRID // 2, GRID + 1)
    sizes = sizes.at[:, 0, :].set(GRID)
    return sizes.at[:, 1, :].set(GRID // 2)


def draw_extent(key, part):
    sizes = image_extents(key)
    return sizes


def draw_route(key, part):
    sizes = image_extents(key)
    key = jax.random.fold_in(key, 2)
    side = GRID // WS
    position = jnp.arange(GRID)
    source_pos = (position + SHIFT) % GRID
    rows_inside = source_pos[None, None, :] < sizes[:, :, 0:1]
    cols_inside = source_pos[None, None, :] < sizes[:, :, 1:2]
    band_rows = jnp.any(rows_inside.reshape(MICRO, IMAGES, side, WS), axis=-1)
    band_cols = jnp.any(cols_inside.reshape(MICRO, IMAGES, side, WS), axis=-1)
    live = (band_rows[:, :, :, None] & band_cols[:, :, None, :]).reshape(MICRO, GROUPS, GROUP_WIN).astype(jnp.int32)
    order_keys = jax.random.split(jax.random.fold_in(key, 5), MICRO * GROUPS)
    orders = jax.vmap(lambda single: jax.random.permutation(single, GROUP_WIN))(order_keys).reshape(MICRO, GROUPS, GROUP_WIN)
    live_sorted = jnp.take_along_axis(live, orders, axis=-1)
    ranks_sorted = jnp.cumsum(live_sorted, axis=-1) - live_sorted
    inverse = jnp.argsort(orders, axis=-1, stable=True)
    ranks = jnp.take_along_axis(ranks_sorted, inverse, axis=-1)
    target_keys = jax.random.split(jax.random.fold_in(key, 7), MICRO * GROUPS)
    targets = jax.vmap(lambda single: jax.random.permutation(single, GROUPS))(target_keys).reshape(MICRO, GROUPS, GROUPS)
    chosen = jnp.take_along_axis(targets, ranks // CAP, axis=-1)
    routed = jnp.where(live > 0, chosen * CAP + ranks % CAP, -1)
    return routed.reshape(MICRO, IMAGES, WPI).astype(jnp.int32)


def draw_vectors(key, part):
    key = jax.random.fold_in(key, 3)
    keys = jax.random.split(key, 2)
    ramp = jnp.arange(C, dtype=jnp.float32) / (C - 1)
    rise = 1.0 + 2.0 * ramp
    noise = 0.1 * jax.random.normal(keys[0], (2, C))
    others = 0.4 * jax.random.normal(keys[1], (VEC_ROWS - 2, C))
    gains = rise[None] * (1.0 + noise)
    return jnp.concatenate([gains[0:1], others[0:4], gains[1:2], others[4:]], axis=0).astype(jnp.float32)


def shard_levels(own_key, dims, pieces, smallest, high):
    loudness, own = 1.0, jax.random.fold_in(own_key, 6)
    for dim, parts in pieces:
        heights = jnp.exp(jax.random.uniform(jax.random.fold_in(own, dim), (parts,), jnp.float32, smallest / len(pieces), high / len(pieces)))
        loudness = loudness * jnp.repeat(heights, dims[dim] // parts).reshape([-1 if axis == dim else 1 for axis in range(len(dims))])
    return loudness


def gaussian(stream_key, shape, scale, bound, cuts=(), kind=jnp.bfloat16):
    array = jax.random.normal(stream_key, shape, jnp.float32) * scale
    if len(cuts) > 0:
        array = shard_levels(stream_key, shape, cuts, -0.22, 0.18) * array
    return jnp.clip(array, min=-bound, max=bound).astype(kind)


def setup_inputs(seed: int = 0) -> dict:
    seeds = jax.random.split(jax.random.key(seed), 23)
    tokens_in = gaussian(seeds[0], (MICRO, IMAGES, GRID, GRID, C), 1.0, 6.0, ((1, 32),))
    cotangent = gaussian(seeds[1], (MICRO, IMAGES, GRID, GRID, C), 1.0, 6.0, ((1, 32),))
    route = draw_route(jax.random.fold_in(seeds[22], 71), 0)
    extent = draw_extent(jax.random.fold_in(seeds[22], 71), 0)
    qkv_weight = gaussian(seeds[4], (3, C, C), (4 * C) ** -0.5, 0.15625, ((1, 8), (2, 4)), jnp.float32)
    proj_weight = gaussian(seeds[5], (C, C), (C // 8) ** -0.5, 0.875, ((0, 4), (1, 8)), jnp.float32)
    fc1_weight = gaussian(seeds[6], (C, FF), (4 * C) ** -0.5, 0.15625, ((0, 8), (1, 4)), jnp.float32)
    fc2_weight = gaussian(seeds[7], (FF, C), (FF // 2) ** -0.5, 0.21875, ((0, 4), (1, 8)), jnp.float32)
    vectors = draw_vectors(jax.random.fold_in(seeds[22], 71), 0)
    rel_table = gaussian(seeds[9], (REL, NH), 1.0, 5.0, (), jnp.float32)
    qkv_first = gaussian(seeds[10], (3, C, C), (0.0055 * (4 * C * C + 2 * C * FF) ** -0.5), 6.103515625e-05, ((1, 8), (2, 4)), jnp.float32)
    proj_first = gaussian(seeds[11], (C, C), (0.0055 * (4 * C * C + 2 * C * FF) ** -0.5), 6.103515625e-05, ((0, 4), (1, 8)), jnp.float32)
    fc1_first = gaussian(seeds[12], (C, FF), (0.0055 * (4 * C * C + 2 * C * FF) ** -0.5), 6.103515625e-05, ((0, 8), (1, 4)), jnp.float32)
    fc2_first = gaussian(seeds[13], (FF, C), (0.0055 * (4 * C * C + 2 * C * FF) ** -0.5), 6.103515625e-05, ((0, 4), (1, 8)), jnp.float32)
    vectors_first = gaussian(seeds[14], (VEC_ROWS, C), (0.0055 * (4 * C * C + 2 * C * FF) ** -0.5), 6.103515625e-05, (), jnp.float32)
    table_first = gaussian(seeds[15], (REL, NH), (0.0055 * (4 * C * C + 2 * C * FF) ** -0.5), 6.103515625e-05, (), jnp.float32)
    qkv_second = jnp.clip(jnp.exp(math.log(1.1302806780799646e-11) - 2.7725887 * jax.random.uniform(seeds[16], (3, C, C), jnp.float32) ** shard_levels(seeds[16], (3, C, C), ((1, 8), (2, 4)), -0.2, 0.2)), 7.064254237999779e-13, 1.1302806780799646e-11)
    proj_second = jnp.clip(jnp.exp(math.log(1.1302806780799646e-11) - 2.7725887 * jax.random.uniform(seeds[17], (C, C), jnp.float32) ** shard_levels(seeds[17], (C, C), ((0, 4), (1, 8)), -0.2, 0.2)), 7.064254237999779e-13, 1.1302806780799646e-11)
    fc1_second = jnp.clip(jnp.exp(math.log(1.1302806780799646e-11) - 2.7725887 * jax.random.uniform(seeds[18], (C, FF), jnp.float32) ** shard_levels(seeds[18], (C, FF), ((0, 8), (1, 4)), -0.2, 0.2)), 7.064254237999779e-13, 1.1302806780799646e-11)
    fc2_second = jnp.clip(jnp.exp(math.log(1.1302806780799646e-11) - 2.7725887 * jax.random.uniform(seeds[19], (FF, C), jnp.float32) ** shard_levels(seeds[19], (FF, C), ((0, 4), (1, 8)), -0.2, 0.2)), 7.064254237999779e-13, 1.1302806780799646e-11)
    vectors_second = jnp.clip(jnp.exp(jax.random.uniform(seeds[20], (VEC_ROWS, C), jnp.float32, math.log(7.064254237999779e-13), math.log(1.1302806780799646e-11))), 7.064254237999779e-13, 1.1302806780799646e-11)
    table_second = jnp.clip(jnp.exp(jax.random.uniform(seeds[21], (REL, NH), jnp.float32, math.log(7.064254237999779e-13), math.log(1.1302806780799646e-11))), 7.064254237999779e-13, 1.1302806780799646e-11)
    return dict(tokens_in=tokens_in, cotangent=cotangent, route=route, extent=extent, qkv_weight=qkv_weight, proj_weight=proj_weight, fc1_weight=fc1_weight, fc2_weight=fc2_weight, vectors=vectors, rel_table=rel_table, qkv_first=qkv_first, proj_first=proj_first, fc1_first=fc1_first, fc2_first=fc2_first, vectors_first=vectors_first, table_first=table_first, qkv_second=qkv_second, proj_second=proj_second, fc1_second=fc1_second, fc2_second=fc2_second, vectors_second=vectors_second, table_second=table_second)


EPS_NORM = 1e-05
BETA_ONE = 0.9
BETA_TWO = 0.999
ADAM_EPS = 1e-08
RATE_MATRIX = 0.08
RATE_VECTOR = 1.0
DECAY_MATRIX = 0.05
CLIP_NORM = 0.05
NEG_FILL = -1e+30
HIGH = lax.Precision.HIGHEST

@jax.custom_vjp
def low(v):
    return lax.optimization_barrier(v.astype(jnp.bfloat16)).astype(jnp.float32)

@jax.custom_vjp
def low_back(v):
    return v

def low_keep(v):
    return (low(v), None)

def low_pass(kept, grad):
    return (grad,)

def back_keep(v):
    return (v, None)

def back_low(kept, grad):
    return (low(grad),)
low.defvjp(low_keep, low_pass)
low_back.defvjp(back_keep, back_low)

def layer_norm(rows, gain, shift):
    average = lax.optimization_barrier(jnp.mean(rows, axis=-1, keepdims=True))
    centered = rows - average
    spread = lax.optimization_barrier(jnp.mean(centered * centered, axis=-1, keepdims=True))
    return centered * lax.rsqrt(spread + EPS_NORM) * gain + shift

def to_windows(grid):
    images = grid.shape[0]
    features = grid.shape[3]
    side = grid.shape[1] // WS
    rolled = jnp.roll(grid, (-SHIFT, -SHIFT), axis=(1, 2))
    blocks = rolled.reshape(images, side, WS, side, WS, features).transpose(0, 1, 3, 2, 4, 5)
    return blocks.reshape(images * side * side, WS * WS, features)

def from_windows(windows, images):
    side = GRID // WS
    features = windows.shape[-1]
    blocks = windows.reshape(images, side, side, WS, WS, features).transpose(0, 1, 3, 2, 4, 5)
    return jnp.roll(blocks.reshape(images, GRID, GRID, features), (SHIFT, SHIFT), axis=(1, 2))

def patch_labels(extent_rows):
    position = jnp.arange(GRID)
    source_pos = (position + SHIFT) % GRID
    region_band = jnp.where(position < GRID - WS, 0, jnp.where(position < GRID - SHIFT, 1, 2))
    region = region_band[:, None] * 3 + region_band[None, :] + 1
    rows_inside = source_pos[None, :] < extent_rows[:, 0:1]
    cols_inside = source_pos[None, :] < extent_rows[:, 1:2]
    inside = rows_inside[:, :, None] & cols_inside[:, None, :]
    return jnp.where(inside, region[None], 0).astype(jnp.float32)

def valid_patches(extent_rows):
    position = jnp.arange(GRID)
    rows_inside = position[None, :] < extent_rows[:, 0:1]
    cols_inside = position[None, :] < extent_rows[:, 1:2]
    return (rows_inside[:, :, None] & cols_inside[:, None, :]).astype(jnp.float32)

def relative_index():
    cell_pos = jnp.arange(WS * WS)
    cell_row = cell_pos // WS
    cell_col = cell_pos % WS
    return (cell_row[:, None] - cell_row[None, :] + WS - 1) * (2 * WS - 1) + cell_col[:, None] - cell_col[None, :] + WS - 1

def window_attention(packed, labels, rel_table):
    windows = packed.shape[0]
    cells = WS * WS
    split_heads = packed.reshape(windows, cells, 3, NH, HD)
    queries = split_heads[:, :, 0]
    key_part = split_heads[:, :, 1]
    values = split_heads[:, :, 2]
    scores = jnp.einsum('wqhd,wkhd->whqk', queries, key_part, precision=HIGH) * HD ** (-0.5)
    bias_term = jnp.transpose(rel_table[relative_index()], (2, 0, 1))
    scores = low_back(scores + bias_term[None])
    same = (labels[:, :, None] == labels[:, None, :]) & (labels[:, None, :] > 0)
    allowed = same | jnp.eye(cells, dtype=bool)[None]
    scores = jnp.where(allowed[:, None], scores, NEG_FILL)
    weights_soft = low(jax.nn.softmax(scores, axis=-1))
    result = jnp.einsum('whqk,wkhd->wqhd', weights_soft, values, precision=HIGH)
    return low_back(low(result.reshape(windows, cells, C)))

def block(images, route_rows, extent_rows, qkv_weight, proj_weight, fc1_weight, fc2_weight, vectors, rel_table):
    count = images.shape[0]
    tokens = images.reshape(count * GRID * GRID, C)
    normed_one = low(layer_norm(tokens, vectors[0], vectors[1]))
    qkv_bias = jnp.stack([vectors[2], jnp.zeros_like(vectors[2]), vectors[3]])
    packed = jnp.einsum('nc,wcd->nwd', normed_one, low(qkv_weight), precision=HIGH) + qkv_bias[None]
    packed = low_back(low(packed.reshape(-1, 3 * C)))
    windows = to_windows(packed.reshape(count, GRID, GRID, 3 * C))
    labels = to_windows(patch_labels(extent_rows)[..., None])[..., 0]
    attended = window_attention(windows, labels, rel_table)
    keep = (route_rows.reshape(-1) >= 0).astype(jnp.float32)
    attended = from_windows(attended * keep[:, None, None], count) * valid_patches(extent_rows)[..., None]
    projected = low_back(jnp.dot(attended.reshape(-1, C), low(proj_weight), precision=HIGH)) + vectors[4]
    middle = tokens + projected
    normed_two = low(layer_norm(middle, vectors[5], vectors[6]))
    fc1_bias = vectors[8:].reshape(FF)
    hidden_in = low_back(jnp.dot(normed_two, low(fc1_weight), precision=HIGH)) + fc1_bias
    hidden_out = low(jax.nn.gelu(hidden_in, approximate=False))
    down = low_back(jnp.dot(hidden_out, low(fc2_weight), precision=HIGH)) + vectors[7]
    return (middle + down).reshape(images.shape)

def adam_update(weight, first, second, gradient, rate, decay):
    first_new = BETA_ONE * first + (1.0 - BETA_ONE) * gradient
    second_new = BETA_TWO * second + (1.0 - BETA_TWO) * gradient * gradient
    first_hat = first_new / (1.0 - BETA_ONE ** STEP)
    second_hat = second_new / (1.0 - BETA_TWO ** STEP)
    weight_new = weight * (1.0 - rate * decay) - rate * first_hat / (jnp.sqrt(second_hat) + ADAM_EPS)
    return (weight_new, first_new, second_new)

def reference(tokens_in, cotangent, route, extent, qkv_weight, proj_weight, fc1_weight, fc2_weight, vectors, rel_table, qkv_first, proj_first, fc1_first, fc2_first, vectors_first, table_first, qkv_second, proj_second, fc1_second, fc2_second, vectors_second, table_second):
    params = (qkv_weight, proj_weight, fc1_weight, fc2_weight, vectors, rel_table)
    groups = MICRO * IMAGES // N_HEAD
    inputs_all = tokens_in.reshape(groups, N_HEAD, GRID, GRID, C)
    grads_all = cotangent.reshape(groups, N_HEAD, GRID, GRID, C)
    routes_all = route.reshape(groups, N_HEAD, WPI)
    extents_all = extent.reshape(groups, N_HEAD, 2)

    def one_group(totals, inputs):
        images, grads_out, route_rows, extent_rows = inputs

        def forward(images_in, *weights):
            return block(images_in, route_rows, extent_rows, *weights)
        result, pullback = jax.vjp(forward, images.astype(jnp.float32), *params)
        grads = pullback(grads_out.astype(jnp.float32))
        totals = tuple((summed + added for summed, added in zip(totals, grads[1:])))
        return (totals, (result.astype(jnp.bfloat16), grads[0].astype(jnp.bfloat16)))
    starts = tuple((jnp.zeros_like(member) for member in params))
    totals, (results, grads_in) = lax.scan(one_group, starts, (inputs_all, grads_all, routes_all, extents_all))
    gradients = tuple((member / PATCHES for member in totals))
    squares = jnp.float32(0.0)
    for member in gradients:
        squares = squares + jnp.sum(member * member)
    grad_norm = jnp.sqrt(squares)
    factor = jnp.minimum(1.0, CLIP_NORM / (grad_norm + 1e-06))
    firsts = (qkv_first, proj_first, fc1_first, fc2_first, vectors_first, table_first)
    seconds = (qkv_second, proj_second, fc1_second, fc2_second, vectors_second, table_second)
    rates = (RATE_MATRIX, RATE_MATRIX, RATE_MATRIX, RATE_MATRIX, RATE_VECTOR, RATE_VECTOR)
    decays = (DECAY_MATRIX, DECAY_MATRIX, DECAY_MATRIX, DECAY_MATRIX, 0.0, 0.0)
    updated = [adam_update(params[index], firsts[index], seconds[index], gradients[index] * factor, rates[index], decays[index]) for index in range(6)]
    return (results.reshape(tokens_in.shape), grads_in.reshape(tokens_in.shape), grad_norm, updated[0][0], updated[0][1], updated[0][2], updated[1][0], updated[1][1], updated[1][2], updated[2][0], updated[2][1], updated[2][2], updated[3][0], updated[3][1], updated[3][2], updated[4][0], updated[4][1], updated[4][2], updated[5][0], updated[5][1], updated[5][2])
```

```python
import math

import jax
import jax.numpy as jnp
from jax import lax
from jax.sharding import PartitionSpec as P

C = 384
HD = 32
FF = 1536
WS = 7
SHIFT = 3
STEP = 10
GRID = 14


EPS_NORM = 1e-05
BETA_ONE = 0.9
BETA_TWO = 0.999
ADAM_EPS = 1e-08
RATE_MATRIX = 0.08
RATE_VECTOR = 1.0
DECAY_MATRIX = 0.05
CLIP_NORM = 0.05
NEG_FILL = -1e30
HIGH = lax.Precision.HIGHEST


def layer_norm(rows, gain, shift):
    average = jnp.mean(rows, axis=-1, keepdims=True)
    centered = rows - average
    inverse = lax.rsqrt(jnp.mean(centered * centered, axis=-1, keepdims=True) + EPS_NORM)
    normed = centered * inverse
    return (normed * gain + shift, normed, inverse)


def norm_back(gradient, normed, inverse, gain):
    scaled = gradient * gain
    backward = inverse * (
        scaled
        - jnp.mean(scaled, axis=-1, keepdims=True)
        - normed * jnp.mean(scaled * normed, axis=-1, keepdims=True)
    )
    return (backward, jnp.sum(gradient * normed, axis=0), jnp.sum(gradient, axis=0))


def gelu_value(pre_act):
    return pre_act * 0.5 * (1.0 + lax.erf(pre_act * 2.0 ** (-0.5)))


def gelu_slope(pre_act):
    return 0.5 * (1.0 + lax.erf(pre_act * 2.0 ** (-0.5))) + pre_act * jnp.exp(
        -0.5 * pre_act * pre_act
    ) * (2.0 * math.pi) ** (-0.5)


def to_windows(grid):
    images = grid.shape[0]
    features = grid.shape[3]
    side = grid.shape[1] // WS
    rolled = jnp.roll(grid, (-SHIFT, -SHIFT), axis=(1, 2))
    blocks = rolled.reshape(images, side, WS, side, WS, features).transpose(0, 1, 3, 2, 4, 5)
    return blocks.reshape(images * side * side, WS * WS, features)


def from_windows(windows, images):
    side = GRID // WS
    features = windows.shape[-1]
    blocks = windows.reshape(images, side, side, WS, WS, features).transpose(0, 1, 3, 2, 4, 5)
    return jnp.roll(blocks.reshape(images, GRID, GRID, features), (SHIFT, SHIFT), axis=(1, 2))


def patch_labels(extent_rows):
    position = jnp.arange(GRID)
    source_pos = (position + SHIFT) % GRID
    region_band = jnp.where(position < GRID - WS, 0, jnp.where(position < GRID - SHIFT, 1, 2))
    region = region_band[:, None] * 3 + region_band[None, :] + 1
    rows_inside = source_pos[None, :] < extent_rows[:, 0:1]
    cols_inside = source_pos[None, :] < extent_rows[:, 1:2]
    inside = rows_inside[:, :, None] & cols_inside[:, None, :]
    return jnp.where(inside, region[None], 0).astype(jnp.float32)


def valid_patches(extent_rows):
    position = jnp.arange(GRID)
    rows_inside = position[None, :] < extent_rows[:, 0:1]
    cols_inside = position[None, :] < extent_rows[:, 1:2]
    return rows_inside[:, :, None, None] & cols_inside[:, None, :, None]


def position_lookup():
    cell_pos = jnp.arange(WS * WS)
    cell_row = cell_pos // WS
    cell_col = cell_pos % WS
    offsets = (
        (cell_row[:, None] - cell_row[None, :] + WS - 1) * (2 * WS - 1)
        + cell_col[:, None]
        - cell_col[None, :]
        + WS
        - 1
    )
    return (offsets.reshape(-1)[:, None] == jnp.arange((2 * WS - 1) ** 2)[None, :]).astype(
        jnp.float32
    )


def window_scores(packed, labels, table_cols, lookup):
    windows = packed.shape[0]
    cells = packed.shape[1]
    head_count = table_cols.shape[1]
    split_heads = packed.reshape(windows, cells, 3, head_count, HD)
    queries = split_heads[:, :, 0]
    key_part = split_heads[:, :, 1]
    values = split_heads[:, :, 2]
    bias_term = jnp.dot(lookup, table_cols, precision=HIGH).T.reshape(head_count, cells, cells)
    scores = (
        jnp.einsum("wqhd,wkhd->whqk", queries, key_part, preferred_element_type=jnp.float32)
        * HD ** (-0.5)
        + bias_term[None]
    )
    same = (labels[:, :, None] == labels[:, None, :]) & (labels[:, None, :] > 0)
    allowed = same | jnp.eye(cells, dtype=bool)[None]
    return (jnp.where(allowed[:, None], scores, NEG_FILL), queries, key_part, values)


def attend(packed, labels, table_cols, lookup):
    scores, queries, key_part, values = window_scores(packed, labels, table_cols, lookup)
    peak = jnp.max(scores, axis=-1, keepdims=True)
    exponent = jnp.exp(scores - peak)
    totals = jnp.sum(exponent, axis=-1, keepdims=True)
    weights_soft = (exponent / totals).astype(jnp.bfloat16)
    result = jnp.einsum("whqk,wkhd->wqhd", weights_soft, values, preferred_element_type=jnp.float32)
    return (
        result.reshape(packed.shape[0], packed.shape[1], -1).astype(jnp.bfloat16),
        peak + jnp.log(totals),
    )


def attend_back(packed, labels, table_cols, lookup, log_totals, gradient):
    scores, queries, key_part, values = window_scores(packed, labels, table_cols, lookup)
    windows = packed.shape[0]
    cells = packed.shape[1]
    head_count = table_cols.shape[1]
    weights_soft = jnp.exp(scores - log_totals)
    weights_low = weights_soft.astype(jnp.bfloat16)
    grad_result = gradient.reshape(windows, cells, head_count, HD)
    grad_soft = jnp.einsum(
        "wqhd,wkhd->whqk", grad_result, values, preferred_element_type=jnp.float32
    )
    grad_values = jnp.einsum(
        "whqk,wqhd->wkhd", weights_low, grad_result, preferred_element_type=jnp.float32
    )
    inner = jnp.sum(weights_soft * grad_soft, axis=-1, keepdims=True)
    grad_scores = (weights_soft * (grad_soft - inner)).astype(jnp.bfloat16)
    grad_queries = jnp.einsum(
        "whqk,wkhd->wqhd", grad_scores, key_part, preferred_element_type=jnp.float32
    ) * HD ** (-0.5)
    grad_keys = jnp.einsum(
        "whqk,wqhd->wkhd", grad_scores, queries, preferred_element_type=jnp.float32
    ) * HD ** (-0.5)
    grad_bias = jnp.sum(grad_scores, axis=0, dtype=jnp.float32).reshape(head_count, cells * cells)
    grad_table = jnp.dot(lookup.T, grad_bias.T, precision=HIGH)
    grad_packed = (
        jnp.stack([grad_queries, grad_keys, grad_values], axis=2)
        .reshape(windows, cells, -1)
        .astype(jnp.bfloat16)
    )
    return (grad_packed, grad_table)


def block_pass(x_own, grad_own, route_rows, extent_rows, w_qkv, w_proj, w_fc1, w_fc2, vectors, rel_table, lookup):
    images = x_own.shape[0]
    rows = images * GRID * GRID
    x_rows = x_own.reshape(rows, C)
    g_rows = grad_own.reshape(rows, C)
    zero_low = jnp.zeros((), jnp.bfloat16)
    qkv_bias = jnp.stack([vectors[2], jnp.zeros_like(vectors[2]), vectors[3]])
    fc1_bias = vectors[8:].reshape(-1)
    normed_one, unit_one, inverse_one = layer_norm(x_rows, vectors[0], vectors[1])
    low_one = normed_one.astype(jnp.bfloat16)
    made = jnp.einsum("nc,wcd->nwd", low_one, w_qkv, preferred_element_type=jnp.float32) + qkv_bias[None]
    packed = made.reshape(images, GRID, GRID, 3 * C).astype(jnp.bfloat16)
    labels = to_windows(patch_labels(extent_rows)[..., None])[..., 0]
    windows = to_windows(packed)
    attended, log_totals = attend(windows, labels, rel_table, lookup)
    keep = (route_rows.reshape(-1) >= 0)[:, None, None]
    attended = jnp.where(keep, attended, zero_low)
    valid = valid_patches(extent_rows)
    attn = jnp.where(valid, from_windows(attended, images), zero_low).reshape(rows, C)
    middle = x_rows + jnp.dot(attn, w_proj, preferred_element_type=jnp.float32) + vectors[4]
    normed_two, unit_two, inverse_two = layer_norm(middle, vectors[5], vectors[6])
    low_two = normed_two.astype(jnp.bfloat16)
    hidden_in = jnp.dot(low_two, w_fc1, preferred_element_type=jnp.float32) + fc1_bias
    hidden_out = gelu_value(hidden_in).astype(jnp.bfloat16)
    result = middle + jnp.dot(hidden_out, w_fc2, preferred_element_type=jnp.float32) + vectors[7]
    grad_low = g_rows.astype(jnp.bfloat16)
    grad_pre = jnp.einsum("nc,fc->nf", grad_low, w_fc2, preferred_element_type=jnp.float32) * gelu_slope(hidden_in)
    grad_hidden = grad_pre.astype(jnp.bfloat16)
    grad_fc2 = jnp.einsum("nf,nc->fc", hidden_out, grad_low, preferred_element_type=jnp.float32)
    grad_fc1_shift = jnp.sum(grad_pre, axis=0)
    grad_fc1 = jnp.einsum("nc,nf->cf", low_two, grad_hidden, preferred_element_type=jnp.float32)
    back_two, gain_two, shift_two = norm_back(
        jnp.einsum("nf,cf->nc", grad_hidden, w_fc1, preferred_element_type=jnp.float32), unit_two, inverse_two, vectors[5]
    )
    grad_middle = g_rows + back_two
    middle_low = grad_middle.astype(jnp.bfloat16)
    grad_attn = jnp.einsum("nc,dc->nd", middle_low, w_proj, preferred_element_type=jnp.float32).astype(jnp.bfloat16)
    grad_proj = jnp.einsum("nd,nc->dc", attn, middle_low, preferred_element_type=jnp.float32)
    grad_attn = jnp.where(valid, grad_attn.reshape(images, GRID, GRID, C), zero_low)
    grad_windows = jnp.where(keep, to_windows(grad_attn), zero_low)
    grad_packed, grad_table = attend_back(windows, labels, rel_table, lookup, log_totals, grad_windows)
    grad_rows = from_windows(grad_packed, images).reshape(rows, 3, C)
    grad_qkv = jnp.einsum("nc,nwd->wcd", low_one, grad_rows, preferred_element_type=jnp.float32)
    grad_shift = jnp.sum(grad_rows, axis=0, dtype=jnp.float32)
    back_one, gain_one, shift_one = norm_back(
        jnp.einsum("nwd,wcd->nc", grad_rows, w_qkv, preferred_element_type=jnp.float32), unit_one, inverse_one, vectors[0]
    )
    grad_in = grad_middle + back_one
    vec_grad = jnp.concatenate(
        [
            jnp.stack([gain_one, shift_one, grad_shift[0], grad_shift[2], jnp.sum(grad_middle, axis=0), gain_two, shift_two, jnp.sum(g_rows, axis=0)]),
            grad_fc1_shift.reshape(-1, C),
        ],
        axis=0,
    )
    return (result, grad_in, (grad_qkv, grad_proj, grad_fc1, grad_fc2), vec_grad, grad_table)


def adam_update(weight, first, second, gradient, rate, decay):
    first_new = BETA_ONE * first + (1.0 - BETA_ONE) * gradient
    second_new = BETA_TWO * second + (1.0 - BETA_TWO) * gradient * gradient
    first_hat = first_new / (1.0 - BETA_ONE**STEP)
    second_hat = second_new / (1.0 - BETA_TWO**STEP)
    weight_new = weight * (1.0 - rate * decay) - rate * first_hat / (
        jnp.sqrt(second_hat) + ADAM_EPS
    )
    return (weight_new, first_new, second_new)


def body(
    tokens_in,
    cotangent,
    route,
    extent,
    qkv_weight,
    proj_weight,
    fc1_weight,
    fc2_weight,
    vectors,
    rel_table,
    qkv_first,
    proj_first,
    fc1_first,
    fc2_first,
    vectors_first,
    table_first,
    qkv_second,
    proj_second,
    fc1_second,
    fc2_second,
    vectors_second,
    table_second,
):
    lookup = position_lookup()
    micro_count = tokens_in.shape[0]
    qkv_low = qkv_weight.astype(jnp.bfloat16)
    proj_low = proj_weight.astype(jnp.bfloat16)
    fc1_low = fc1_weight.astype(jnp.bfloat16)
    fc2_low = fc2_weight.astype(jnp.bfloat16)
    def full(low, tok_dim, head_dim):
        return lax.all_gather(lax.all_gather(low, "tok", axis=tok_dim, tiled=True), "head", axis=head_dim, tiled=True)

    def share(total, tok_dim, head_dim):
        part = lax.psum_scatter(total, "head", scatter_dimension=head_dim, tiled=True)
        return lax.psum_scatter(part, "tok", scatter_dimension=tok_dim, tiled=True)

    w_qkv, w_proj, w_fc1, w_fc2 = full(qkv_low, 1, 2), full(proj_low, 1, 0), full(fc1_low, 0, 1), full(fc2_low, 1, 0)
    head_at = lax.axis_index("head")
    result, grad_in, mats, vector_total, table_total = block_pass(
        tokens_in[:, 0].astype(jnp.float32),
        cotangent[:, 0].astype(jnp.float32),
        lax.dynamic_index_in_dim(route, head_at, 1, False),
        lax.dynamic_index_in_dim(extent, head_at, 1, False),
        w_qkv,
        w_proj,
        w_fc1,
        w_fc2,
        vectors,
        rel_table,
        lookup,
    )
    matrix_totals = [share(mats[0], 1, 2), share(mats[1], 1, 0), share(mats[2], 0, 1), share(mats[3], 1, 0)]
    patches = micro_count * lax.axis_size("tok") * lax.axis_size("head") * GRID * GRID
    vector_total, table_total = lax.psum((vector_total, table_total), ("tok", "head"))
    gradients = [member / patches for member in matrix_totals] + [
        vector_total / patches,
        table_total / patches,
    ]
    matrix_squares = jnp.float32(0.0)
    for member in gradients[:4]:
        matrix_squares = matrix_squares + jnp.sum(member * member)
    matrix_squares = lax.psum(matrix_squares, ("tok", "head"))
    grad_norm = jnp.sqrt(
        matrix_squares + jnp.sum(gradients[4] * gradients[4]) + jnp.sum(gradients[5] * gradients[5])
    )
    factor = jnp.minimum(1.0, CLIP_NORM / (grad_norm + 1e-06))
    params = (qkv_weight, proj_weight, fc1_weight, fc2_weight, vectors, rel_table)
    firsts = (qkv_first, proj_first, fc1_first, fc2_first, vectors_first, table_first)
    seconds = (qkv_second, proj_second, fc1_second, fc2_second, vectors_second, table_second)
    rates = (RATE_MATRIX, RATE_MATRIX, RATE_MATRIX, RATE_MATRIX, RATE_VECTOR, RATE_VECTOR)
    decays = (DECAY_MATRIX, DECAY_MATRIX, DECAY_MATRIX, DECAY_MATRIX, 0.0, 0.0)
    updated = [
        adam_update(
            params[index],
            firsts[index],
            seconds[index],
            gradients[index] * factor,
            rates[index],
            decays[index],
        )
        for index in range(6)
    ]
    block_out = result.astype(jnp.bfloat16).reshape(tokens_in.shape)
    grad_block = grad_in.astype(jnp.bfloat16).reshape(tokens_in.shape)
    return (
        block_out,
        grad_block,
        grad_norm,
        updated[0][0],
        updated[0][1],
        updated[0][2],
        updated[1][0],
        updated[1][1],
        updated[1][2],
        updated[2][0],
        updated[2][1],
        updated[2][2],
        updated[3][0],
        updated[3][1],
        updated[3][2],
        updated[4][0],
        updated[4][1],
        updated[4][2],
        updated[5][0],
        updated[5][1],
        updated[5][2],
    )


def solution(mesh):
    return jax.shard_map(
        body,
        mesh=mesh,
        in_specs=(
            P(None, ("tok", "head"), None, None, None),
            P(None, ("tok", "head"), None, None, None),
            P(None, "tok", None),
            P(None, "tok", None),
            P(None, "tok", "head"),
            P("head", "tok"),
            P("tok", "head"),
            P("head", "tok"),
            P(),
            P(),
            P(None, "tok", "head"),
            P("head", "tok"),
            P("tok", "head"),
            P("head", "tok"),
            P(),
            P(),
            P(None, "tok", "head"),
            P("head", "tok"),
            P("tok", "head"),
            P("head", "tok"),
            P(),
            P(),
        ),
        out_specs=(
            P(None, ("tok", "head"), None, None, None),
            P(None, ("tok", "head"), None, None, None),
            P(),
            P(None, "tok", "head"),
            P(None, "tok", "head"),
            P(None, "tok", "head"),
            P("head", "tok"),
            P("head", "tok"),
            P("head", "tok"),
            P("tok", "head"),
            P("tok", "head"),
            P("tok", "head"),
            P("head", "tok"),
            P("head", "tok"),
            P("head", "tok"),
            P(),
            P(),
            P(),
            P(),
            P(),
            P(),
        ),
        check_vma=False,
    )
```

```python
import math

import jax
import jax.numpy as jnp
import numpy as np
from jax import lax
from jax.experimental import pallas as pl
from jax.experimental.pallas import tpu as pltpu
from jax.sharding import PartitionSpec as P

C = 384
NH = 12
HD = 32
FF = 1536
WS = 7
SHIFT = 3
STEP = 10
GRID = 14
CELLS = WS * WS
REL = (2 * WS - 1) ** 2
MICRO = 5

WIN = 64
IMG = 4 * WIN
PAD = 16 * GRID
ROWS = MICRO * IMG
GROUP = 4
GROUPS = NH // GROUP
LANES = GROUP * HD
BLOCKS = 32
PIECE = 48

EPS_NORM = 1e-05
BETA_ONE = 0.9
BETA_TWO = 0.999
ADAM_EPS = 1e-08
RATE_MATRIX = 0.08
RATE_VECTOR = 1.0
DECAY_MATRIX = 0.05
CLIP_NORM = 0.05
NEG_FILL = -1e30
HIGH = lax.Precision.HIGHEST
LOW = jnp.bfloat16
F32 = jnp.float32
NEVER = 99.0
BOTH = ("tok", "head")


def window_tables():
    cell = np.arange(WIN)
    real = cell < CELLS
    rolled_row = np.stack([WS * (w // 2) + cell // WS for w in range(4)])
    rolled_col = np.stack([WS * (w % 2) + cell % WS for w in range(4)])
    source_row = (rolled_row + SHIFT) % GRID
    source_col = (rolled_col + SHIFT) % GRID

    def band(position):
        return np.where(position < GRID - WS, 0, np.where(position < GRID - SHIFT, 1, 2))

    label_row = (rolled_row + SHIFT) % GRID
    label_col = (rolled_col + SHIFT) % GRID
    region = 3 * band(label_row) + band(label_col)
    label_row = (label_row + SHIFT) % GRID
    label_col = (label_col + SHIFT) % GRID
    deal = np.zeros((IMG, PAD), np.float32)
    for w in range(4):
        for c in range(CELLS):
            deal[w * WIN + c, 16 * source_row[w, c] + source_col[w, c]] = 1.0
    place = np.full((2, IMG, 128), NEVER, np.float32)
    place[0] = np.where(real[None], source_row, NEVER).reshape(IMG, 1)
    place[1] = np.where(real[None], source_col, NEVER).reshape(IMG, 1)
    reach = np.full((2, 2, WIN, 128), NEVER, np.float32)
    for pair in range(2):
        for side in range(2):
            w = 2 * pair + side
            same = (region[w][:, None] == region[w][None, :]) & real[:, None] & real[None, :]
            for kind, source in enumerate((label_row, label_col)):
                far = np.where(same, np.maximum(source[w][:, None], source[w][None, :]), NEVER)
                far = np.where(np.eye(WIN, dtype=bool) & real[:, None], -1.0, far)
                reach[pair, kind, :, side * WIN : (side + 1) * WIN] = far
    row, col = cell // WS, cell % WS
    offset = (row[None, :] - row[:, None] + WS - 1) * (2 * WS - 1) + col[None, :] - col[:, None] + WS - 1
    offset = np.where(real[None, :] & real[:, None], offset, -1)
    lookup = (offset.reshape(1, -1) == np.arange(REL)[:, None]).astype(np.float32)
    heads = (np.arange(LANES)[None, :] // HD == np.arange(GROUP)[:, None]).astype(np.float32)
    heads = np.repeat(np.concatenate([heads, heads], axis=1), WIN, axis=0)
    return deal, place, reach, lookup, heads


DEAL, PLACE, REACH, LOOKUP, HEADS = window_tables()


def dot_nn(a, b):
    return lax.dot_general(a, b, (((1,), (0,)), ((), ())), preferred_element_type=F32)


def dot_nt(a, b):
    return lax.dot_general(a, b, (((1,), (1,)), ((), ())), preferred_element_type=F32)


def dot_tn(a, b):
    return lax.dot_general(a, b, (((0,), (0,)), ((), ())), preferred_element_type=F32)


def norm_parts(rows):
    average = jnp.mean(rows, axis=-1, keepdims=True)
    centered = rows - average
    inverse = lax.rsqrt(jnp.mean(centered * centered, axis=-1, keepdims=True) + EPS_NORM)
    return centered * inverse, inverse


def norm_back(gradient, normed, inverse, gain):
    scaled = gradient * gain
    return inverse * (
        scaled
        - jnp.mean(scaled, axis=-1, keepdims=True)
        - normed * jnp.mean(scaled * normed, axis=-1, keepdims=True)
    )


def gelu_parts(pre_act):
    size = jnp.abs(pre_act) * 2.0 ** (-0.5)
    bell = jnp.exp(-size * size)
    t = 1.0 / (1.0 + 0.3275911 * size)
    poly = t * (0.254829592 + t * (-0.284496736 + t * (1.421413741 + t * (-1.453152027 + t * 1.061405429))))
    tail = 0.5 * poly * bell
    return jnp.where(pre_act < 0.0, tail, 1.0 - tail), bell * (2.0 * math.pi) ** (-0.5)


def full(shape):
    zeros = (0,) * len(shape)
    return pl.BlockSpec(shape, lambda i: zeros)


def rows_of(width):
    return pl.BlockSpec((IMG, width), lambda i: (i, 0))


IMAGE = pl.BlockSpec((1, 1, GRID, GRID, C), lambda i: (i, 0, 0, 0, 0))
SCALARS = pl.BlockSpec(memory_space=pltpu.SMEM)


def params(limit=56):
    return pltpu.CompilerParams(vmem_limit_bytes=limit * 1024 * 1024, dimension_semantics=("arbitrary",))


def cost(flops, moved):
    return pl.CostEstimate(flops=int(flops), bytes_accessed=int(moved), transcendentals=0)


def sds(shape, dtype):
    return jax.ShapeDtypeStruct(shape, dtype)


def row_mask(place_ref, extent_ref, route_ref, image):
    parts = []
    for w in range(4):
        rows = slice(w * WIN, (w + 1) * WIN)
        high = jnp.where(route_ref[image, w] >= 0, extent_ref[image, 0], -1).astype(F32)
        wide = extent_ref[image, 1].astype(F32)
        inside = (place_ref[0, rows] < high) & (place_ref[1, rows] < wide)
        parts.append(jnp.where(inside, 1.0, 0.0))
    return jnp.concatenate(parts, axis=0)


def pack_body(qkv_ref, proj_ref, fc1_ref, fc2_ref, near_ref, far_ref):
    near_ref[...] = jnp.concatenate([qkv_ref[0], qkv_ref[1], qkv_ref[2], proj_ref[...]], axis=1).astype(LOW)
    depth = fc1_ref.shape[0]
    far_ref[:depth] = fc1_ref[...].astype(LOW)
    far_ref[depth:] = fc2_ref[...].astype(LOW)


def prep_body(tok_ref, cot_ref, deal_ref, vec_ref, x_ref, g_ref, n_ref, pad):
    @pl.when(pl.program_id(0) == 0)
    def _():
        pad[...] = jnp.zeros_like(pad)

    for source, target in ((cot_ref, g_ref), (tok_ref, x_ref)):
        for r in range(GRID):
            pad[16 * r : 16 * r + GRID, :] = source[0, 0, r]
        rows = dot_nn(deal_ref[...], pad[...])
        target[...] = rows.astype(LOW)
    unit, _ = norm_parts(rows)
    n_ref[...] = (unit * vec_ref[0:1] + vec_ref[1:2]).astype(LOW)


def put_back(rows, deal_ref, target):
    grid = dot_tn(deal_ref[...], rows.astype(LOW)).astype(LOW)
    for r in range(GRID):
        target[0, 0, r] = grid[16 * r : 16 * r + GRID]


def spread_keys(part, heads_ref):
    wide = jnp.concatenate([part[:WIN], part[WIN:]], axis=1)
    return jnp.concatenate([wide] * GROUP, axis=0) * heads_ref[...]


def spread_rows(part):
    zero = jnp.zeros((WIN, LANES), part.dtype)
    top = jnp.concatenate([part[:WIN], zero], axis=1)
    return jnp.concatenate([top, jnp.concatenate([zero, part[WIN:]], axis=1)], axis=0)


def own_rows(product):
    return jnp.concatenate([product[:WIN, :LANES], product[WIN:, LANES:]], axis=0)


def own_keys(product, heads_ref):
    kept = product * heads_ref[...].astype(F32)
    total = kept[:WIN]
    for h in range(1, GROUP):
        total = total + kept[h * WIN : (h + 1) * WIN]
    return jnp.concatenate([total[:, :LANES], total[:, LANES:]], axis=0)


def attend_body(
    order_ref, extent_ref, route_ref, near_ref, x_ref, n_ref, vec_ref, bias_ref, reach_ref, place_ref, heads_ref,
    packed_ref, soft_ref, attn_ref, middle_ref, wq_ref, wp_ref, parts,
):
    image = pl.program_id(0)

    @pl.when(image == 0)
    def _():
        for j in range(BLOCKS):
            at = order_ref[j]
            row = pl.multiple_of((at // 4) * PIECE, PIECE)
            parts[at % 4, pl.ds(row, PIECE), :] = near_ref[j]
        for w in range(3):
            wq_ref[:, w * C : (w + 1) * C] = jnp.concatenate(
                [parts[h, :, w * 96 : (w + 1) * 96] for h in range(4)], axis=1
            )
        wp_ref[...] = jnp.concatenate([parts[h, :, 288:] for h in range(4)], axis=1)

    made = dot_nn(n_ref[...], wq_ref[...])
    packed_ref[:, :C] = (made[:, :C] + vec_ref[2:3]).astype(LOW)
    packed_ref[:, C : 2 * C] = made[:, C : 2 * C].astype(LOW)
    packed_ref[:, 2 * C :] = (made[:, 2 * C :] + vec_ref[3:4]).astype(LOW)
    mask = row_mask(place_ref, extent_ref, route_ref, image)
    high = extent_ref[image, 0].astype(F32)
    wide = extent_ref[image, 1].astype(F32)
    for pair in range(2):
        rows = slice(pair * 2 * WIN, (pair + 1) * 2 * WIN)
        allowed = (reach_ref[pair, 0] < high) & (reach_ref[pair, 1] < wide)
        for g in range(GROUPS):
            at = g * LANES
            queries = packed_ref[rows, at : at + LANES]
            keys = packed_ref[rows, C + at : C + at + LANES]
            values = packed_ref[rows, 2 * C + at : 2 * C + at + LANES]
            raw = dot_nt(spread_keys(keys, heads_ref), spread_rows(queries))
            raw = (raw * HD ** (-0.5) + bias_ref[g]).reshape(GROUP, WIN, 128)
            scores = jnp.where(allowed[None], raw, NEG_FILL)
            exponent = jnp.exp(scores - jnp.max(scores, axis=1, keepdims=True))
            soft = exponent * (1.0 / jnp.sum(exponent, axis=1, keepdims=True))
            soft = soft.reshape(GROUP * WIN, 128)
            soft_ref[0, pair * GROUPS + g] = soft
            result = own_rows(dot_tn(soft.astype(LOW), spread_keys(values, heads_ref)))
            attn_ref[rows, at : at + LANES] = (result * mask[rows]).astype(LOW)
    middle_ref[...] = x_ref[...].astype(F32) + dot_nt(attn_ref[...], wp_ref[...]) + vec_ref[4:5]


def mlp_body(
    order_ref, back_ref, far_ref, middle_ref, g_ref, vec_ref, deal_ref,
    out_ref, grad_ref, keep_ref, send_ref, sums_ref, w1, w2, hidden, grad_hidden, n_turned, g_turned, made, bias,
):
    image = pl.program_id(0)

    @pl.when(image == 0)
    def _():
        for j in range(BLOCKS):
            at = order_ref[j]
            row = pl.multiple_of((at // 4) * PIECE, PIECE)
            col = pl.multiple_of((at % 4) * C, C)
            w1[pl.ds(row, PIECE), pl.ds(col, C)] = far_ref[j, :PIECE]
            w2[pl.ds(row, PIECE), pl.ds(col, C)] = far_ref[j, PIECE:]
        for r in range(4):
            bias[:, r * C : (r + 1) * C] = vec_ref[8 + r : 9 + r]
        sums_ref[...] = jnp.zeros_like(sums_ref)

    rows = pl.ds(pl.multiple_of(image * IMG, IMG), IMG)
    middle = middle_ref[...]
    unit, inverse = norm_parts(middle)
    normed = (unit * vec_ref[5:6] + vec_ref[6:7]).astype(LOW)
    g_low = g_ref[...]
    g = g_low.astype(F32)
    n_turned[:, rows] = normed.T
    g_turned[:, rows] = g_low.T
    for part in range(4):
        cols = slice(part * C, (part + 1) * C)
        pre_act = dot_nn(normed, w1[:, cols]) + bias[:, cols]
        grad_post = dot_nn(g_low, w2[:, cols])
        below, density = gelu_parts(pre_act)
        hidden[rows, cols] = (pre_act * below).astype(LOW)
        grad_pre = grad_post * (below + pre_act * density)
        grad_hidden[rows, cols] = grad_pre.astype(LOW)
        sums_ref[8 + part : 9 + part] += jnp.sum(grad_pre, axis=0, keepdims=True)
    result = middle + dot_nt(hidden[rows, :], w2[...]) + vec_ref[7:8]
    put_back(result, deal_ref, out_ref)
    back = dot_nt(grad_hidden[rows, :], w1[...])
    sums_ref[5:6] += jnp.sum(back * unit, axis=0, keepdims=True)
    sums_ref[6:7] += jnp.sum(back, axis=0, keepdims=True)
    grad_middle = g + norm_back(back, unit, inverse, vec_ref[5:6])
    grad_ref[...] = grad_middle
    sums_ref[4:5] += jnp.sum(grad_middle, axis=0, keepdims=True)
    sums_ref[7:8] += jnp.sum(g, axis=0, keepdims=True)

    @pl.when(image == MICRO - 1)
    def _():
        for part in range(4):
            cols = slice(part * C, (part + 1) * C)
            first = dot_nn(n_turned[...], grad_hidden[:, cols]).astype(LOW)
            second = dot_nn(g_turned[...], hidden[:, cols]).astype(LOW)
            for t in range(8):
                at = back_ref[4 * t + part]
                made[at, :PIECE] = first[t * PIECE : (t + 1) * PIECE]
                made[at, PIECE:] = second[t * PIECE : (t + 1) * PIECE]
        keep_ref[...] = made[: BLOCKS // 2]
        send_ref[...] = made[BLOCKS // 2 :]


def attend_back_body(
    back_ref, extent_ref, route_ref, grad_ref, attn_ref, packed_ref, soft_ref, n_ref, wp_ref, place_ref, heads_ref,
    packed_grad_ref, keep_ref, send_ref, bias_sum_ref, sums_ref, n_turned, g_turned, attn_all, packed_all, made,
):
    image = pl.program_id(0)
    rows_all = pl.ds(pl.multiple_of(image * IMG, IMG), IMG)

    @pl.when(image == 0)
    def _():
        bias_sum_ref[...] = jnp.zeros_like(bias_sum_ref)
        sums_ref[...] = jnp.zeros_like(sums_ref)

    n_turned[:, rows_all] = n_ref[...].T
    grad_low = grad_ref[...].astype(LOW)
    g_turned[:, rows_all] = grad_low.T
    attn_all[rows_all, :] = attn_ref[...]
    mask = row_mask(place_ref, extent_ref, route_ref, image)
    grad_attn = dot_nn(grad_low, wp_ref[...])
    grad_attn = (grad_attn * jnp.concatenate([mask] * 3, axis=1)).astype(LOW)
    for pair in range(2):
        rows = slice(pair * 2 * WIN, (pair + 1) * 2 * WIN)
        for g in range(GROUPS):
            at = g * LANES
            queries = packed_ref[rows, at : at + LANES]
            keys = packed_ref[rows, C + at : C + at + LANES]
            values = packed_ref[rows, 2 * C + at : 2 * C + at + LANES]
            incoming = spread_rows(grad_attn[rows, at : at + LANES])
            soft = soft_ref[0, pair * GROUPS + g]
            grad_soft = dot_nt(spread_keys(values, heads_ref), incoming)
            joint = (soft * grad_soft).reshape(GROUP, WIN, 128)
            inner = jnp.sum(joint, axis=1, keepdims=True)
            grad_scores = (joint - soft.reshape(GROUP, WIN, 128) * inner).reshape(GROUP * WIN, 128)
            grad_low_scores = grad_scores.astype(LOW)
            bias_sum_ref[g] += grad_low_scores.astype(F32)
            grad_values = own_keys(dot_nn(soft.astype(LOW), incoming), heads_ref)
            grad_keys = own_keys(dot_nn(grad_low_scores, spread_rows(queries)), heads_ref)
            grad_queries = own_rows(dot_tn(grad_low_scores, spread_keys(keys, heads_ref)))
            packed_grad_ref[rows, at : at + LANES] = (grad_queries * HD ** (-0.5)).astype(LOW)
            packed_grad_ref[rows, C + at : C + at + LANES] = (grad_keys * HD ** (-0.5)).astype(LOW)
            packed_grad_ref[rows, 2 * C + at : 2 * C + at + LANES] = grad_values.astype(LOW)
    packed_all[rows_all, :] = packed_grad_ref[...]
    sums_ref[0:1] += jnp.sum(packed_grad_ref[:, :C].astype(F32), axis=0, keepdims=True)
    sums_ref[1:2] += jnp.sum(packed_grad_ref[:, 2 * C :].astype(F32), axis=0, keepdims=True)

    @pl.when(image == MICRO - 1)
    def _():
        whole = [dot_nn(n_turned[...], packed_all[:, w * C : (w + 1) * C]).astype(LOW) for w in range(3)]
        whole.append(dot_nn(g_turned[...], attn_all[...]).astype(LOW))
        for h in range(4):
            block = jnp.concatenate([part[:, h * 96 : (h + 1) * 96] for part in whole], axis=1)
            for t in range(8):
                made[back_ref[4 * t + h]] = block[t * PIECE : (t + 1) * PIECE]
        keep_ref[...] = made[: BLOCKS // 2]
        send_ref[...] = made[BLOCKS // 2 :]


def input_body(packed_grad_ref, wq_ref, x_ref, grad_ref, vec_ref, deal_ref, out_ref, sums_ref):
    @pl.when(pl.program_id(0) == 0)
    def _():
        sums_ref[...] = jnp.zeros_like(sums_ref)

    back = dot_nt(packed_grad_ref[...], wq_ref[...])
    unit, inverse = norm_parts(x_ref[...].astype(F32))
    sums_ref[0:1] += jnp.sum(back * unit, axis=0, keepdims=True)
    sums_ref[1:2] += jnp.sum(back, axis=0, keepdims=True)
    put_back(grad_ref[...] + norm_back(back, unit, inverse, vec_ref[0:1]), deal_ref, out_ref)


def adam_update(weight, first, second, gradient, rate, decay):
    first_new = BETA_ONE * first + (1.0 - BETA_ONE) * gradient
    second_new = BETA_TWO * second + (1.0 - BETA_TWO) * gradient * gradient
    first_hat = first_new / (1.0 - BETA_ONE**STEP)
    second_hat = second_new / (1.0 - BETA_TWO**STEP)
    weight_new = weight * (1.0 - rate * decay) - rate * first_hat / (jnp.sqrt(second_hat) + ADAM_EPS)
    return (weight_new, first_new, second_new)


def adam_body(near_ref, far_ref, vec_ref, table_ref, square_ref, *refs):
    olds, news = refs[:18], refs[18:]
    total = square_ref[0:1, 0:1]
    total = total + jnp.sum(jnp.sum(vec_ref[...] * vec_ref[...], axis=1, keepdims=True), axis=0, keepdims=True)
    total = total + jnp.sum(jnp.sum(table_ref[...] * table_ref[...], axis=1, keepdims=True), axis=0, keepdims=True)
    grad_norm = jnp.sqrt(total)
    factor = jnp.minimum(1.0, CLIP_NORM / (grad_norm + 1e-06))
    news[0][...] = grad_norm
    depth = far_ref.shape[0] // 2
    grads = [None, near_ref[:, 288:], far_ref[:depth], far_ref[depth:], vec_ref[...], table_ref[...]]
    for index in range(6):
        weight, first, second = olds[index], olds[6 + index], olds[12 + index]
        rate, decay = (RATE_MATRIX, DECAY_MATRIX) if index < 4 else (RATE_VECTOR, 0.0)
        for w in range(3 if index == 0 else 1):
            pick = (w,) if index == 0 else (Ellipsis,)
            gradient = near_ref[:, w * 96 : (w + 1) * 96] if index == 0 else grads[index]
            made = adam_update(weight[pick], first[pick], second[pick], gradient * factor, rate, decay)
            for kind in range(3):
                news[1 + 3 * index + kind][pick] = made[kind]


def exchange(rows, mask, devices):
    return lax.ppermute(rows, BOTH, [(i, i ^ mask) for i in range(devices)])


def body(
    mesh_sizes, tokens_in, cotangent, route, extent, qkv_weight, proj_weight, fc1_weight, fc2_weight, vectors, rel_table,
    qkv_first, proj_first, fc1_first, fc2_first, vectors_first, table_first,
    qkv_second, proj_second, fc1_second, fc2_second, vectors_second, table_second,
):
    toks, heads = mesh_sizes
    devices = toks * heads
    direct = toks == 8 and heads == 4
    micro = tokens_in.shape[0]
    patches = micro * devices * GRID * GRID
    head_at = lax.axis_index("head")
    me = lax.axis_index("tok") * heads + head_at
    masks = (16, 8, 2, 4, 1)
    counts = np.arange(BLOCKS)
    if direct:
        away = sum(((counts >> bit) & 1) * mask for bit, mask in enumerate(masks))
        order = jnp.bitwise_xor(jnp.asarray(away, jnp.int32), me)
        apart = jnp.bitwise_xor(jnp.asarray(counts, jnp.int32), me)
        backward = sum((((apart & mask) > 0).astype(jnp.int32) << bit) for bit, mask in enumerate(masks))
    else:
        order = jnp.asarray((counts % 8) * 4 + counts // 8, jnp.int32)
        backward = jnp.asarray((counts % 4) * 8 + counts // 4, jnp.int32)
    route_own = lax.dynamic_index_in_dim(route, head_at, 1, False)
    extent_own = lax.dynamic_index_in_dim(extent, head_at, 1, False)

    depth = fc1_weight.shape[0]
    near, far = pl.pallas_call(
        pack_body,
        out_shape=(sds((depth, C), LOW), sds((2 * depth, C), LOW)),
        name="pack",
    )(qkv_weight, proj_weight.T, fc1_weight, fc2_weight.T)

    def gather(piece):
        if not direct:
            spread = lax.all_gather(lax.all_gather(piece, "tok", axis=0), "head", axis=0)
            half = piece.shape[0] // depth
            spread = spread.reshape(heads, toks, half, depth, C).transpose(0, 2, 1, 3, 4)
            spread = spread.reshape(heads, half, 8, PIECE, C).transpose(0, 2, 1, 3, 4)
            return spread.reshape(BLOCKS, half * PIECE, C)
        held = piece[None]
        for mask in masks[:2]:
            held = jnp.concatenate([held, exchange(held, mask, devices)], axis=0)
        held = jnp.concatenate([held] + [exchange(held, mask, devices) for mask in (2, 4, 6)], axis=0)
        return jnp.concatenate([held, exchange(held, masks[4], devices)], axis=0)

    def share(keep, send):
        if not direct:
            both = jnp.concatenate([keep, send], axis=0)
            half = both.shape[1] // PIECE
            both = both.reshape(heads, 8, half, PIECE, C).transpose(0, 2, 1, 3, 4)
            both = both.reshape(heads, half, toks, depth, C).transpose(0, 2, 1, 3, 4).reshape(devices, half * depth, C)
            both = lax.psum_scatter(both.astype(F32), "head", scatter_dimension=0, tiled=True)
            return lax.psum_scatter(both, "tok", scatter_dimension=0, tiled=True)[0]
        held = keep.astype(F32) + exchange(send, masks[4], devices).astype(F32)
        low = held.astype(LOW)
        held = held[:4]
        for place, mask in ((4, 2), (8, 4), (12, 6)):
            held = held + exchange(low[place : place + 4], mask, devices).astype(F32)
        held = held[:2] + exchange(held[2:].astype(LOW), masks[1], devices).astype(F32)
        held = held[:1] + exchange(held[1:].astype(LOW), masks[0], devices).astype(F32)
        return held[0]

    deal = jnp.asarray(DEAL, LOW)
    place = jnp.asarray(PLACE)
    reach = jnp.asarray(REACH)
    heads_low = jnp.asarray(HEADS, LOW)
    x_rows, g_rows, n_rows = pl.pallas_call(
        prep_body,
        grid=(MICRO,),
        in_specs=[IMAGE, IMAGE, full((IMG, PAD)), full((12, C))],
        out_specs=[rows_of(C)] * 3,
        out_shape=[sds((ROWS, C), LOW)] * 3,
        scratch_shapes=[pltpu.VMEM((PAD, C), LOW)],
        compiler_params=params(32),
        cost_estimate=cost(2e9, 6e6),
        name="prep",
    )(tokens_in, cotangent, deal, vectors)

    bias = jnp.dot(rel_table.T, jnp.asarray(LOOKUP), precision=HIGH).reshape(GROUPS, GROUP * WIN, WIN)
    bias = jnp.concatenate([bias, bias], axis=2)

    near_all = gather(near)
    far_all = gather(far)

    packed, soft, attn, middle, w_qkv, w_proj = pl.pallas_call(
        attend_body,
        grid=(MICRO,),
        in_specs=[
            SCALARS, SCALARS, SCALARS, full((BLOCKS, PIECE, C)), rows_of(C), rows_of(C), full((12, C)),
            full((GROUPS, GROUP * WIN, 128)), full((2, 2, WIN, 128)), full((2, IMG, 128)), full((IMG, 256)),
        ],
        out_specs=[
            rows_of(3 * C), pl.BlockSpec((1, 2 * GROUPS, GROUP * WIN, 128), lambda i: (i, 0, 0, 0)), rows_of(C), rows_of(C),
            full((C, 3 * C)), full((C, C)),
        ],
        out_shape=[
            sds((ROWS, 3 * C), LOW), sds((MICRO, 2 * GROUPS, GROUP * WIN, 128), F32), sds((ROWS, C), LOW), sds((ROWS, C), F32),
            sds((C, 3 * C), LOW), sds((C, C), LOW),
        ],
        scratch_shapes=[pltpu.VMEM((4, C, C), LOW)],
        compiler_params=params(),
        cost_estimate=cost(8e9, 12e6),
        name="attend",
    )(order, extent_own, route_own, near_all, x_rows, n_rows, vectors, bias, reach, place, heads_low)

    half = BLOCKS // 2
    block_out, grad_middle, far_keep, far_send, sums_mlp = pl.pallas_call(
        mlp_body,
        grid=(MICRO,),
        in_specs=[SCALARS, SCALARS, full((BLOCKS, 2 * PIECE, C)), rows_of(C), rows_of(C), full((12, C)), full((IMG, PAD))],
        out_specs=[IMAGE, rows_of(C), full((half, 2 * PIECE, C)), full((half, 2 * PIECE, C)), full((12, C))],
        out_shape=[
            sds(tokens_in.shape, LOW), sds((ROWS, C), F32), sds((half, 2 * PIECE, C), LOW), sds((half, 2 * PIECE, C), LOW),
            sds((12, C), F32),
        ],
        scratch_shapes=[
            pltpu.VMEM((C, FF), LOW), pltpu.VMEM((C, FF), LOW), pltpu.VMEM((ROWS, FF), LOW), pltpu.VMEM((ROWS, FF), LOW),
            pltpu.VMEM((C, ROWS), LOW), pltpu.VMEM((C, ROWS), LOW), pltpu.VMEM((BLOCKS, 2 * PIECE, C), LOW),
            pltpu.VMEM((1, FF), F32),
        ],
        compiler_params=params(),
        cost_estimate=cost(20e9, 12e6),
        name="mlp",
    )(order, backward, far_all, middle, g_rows, vectors, deal)

    packed_grad, near_keep, near_send, bias_sum, sums_attend = pl.pallas_call(
        attend_back_body,
        grid=(MICRO,),
        in_specs=[
            SCALARS, SCALARS, SCALARS, rows_of(C), rows_of(C), rows_of(3 * C),
            pl.BlockSpec((1, 2 * GROUPS, GROUP * WIN, 128), lambda i: (i, 0, 0, 0)), rows_of(C), full((C, C)),
            full((2, IMG, 128)), full((IMG, 256)),
        ],
        out_specs=[
            rows_of(3 * C), full((half, PIECE, C)), full((half, PIECE, C)), full((GROUPS, GROUP * WIN, 128)), full((2, C)),
        ],
        out_shape=[
            sds((ROWS, 3 * C), LOW), sds((half, PIECE, C), LOW), sds((half, PIECE, C), LOW),
            sds((GROUPS, GROUP * WIN, 128), F32), sds((2, C), F32),
        ],
        scratch_shapes=[
            pltpu.VMEM((C, ROWS), LOW), pltpu.VMEM((C, ROWS), LOW), pltpu.VMEM((ROWS, C), LOW), pltpu.VMEM((ROWS, 3 * C), LOW),
            pltpu.VMEM((BLOCKS, PIECE, C), LOW),
        ],
        compiler_params=params(),
        cost_estimate=cost(12e9, 12e6),
        name="attend_back",
    )(backward, extent_own, route_own, grad_middle, attn, packed, soft, n_rows, w_proj, place, heads_low)

    grad_block, sums_input = pl.pallas_call(
        input_body,
        grid=(MICRO,),
        in_specs=[rows_of(3 * C), full((C, 3 * C)), rows_of(C), rows_of(C), full((12, C)), full((IMG, PAD))],
        out_specs=[IMAGE, full((2, C))],
        out_shape=[sds(tokens_in.shape, LOW), sds((2, C), F32)],
        compiler_params=params(32),
        cost_estimate=cost(4e9, 8e6),
        name="input_grad",
    )(packed_grad, w_qkv, x_rows, grad_middle, vectors, deal)

    far_grad = share(far_keep, far_send) / patches
    near_grad = share(near_keep, near_send) / patches
    vec_grad = jnp.concatenate([sums_input, sums_attend, sums_mlp[4:]], axis=0)
    bias_sum = (bias_sum[:, :, :WIN] + bias_sum[:, :, WIN:]).reshape(NH, WIN * WIN)
    table_grad = jnp.dot(bias_sum, jnp.asarray(LOOKUP.T), precision=HIGH)
    squares = jnp.sum(near_grad * near_grad) + jnp.sum(far_grad * far_grad)
    if direct:
        spare = jnp.concatenate([vec_grad.reshape(-1), table_grad.reshape(-1)]).reshape(-1, 12)
        for mask in masks[::-1]:
            spare = spare + exchange(spare, mask, devices)
        squares = jnp.broadcast_to(squares, (1, 128))
        for mask in masks[::-1]:
            squares = squares + exchange(squares, mask, devices)
        vec_grad = spare.reshape(-1)[: 12 * C].reshape(12, C)
        table_grad = spare.reshape(-1)[12 * C :].reshape(NH, REL)
    else:
        vec_grad, table_grad, squares = lax.psum((vec_grad, table_grad, squares), BOTH)
        squares = jnp.broadcast_to(squares, (1, 128))
    vec_grad, table_grad = vec_grad / patches, table_grad / patches

    olds = (
        qkv_weight, proj_weight.T, fc1_weight, fc2_weight.T, vectors, rel_table.T,
        qkv_first, proj_first.T, fc1_first, fc2_first.T, vectors_first, table_first.T,
        qkv_second, proj_second.T, fc1_second, fc2_second.T, vectors_second, table_second.T,
    )
    shapes = [sds((1, 1), F32)] + [sds(olds[index].shape, F32) for index in range(6) for _ in range(3)]
    news = pl.pallas_call(
        adam_body,
        out_shape=shapes,
        compiler_params=pltpu.CompilerParams(vmem_limit_bytes=32 * 1024 * 1024),
        name="adam",
    )(near_grad, far_grad, vec_grad, table_grad, squares, *olds)
    turned = [new.T if index // 3 in (1, 3, 5) else new for index, new in enumerate(news[1:])]
    return (block_out, grad_block, news[0][0, 0], *turned)


def solution(mesh):
    sizes = (mesh.shape["tok"], mesh.shape["head"])
    weights = (P(None, "tok", "head"), P("head", "tok"), P("tok", "head"), P("head", "tok"), P(), P())
    images = P(None, ("tok", "head"), None, None, None)
    return jax.shard_map(
        lambda *args: body(sizes, *args),
        mesh=mesh,
        in_specs=(images, images, P(None, "tok", None), P(None, "tok", None)) + weights * 3,
        out_specs=(images, images, P()) + tuple(spec for spec in weights for _ in range(3)),
        check_vma=False,
    )
```

```python
import functools
import math

import jax
import jax.numpy as jnp
import numpy as np
from jax import lax
from jax.experimental import pallas as pl
from jax.experimental.pallas import tpu as pltpu
from jax.sharding import PartitionSpec as P

C = 384
NH = 12
HD = 32
FF = 1536
WS = 7
SHIFT = 3
STEP = 10
GRID = 14
CELLS = WS * WS
REL = (2 * WS - 1) ** 2
MICRO = 5

WIN = 64
IMG = 4 * WIN
PAD = 16 * GRID
ROWS = MICRO * IMG
GROUP = 4
GROUPS = NH // GROUP
LANES = GROUP * HD
BLOCKS = 32
PIECE = 48

EPS_NORM = 1e-05
BETA_ONE = 0.9
BETA_TWO = 0.999
ADAM_EPS = 1e-08
RATE_MATRIX = 0.08
RATE_VECTOR = 1.0
DECAY_MATRIX = 0.05
CLIP_NORM = 0.05
NEG_FILL = -1e30
HIGH = lax.Precision.HIGHEST
LOW = jnp.bfloat16
F32 = jnp.float32
NEVER = 99.0
BOTH = ("tok", "head")
MASKS = (16, 8, 2, 4, 1)
ME, SLOT, EXTENT, ROUTE = 0, 1, 2, 12


def swap_bits(position):
    return sum((position & mask) // mask << bit for bit, mask in enumerate(MASKS))


def block_at(place):
    return sum(((place >> bit) & 1) * mask for bit, mask in enumerate(MASKS))


def window_tables():
    cell = np.arange(WIN)
    real = cell < CELLS
    rolled_row = np.stack([WS * (w // 2) + cell // WS for w in range(4)])
    rolled_col = np.stack([WS * (w % 2) + cell % WS for w in range(4)])
    source_row = (rolled_row + SHIFT) % GRID
    source_col = (rolled_col + SHIFT) % GRID

    def band(position):
        return np.where(position < GRID - WS, 0, np.where(position < GRID - SHIFT, 1, 2))

    label_row = (rolled_row + SHIFT) % GRID
    label_col = (rolled_col + SHIFT) % GRID
    region = 3 * band(label_row) + band(label_col)
    label_row = (label_row + SHIFT) % GRID
    label_col = (label_col + SHIFT) % GRID
    deal = np.zeros((IMG, PAD), np.float32)
    for w in range(4):
        for c in range(CELLS):
            deal[w * WIN + c, 16 * source_row[w, c] + source_col[w, c]] = 1.0
    place = np.full((2, IMG, 128), NEVER, np.float32)
    place[0] = np.where(real[None], source_row, NEVER).reshape(IMG, 1)
    place[1] = np.where(real[None], source_col, NEVER).reshape(IMG, 1)
    reach = np.full((2, 2, WIN, 128), NEVER, np.float32)
    for pair in range(2):
        for side in range(2):
            w = 2 * pair + side
            same = (region[w][:, None] == region[w][None, :]) & real[:, None] & real[None, :]
            for kind, source in enumerate((label_row, label_col)):
                far = np.where(same, np.maximum(source[w][:, None], source[w][None, :]), NEVER)
                far = np.where(np.eye(WIN, dtype=bool) & real[:, None], -1.0, far)
                reach[pair, kind, :, side * WIN : (side + 1) * WIN] = far
    row, col = cell // WS, cell % WS
    offset = (row[None, :] - row[:, None] + WS - 1) * (2 * WS - 1) + col[None, :] - col[:, None] + WS - 1
    offset = np.where(real[None, :] & real[:, None], offset, -1)
    lookup = (offset.reshape(1, -1) == np.arange(REL)[:, None]).astype(np.float32)
    heads = (np.arange(LANES)[None, :] // HD == np.arange(GROUP)[:, None]).astype(np.float32)
    heads = np.repeat(np.concatenate([heads, heads], axis=1), WIN, axis=0)
    return deal, place, reach, lookup, heads


DEAL, PLACE, REACH, LOOKUP, HEADS = window_tables()


def dot_nn(a, b):
    return lax.dot_general(a, b, (((1,), (0,)), ((), ())), preferred_element_type=F32)


def dot_nt(a, b):
    return lax.dot_general(a, b, (((1,), (1,)), ((), ())), preferred_element_type=F32)


def dot_tn(a, b):
    return lax.dot_general(a, b, (((0,), (0,)), ((), ())), preferred_element_type=F32)


def norm_parts(rows):
    average = jnp.mean(rows, axis=-1, keepdims=True)
    centered = rows - average
    inverse = lax.rsqrt(jnp.mean(centered * centered, axis=-1, keepdims=True) + EPS_NORM)
    return centered * inverse, inverse


def norm_back(gradient, normed, inverse, gain):
    scaled = gradient * gain
    return inverse * (
        scaled
        - jnp.mean(scaled, axis=-1, keepdims=True)
        - normed * jnp.mean(scaled * normed, axis=-1, keepdims=True)
    )


def gelu_parts(pre_act):
    size = jnp.abs(pre_act) * 2.0 ** (-0.5)
    bell = jnp.exp(-size * size)
    t = 1.0 / (1.0 + 0.3275911 * size)
    poly = t * (0.254829592 + t * (-0.284496736 + t * (1.421413741 + t * (-1.453152027 + t * 1.061405429))))
    tail = 0.5 * poly * bell
    return jnp.where(pre_act < 0.0, tail, 1.0 - tail), bell * (2.0 * math.pi) ** (-0.5)


def full(shape):
    zeros = (0,) * len(shape)
    return pl.BlockSpec(shape, lambda i: zeros)


def rows_of(width):
    return pl.BlockSpec((IMG, width), lambda i: (i, 0))


IMAGE = pl.BlockSpec((1, 1, GRID, GRID, C), lambda i: (i, 0, 0, 0, 0))
SCALARS = pl.BlockSpec(memory_space=pltpu.SMEM)


def params(limit=56):
    return pltpu.CompilerParams(vmem_limit_bytes=limit * 1024 * 1024, dimension_semantics=("arbitrary",))


def cost(flops, moved):
    return pl.CostEstimate(flops=int(flops), bytes_accessed=int(moved), transcendentals=0)


def sds(shape, dtype):
    return jax.ShapeDtypeStruct(shape, dtype)


def row_mask(place_ref, table_ref, image):
    parts = []
    for w in range(4):
        rows = slice(w * WIN, (w + 1) * WIN)
        high = jnp.where(table_ref[ROUTE + 4 * image + w] >= 0, table_ref[EXTENT + 2 * image], -1).astype(F32)
        wide = table_ref[EXTENT + 2 * image + 1].astype(F32)
        inside = (place_ref[0, rows] < high) & (place_ref[1, rows] < wide)
        parts.append(jnp.where(inside, 1.0, 0.0))
    return jnp.concatenate(parts, axis=0)


def pack_body(qkv_ref, proj_ref, fc1_ref, fc2_ref, near_ref, far_ref):
    near_ref[...] = jnp.concatenate([qkv_ref[0], qkv_ref[1], qkv_ref[2], proj_ref[...]], axis=1).astype(LOW)
    depth = fc1_ref.shape[0]
    far_ref[:depth] = fc1_ref[...].astype(LOW)
    far_ref[depth:] = fc2_ref[...].astype(LOW)


def prep_body(tok_ref, cot_ref, deal_ref, vec_ref, x_ref, g_ref, n_ref, pad):
    @pl.when(pl.program_id(0) == 0)
    def _():
        pad[...] = jnp.zeros_like(pad)

    for source, target in ((cot_ref, g_ref), (tok_ref, x_ref)):
        for r in range(GRID):
            pad[16 * r : 16 * r + GRID, :] = source[0, 0, r]
        rows = dot_nn(deal_ref[...], pad[...])
        target[...] = rows.astype(LOW)
    unit, _ = norm_parts(rows)
    n_ref[...] = (unit * vec_ref[0:1] + vec_ref[1:2]).astype(LOW)


def put_back(rows, deal_ref, target):
    grid = dot_tn(deal_ref[...], rows.astype(LOW)).astype(LOW)
    for r in range(GRID):
        target[0, 0, r] = grid[16 * r : 16 * r + GRID]


def spread_keys(part, heads_ref):
    wide = jnp.concatenate([part[:WIN], part[WIN:]], axis=1)
    return jnp.concatenate([wide] * GROUP, axis=0) * heads_ref[...]


def spread_rows(part):
    zero = jnp.zeros((WIN, LANES), part.dtype)
    top = jnp.concatenate([part[:WIN], zero], axis=1)
    return jnp.concatenate([top, jnp.concatenate([zero, part[WIN:]], axis=1)], axis=0)


def own_rows(product):
    return jnp.concatenate([product[:WIN, :LANES], product[WIN:, LANES:]], axis=0)


def own_keys(product, heads_ref):
    kept = product * heads_ref[...].astype(F32)
    total = kept[:WIN]
    for h in range(1, GROUP):
        total = total + kept[h * WIN : (h + 1) * WIN]
    return jnp.concatenate([total[:, :LANES], total[:, LANES:]], axis=0)


def attend_body(
    direct, table_ref, near_ref, n_ref, vec_ref, bias_ref, reach_ref, place_ref, heads_ref,
    packed_ref, soft_ref, attn_ref, wq_ref, wp_ref, parts,
):
    image = pl.program_id(0)

    @pl.when(image == 0)
    def _():
        for j in range(BLOCKS):
            at = table_ref[ME] ^ block_at(j) if direct else (j % 8) * 4 + j // 8
            row = at // 4 * PIECE if not direct else pl.multiple_of((at >> 2) * PIECE, PIECE)
            parts[at & 3, pl.ds(row, PIECE), :] = near_ref[j]
        for w in range(3):
            wq_ref[:, w * C : (w + 1) * C] = jnp.concatenate(
                [parts[h, :, w * 96 : (w + 1) * 96] for h in range(4)], axis=1
            )
        wp_ref[...] = jnp.concatenate([parts[h, :, 288:] for h in range(4)], axis=1)

    made = dot_nn(n_ref[...], wq_ref[...])
    packed_ref[:, :C] = (made[:, :C] + vec_ref[2:3]).astype(LOW)
    packed_ref[:, C : 2 * C] = made[:, C : 2 * C].astype(LOW)
    packed_ref[:, 2 * C :] = (made[:, 2 * C :] + vec_ref[3:4]).astype(LOW)
    mask = row_mask(place_ref, table_ref, image)
    high = table_ref[EXTENT + 2 * image].astype(F32)
    wide = table_ref[EXTENT + 2 * image + 1].astype(F32)
    for pair in range(2):
        rows = slice(pair * 2 * WIN, (pair + 1) * 2 * WIN)
        allowed = (reach_ref[pair, 0] < high) & (reach_ref[pair, 1] < wide)
        for g in range(GROUPS):
            at = g * LANES
            queries = packed_ref[rows, at : at + LANES]
            keys = packed_ref[rows, C + at : C + at + LANES]
            values = packed_ref[rows, 2 * C + at : 2 * C + at + LANES]
            raw = dot_nt(spread_keys(keys, heads_ref), spread_rows(queries))
            raw = (raw * HD ** (-0.5) + bias_ref[g]).reshape(GROUP, WIN, 128)
            scores = jnp.where(allowed[None], raw, NEG_FILL)
            exponent = jnp.exp(scores - jnp.max(scores, axis=1, keepdims=True))
            soft = exponent * (1.0 / jnp.sum(exponent, axis=1, keepdims=True))
            soft = soft.reshape(GROUP * WIN, 128)
            soft_ref[0, pair * GROUPS + g] = soft
            result = own_rows(dot_tn(soft.astype(LOW), spread_keys(values, heads_ref)))
            attn_ref[rows, at : at + LANES] = (result * mask[rows]).astype(LOW)


def middle_body(attn_ref, x_ref, wp_ref, vec_ref, middle_ref, n_ref):
    middle = x_ref[...].astype(F32) + dot_nt(attn_ref[...], wp_ref[...]) + vec_ref[4:5]
    middle_ref[...] = middle
    unit, _ = norm_parts(middle)
    n_ref[...] = (unit * vec_ref[5:6] + vec_ref[6:7]).astype(LOW)


def mlp_body(
    direct, table_ref, far_ref, middle_ref, n_ref, g_ref, vec_ref,
    hidden_ref, grad_hidden_ref, grad_ref, sums_ref, w2_ref, w1, bias,
):
    image = pl.program_id(0)

    @pl.when(image == 0)
    def _():
        for j in range(BLOCKS):
            at = table_ref[ME] ^ block_at(j) if direct else (j % 8) * 4 + j // 8
            row = at // 4 * PIECE if not direct else pl.multiple_of((at >> 2) * PIECE, PIECE)
            col = at % 4 * C if not direct else pl.multiple_of((at & 3) * C, C)
            w1[pl.ds(row, PIECE), pl.ds(col, C)] = far_ref[j, :PIECE]
            w2_ref[pl.ds(row, PIECE), pl.ds(col, C)] = far_ref[j, PIECE:]
        for r in range(4):
            bias[:, r * C : (r + 1) * C] = vec_ref[8 + r : 9 + r]
        sums_ref[...] = jnp.zeros_like(sums_ref)

    unit, inverse = norm_parts(middle_ref[...])
    normed = n_ref[...]
    g_low = g_ref[...]
    g = g_low.astype(F32)
    for part in range(4):
        cols = slice(part * C, (part + 1) * C)
        pre_act = dot_nn(normed, w1[:, cols]) + bias[:, cols]
        grad_post = dot_nn(g_low, w2_ref[:, cols])
        below, density = gelu_parts(pre_act)
        hidden_ref[:, cols] = (pre_act * below).astype(LOW)
        grad_pre = grad_post * (below + pre_act * density)
        grad_hidden_ref[:, cols] = grad_pre.astype(LOW)
        sums_ref[8 + part : 9 + part] += jnp.sum(grad_pre, axis=0, keepdims=True)
    back = dot_nt(grad_hidden_ref[...], w1[...])
    sums_ref[5:6] += jnp.sum(back * unit, axis=0, keepdims=True)
    sums_ref[6:7] += jnp.sum(back, axis=0, keepdims=True)
    grad_middle = g + norm_back(back, unit, inverse, vec_ref[5:6])
    grad_ref[...] = grad_middle
    sums_ref[4:5] += jnp.sum(grad_middle, axis=0, keepdims=True)
    sums_ref[7:8] += jnp.sum(g, axis=0, keepdims=True)


def place_of(direct, table_ref, t, h):
    if not direct:
        return h * 8 + t
    return table_ref[SLOT] ^ swap_bits(4 * t) ^ ((h & 1) * 16 + (h >> 1) * 4)


def mlp_weights_body(direct, table_ref, n_ref, g_ref, hidden_ref, grad_hidden_ref, keep_ref, send_ref, n_turned, g_turned, made):
    part = pl.program_id(0)

    @pl.when(part == 0)
    def _():
        n_turned[...] = n_ref[...].T
        g_turned[...] = g_ref[...].T

    first = dot_nn(n_turned[...], grad_hidden_ref[...]).astype(LOW)
    second = dot_nn(g_turned[...], hidden_ref[...]).astype(LOW)
    for t in range(8):
        at = place_of(direct, table_ref, t, part)
        made[at, :PIECE] = first[t * PIECE : (t + 1) * PIECE]
        made[at, PIECE:] = second[t * PIECE : (t + 1) * PIECE]

    @pl.when(part == 3)
    def _():
        keep_ref[...] = made[: BLOCKS // 2]
        send_ref[...] = made[BLOCKS // 2 :]


def output_body(hidden_ref, w2_ref, middle_ref, vec_ref, deal_ref, out_ref):
    put_back(middle_ref[...] + dot_nt(hidden_ref[...], w2_ref[...]) + vec_ref[7:8], deal_ref, out_ref)


def attend_back_body(
    table_ref, grad_ref, packed_ref, soft_ref, wp_ref, place_ref, heads_ref,
    packed_grad_ref, grad_low_ref, bias_sum_ref, sums_ref,
):
    image = pl.program_id(0)

    @pl.when(image == 0)
    def _():
        bias_sum_ref[...] = jnp.zeros_like(bias_sum_ref)
        sums_ref[...] = jnp.zeros_like(sums_ref)

    grad_low = grad_ref[...].astype(LOW)
    grad_low_ref[...] = grad_low
    mask = row_mask(place_ref, table_ref, image)
    grad_attn = dot_nn(grad_low, wp_ref[...])
    grad_attn = (grad_attn * jnp.concatenate([mask] * 3, axis=1)).astype(LOW)
    for pair in range(2):
        rows = slice(pair * 2 * WIN, (pair + 1) * 2 * WIN)
        for g in range(GROUPS):
            at = g * LANES
            queries = packed_ref[rows, at : at + LANES]
            keys = packed_ref[rows, C + at : C + at + LANES]
            values = packed_ref[rows, 2 * C + at : 2 * C + at + LANES]
            incoming = spread_rows(grad_attn[rows, at : at + LANES])
            soft = soft_ref[0, pair * GROUPS + g]
            grad_soft = dot_nt(spread_keys(values, heads_ref), incoming)
            joint = (soft * grad_soft).reshape(GROUP, WIN, 128)
            inner = jnp.sum(joint, axis=1, keepdims=True)
            grad_scores = (joint - soft.reshape(GROUP, WIN, 128) * inner).reshape(GROUP * WIN, 128)
            grad_low_scores = grad_scores.astype(LOW)
            bias_sum_ref[g] += grad_low_scores.astype(F32)
            grad_values = own_keys(dot_nn(soft.astype(LOW), incoming), heads_ref)
            grad_keys = own_keys(dot_nn(grad_low_scores, spread_rows(queries)), heads_ref)
            grad_queries = own_rows(dot_tn(grad_low_scores, spread_keys(keys, heads_ref)))
            packed_grad_ref[rows, at : at + LANES] = (grad_queries * HD ** (-0.5)).astype(LOW)
            packed_grad_ref[rows, C + at : C + at + LANES] = (grad_keys * HD ** (-0.5)).astype(LOW)
            packed_grad_ref[rows, 2 * C + at : 2 * C + at + LANES] = grad_values.astype(LOW)
    sums_ref[0:1] += jnp.sum(packed_grad_ref[:, :C].astype(F32), axis=0, keepdims=True)
    sums_ref[1:2] += jnp.sum(packed_grad_ref[:, 2 * C :].astype(F32), axis=0, keepdims=True)


def attend_weights_body(direct, table_ref, n_ref, grad_low_ref, packed_grad_ref, attn_ref, keep_ref, send_ref, made):
    n_turned = n_ref[...].T
    whole = [dot_nn(n_turned, packed_grad_ref[:, w * C : (w + 1) * C]).astype(LOW) for w in range(3)]
    whole.append(dot_nn(grad_low_ref[...].T, attn_ref[...]).astype(LOW))
    for h in range(4):
        block = jnp.concatenate([part[:, h * 96 : (h + 1) * 96] for part in whole], axis=1)
        for t in range(8):
            made[place_of(direct, table_ref, t, h)] = block[t * PIECE : (t + 1) * PIECE]
    keep_ref[...] = made[: BLOCKS // 2]
    send_ref[...] = made[BLOCKS // 2 :]


def input_body(packed_grad_ref, wq_ref, x_ref, grad_ref, vec_ref, deal_ref, out_ref, sums_ref):
    @pl.when(pl.program_id(0) == 0)
    def _():
        sums_ref[...] = jnp.zeros_like(sums_ref)

    back = dot_nt(packed_grad_ref[...], wq_ref[...])
    unit, inverse = norm_parts(x_ref[...].astype(F32))
    sums_ref[0:1] += jnp.sum(back * unit, axis=0, keepdims=True)
    sums_ref[1:2] += jnp.sum(back, axis=0, keepdims=True)
    put_back(grad_ref[...] + norm_back(back, unit, inverse, vec_ref[0:1]), deal_ref, out_ref)


def adam_update(weight, first, second, gradient, rate, decay):
    first_new = BETA_ONE * first + (1.0 - BETA_ONE) * gradient
    second_new = BETA_TWO * second + (1.0 - BETA_TWO) * gradient * gradient
    first_hat = first_new / (1.0 - BETA_ONE**STEP)
    second_hat = second_new / (1.0 - BETA_TWO**STEP)
    weight_new = weight * (1.0 - rate * decay) - rate * first_hat / (jnp.sqrt(second_hat) + ADAM_EPS)
    return (weight_new, first_new, second_new)


def adam_body(near_ref, far_ref, vec_ref, table_ref, square_ref, *refs):
    olds, news = refs[:18], refs[18:]
    total = square_ref[0:1, 0:1]
    total = total + jnp.sum(jnp.sum(vec_ref[...] * vec_ref[...], axis=1, keepdims=True), axis=0, keepdims=True)
    total = total + jnp.sum(jnp.sum(table_ref[...] * table_ref[...], axis=1, keepdims=True), axis=0, keepdims=True)
    grad_norm = jnp.sqrt(total)
    factor = jnp.minimum(1.0, CLIP_NORM / (grad_norm + 1e-06))
    news[0][...] = grad_norm
    depth = far_ref.shape[0] // 2
    grads = [None, near_ref[:, 288:], far_ref[:depth], far_ref[depth:], vec_ref[...], table_ref[...]]
    for index in range(6):
        weight, first, second = olds[index], olds[6 + index], olds[12 + index]
        rate, decay = (RATE_MATRIX, DECAY_MATRIX) if index < 4 else (RATE_VECTOR, 0.0)
        for w in range(3 if index == 0 else 1):
            pick = (w,) if index == 0 else (Ellipsis,)
            gradient = near_ref[:, w * 96 : (w + 1) * 96] if index == 0 else grads[index]
            made = adam_update(weight[pick], first[pick], second[pick], gradient * factor, rate, decay)
            for kind in range(3):
                news[1 + 3 * index + kind][pick] = made[kind]


def body(
    mesh_sizes, tokens_in, cotangent, route, extent, qkv_weight, proj_weight, fc1_weight, fc2_weight, vectors, rel_table,
    qkv_first, proj_first, fc1_first, fc2_first, vectors_first, table_first,
    qkv_second, proj_second, fc1_second, fc2_second, vectors_second, table_second,
):
    toks, heads = mesh_sizes
    devices = toks * heads
    direct = toks == 8 and heads == 4
    micro = tokens_in.shape[0]
    patches = micro * devices * GRID * GRID
    head_at = lax.axis_index("head")
    me = lax.axis_index("tok") * heads + head_at
    table = jnp.concatenate(
        [
            jnp.stack([me, swap_bits(me)]).astype(jnp.int32),
            lax.dynamic_index_in_dim(extent, head_at, 1, False).reshape(-1),
            lax.dynamic_index_in_dim(route, head_at, 1, False).reshape(-1),
        ]
    )

    def tie(*arrays):
        return lax.optimization_barrier(arrays)

    def passed(rows, mask):
        return lax.ppermute(rows, BOTH, [(i, i ^ mask) for i in range(devices)])

    depth = fc1_weight.shape[0]
    near, far = pl.pallas_call(
        pack_body,
        out_shape=(sds((depth, C), LOW), sds((2 * depth, C), LOW)),
        name="pack",
    )(qkv_weight, proj_weight.T, fc1_weight, fc2_weight.T)

    def gather_plain(piece):
        spread = lax.all_gather(lax.all_gather(piece, "tok", axis=0), "head", axis=0)
        half = piece.shape[0] // depth
        spread = spread.reshape(heads, toks, half, depth, C).transpose(0, 2, 1, 3, 4)
        spread = spread.reshape(heads, half, 8, PIECE, C).transpose(0, 2, 1, 3, 4)
        return spread.reshape(BLOCKS, half * PIECE, C)

    def share_plain(keep, send):
        both = jnp.concatenate([keep, send], axis=0)
        half = both.shape[1] // PIECE
        both = both.reshape(heads, 8, half, PIECE, C).transpose(0, 2, 1, 3, 4)
        both = both.reshape(heads, half, toks, depth, C).transpose(0, 2, 1, 3, 4).reshape(devices, half * depth, C)
        both = lax.psum_scatter(both.astype(F32), "head", scatter_dimension=0, tiled=True)
        return lax.psum_scatter(both, "tok", scatter_dimension=0, tiled=True)[0]

    def join(*arrays):
        return jnp.concatenate(arrays, axis=0)

    def first_sum(keep, got):
        total = keep.astype(F32) + got.astype(F32)
        return total[:4], [total[at : at + 4].astype(LOW) for at in (4, 8, 12)]

    def plane_sum(stays, got):
        for part in got:
            stays = stays + part.astype(F32)
        return stays[:2], stays[2:].astype(LOW)

    def line_sum(stays, got):
        total = stays + got.astype(F32)
        return total[:1], total[1:].astype(LOW)

    plane = (2, 4, 6)
    deal = jnp.asarray(DEAL, LOW)
    place = jnp.asarray(PLACE)
    reach = jnp.asarray(REACH)
    heads_low = jnp.asarray(HEADS, LOW)
    x_rows, g_rows, n_rows = pl.pallas_call(
        prep_body,
        grid=(MICRO,),
        in_specs=[IMAGE, IMAGE, full((IMG, PAD)), full((12, C))],
        out_specs=[rows_of(C)] * 3,
        out_shape=[sds((ROWS, C), LOW)] * 3,
        scratch_shapes=[pltpu.VMEM((PAD, C), LOW)],
        compiler_params=params(16),
        cost_estimate=cost(2e9, 6e6),
        name="prep",
    )(tokens_in, cotangent, deal, vectors)
    bias = jnp.dot(rel_table.T, jnp.asarray(LOOKUP), precision=HIGH).reshape(GROUPS, GROUP * WIN, WIN)
    bias = jnp.concatenate([bias, bias], axis=2)

    if direct:
        near_all, far_all = near[None], far[None]
        for mask in MASKS[:2]:
            near_all, far_all = join(near_all, passed(near_all, mask)), join(far_all, passed(far_all, mask))
        near_all = join(near_all, *[passed(near_all, mask) for mask in plane])
        near_all, far_all = tie(near_all, far_all)
        far_got = [passed(far_all, mask) for mask in plane]
        near_all = join(near_all, passed(near_all, MASKS[4]))
        near_all, x_rows, g_rows, n_rows, bias, table = tie(near_all, x_rows, g_rows, n_rows, bias, table)
    else:
        near_all, far_all = gather_plain(near), gather_plain(far)

    packed, soft, attn, w_qkv, w_proj = pl.pallas_call(
        functools.partial(attend_body, direct),
        grid=(MICRO,),
        in_specs=[
            SCALARS, full((BLOCKS, PIECE, C)), rows_of(C), full((12, C)),
            full((GROUPS, GROUP * WIN, 128)), full((2, 2, WIN, 128)), full((2, IMG, 128)), full((IMG, 256)),
        ],
        out_specs=[
            rows_of(3 * C), pl.BlockSpec((1, 2 * GROUPS, GROUP * WIN, 128), lambda i: (i, 0, 0, 0)), rows_of(C),
            full((C, 3 * C)), full((C, C)),
        ],
        out_shape=[
            sds((ROWS, 3 * C), LOW), sds((MICRO, 2 * GROUPS, GROUP * WIN, 128), F32), sds((ROWS, C), LOW),
            sds((C, 3 * C), LOW), sds((C, C), LOW),
        ],
        scratch_shapes=[pltpu.VMEM((4, C, C), LOW)],
        compiler_params=params(32),
        cost_estimate=cost(8e9, 12e6),
        name="attend",
    )(table, near_all, n_rows, vectors, bias, reach, place, heads_low)

    if direct:
        attn, *far_got = tie(attn, *far_got)
        far_all = join(far_all, *far_got)
        far_core = passed(far_all, MASKS[4])

    middle, n_two = pl.pallas_call(
        middle_body,
        grid=(MICRO,),
        in_specs=[rows_of(C), rows_of(C), full((C, C)), full((12, C))],
        out_specs=[rows_of(C), rows_of(C)],
        out_shape=[sds((ROWS, C), F32), sds((ROWS, C), LOW)],
        compiler_params=params(16),
        cost_estimate=cost(1e9, 6e6),
        name="middle",
    )(attn, x_rows, w_proj, vectors)

    if direct:
        far_core, middle = tie(far_core, middle)
        far_all = join(far_all, far_core)

    hidden, grad_hidden, grad_middle, sums_mlp, w_fc2 = pl.pallas_call(
        functools.partial(mlp_body, direct),
        grid=(MICRO,),
        in_specs=[SCALARS, full((BLOCKS, 2 * PIECE, C)), rows_of(C), rows_of(C), rows_of(C), full((12, C))],
        out_specs=[rows_of(FF), rows_of(FF), rows_of(C), full((12, C)), full((C, FF))],
        out_shape=[sds((ROWS, FF), LOW), sds((ROWS, FF), LOW), sds((ROWS, C), F32), sds((12, C), F32), sds((C, FF), LOW)],
        scratch_shapes=[pltpu.VMEM((C, FF), LOW), pltpu.VMEM((1, FF), F32)],
        compiler_params=params(32),
        cost_estimate=cost(10e9, 16e6),
        name="mlp",
    )(table, far_all, middle, n_two, g_rows, vectors)

    half = BLOCKS // 2
    columns = pl.BlockSpec((ROWS, C), lambda i: (0, i))
    far_keep, far_send = pl.pallas_call(
        functools.partial(mlp_weights_body, direct),
        grid=(4,),
        in_specs=[SCALARS, full((ROWS, C)), full((ROWS, C)), columns, columns],
        out_specs=[full((half, 2 * PIECE, C)), full((half, 2 * PIECE, C))],
        out_shape=[sds((half, 2 * PIECE, C), LOW), sds((half, 2 * PIECE, C), LOW)],
        scratch_shapes=[pltpu.VMEM((C, ROWS), LOW), pltpu.VMEM((C, ROWS), LOW), pltpu.VMEM((BLOCKS, 2 * PIECE, C), LOW)],
        compiler_params=params(32),
        cost_estimate=cost(4e9, 12e6),
        name="mlp_weights",
    )(table, n_two, g_rows, hidden, grad_hidden)

    if direct:
        far_got = passed(far_send, MASKS[4])

    block_out = pl.pallas_call(
        output_body,
        grid=(MICRO,),
        in_specs=[rows_of(FF), full((C, FF)), rows_of(C), full((12, C)), full((IMG, PAD))],
        out_specs=IMAGE,
        out_shape=sds(tokens_in.shape, LOW),
        compiler_params=params(16),
        cost_estimate=cost(2e9, 8e6),
        name="output",
    )(hidden, w_fc2, middle, vectors, deal)

    if direct:
        block_out, far_got, grad_middle = tie(block_out, far_got, grad_middle)
        far_stays, far_goes = first_sum(far_keep, far_got)
        far_got = [passed(part, mask) for part, mask in zip(far_goes, plane)]

    packed_grad, grad_low, bias_sum, sums_attend = pl.pallas_call(
        attend_back_body,
        grid=(MICRO,),
        in_specs=[
            SCALARS, rows_of(C), rows_of(3 * C), pl.BlockSpec((1, 2 * GROUPS, GROUP * WIN, 128), lambda i: (i, 0, 0, 0)),
            full((C, C)), full((2, IMG, 128)), full((IMG, 256)),
        ],
        out_specs=[rows_of(3 * C), rows_of(C), full((GROUPS, GROUP * WIN, 128)), full((2, C))],
        out_shape=[
            sds((ROWS, 3 * C), LOW), sds((ROWS, C), LOW), sds((GROUPS, GROUP * WIN, 128), F32), sds((2, C), F32),
        ],
        compiler_params=params(32),
        cost_estimate=cost(10e9, 12e6),
        name="attend_back",
    )(table, grad_middle, packed, soft, w_proj, place, heads_low)

    if direct:
        packed_grad, *far_got = tie(packed_grad, *far_got)
        far_stays, far_goes = plane_sum(far_stays, far_got)
        far_got = passed(far_goes, MASKS[1])

    near_keep, near_send = pl.pallas_call(
        functools.partial(attend_weights_body, direct),
        in_specs=[SCALARS] + [pl.BlockSpec(memory_space=pltpu.VMEM)] * 4,
        out_shape=[sds((half, PIECE, C), LOW), sds((half, PIECE, C), LOW)],
        scratch_shapes=[pltpu.VMEM((BLOCKS, PIECE, C), LOW)],
        compiler_params=pltpu.CompilerParams(vmem_limit_bytes=32 * 1024 * 1024),
        cost_estimate=cost(2e9, 8e6),
        name="attend_weights",
    )(table, n_rows, grad_low, packed_grad, attn)

    if direct:
        near_send, far_got = tie(near_send, far_got)
        near_got = passed(near_send, MASKS[4])
        far_stays, far_goes = line_sum(far_stays, far_got)
        near_keep, near_got, packed_grad = tie(near_keep, near_got, packed_grad)
        near_stays, near_goes = first_sum(near_keep, near_got)
        near_got = [passed(part, mask) for part, mask in zip(near_goes, plane)]
        far_got = passed(far_goes, MASKS[0])

    grad_block, sums_input = pl.pallas_call(
        input_body,
        grid=(MICRO,),
        in_specs=[rows_of(3 * C), full((C, 3 * C)), rows_of(C), rows_of(C), full((12, C)), full((IMG, PAD))],
        out_specs=[IMAGE, full((2, C))],
        out_shape=[sds(tokens_in.shape, LOW), sds((2, C), F32)],
        compiler_params=params(16),
        cost_estimate=cost(4e9, 8e6),
        name="input_grad",
    )(packed_grad, w_qkv, x_rows, grad_middle, vectors, deal)

    vec_grad = jnp.concatenate([sums_input, sums_attend, sums_mlp[4:]], axis=0)
    bias_sum = (bias_sum[:, :, :WIN] + bias_sum[:, :, WIN:]).reshape(NH, WIN * WIN)
    table_grad = jnp.dot(bias_sum, jnp.asarray(LOOKUP.T), precision=HIGH)
    if direct:
        spare = jnp.concatenate([vec_grad.reshape(-1), table_grad.reshape(-1), jnp.zeros((20,), F32)]).reshape(52, 128)
        grad_block, spare, *near_got = tie(grad_block, spare, *near_got)
        near_stays, near_goes = plane_sum(near_stays, near_got)
        near_stays, near_goes = line_sum(near_stays, passed(near_goes, MASKS[1]))
        near_grad = (near_stays + passed(near_goes, MASKS[0]).astype(F32))[0] / patches
        far_grad = (far_stays + far_got.astype(F32))[0] / patches
        squares = jnp.sum(near_grad * near_grad) + jnp.sum(far_grad * far_grad)
        spare = join(spare, jnp.broadcast_to(squares, (4, 128)))
        for mask in MASKS[::-1]:
            spare = spare + passed(spare, mask)
        squares = spare[52:53]
        spare = spare[:52].reshape(-1) / patches
        vec_grad = spare[: 12 * C].reshape(12, C)
        table_grad = spare[12 * C : 12 * C + NH * REL].reshape(NH, REL)
    else:
        near_grad, far_grad = share_plain(near_keep, near_send) / patches, share_plain(far_keep, far_send) / patches
        squares = jnp.sum(near_grad * near_grad) + jnp.sum(far_grad * far_grad)
        vec_grad, table_grad, squares = lax.psum((vec_grad, table_grad, squares), BOTH)
        squares = jnp.broadcast_to(squares, (1, 128))
        vec_grad, table_grad = vec_grad / patches, table_grad / patches

    olds = (
        qkv_weight, proj_weight.T, fc1_weight, fc2_weight.T, vectors, rel_table.T,
        qkv_first, proj_first.T, fc1_first, fc2_first.T, vectors_first, table_first.T,
        qkv_second, proj_second.T, fc1_second, fc2_second.T, vectors_second, table_second.T,
    )
    shapes = [sds((1, 1), F32)] + [sds(olds[index].shape, F32) for index in range(6) for _ in range(3)]
    news = pl.pallas_call(
        adam_body,
        out_shape=shapes,
        compiler_params=pltpu.CompilerParams(vmem_limit_bytes=32 * 1024 * 1024),
        name="adam",
    )(near_grad, far_grad, vec_grad, table_grad, squares, *olds)
    turned = [new.T if index // 3 in (1, 3, 5) else new for index, new in enumerate(news[1:])]
    return (block_out, grad_block, news[0][0, 0], *turned)


def solution(mesh):
    sizes = (mesh.shape["tok"], mesh.shape["head"])
    weights = (P(None, "tok", "head"), P("head", "tok"), P("tok", "head"), P("head", "tok"), P(), P())
    images = P(None, ("tok", "head"), None, None, None)
    return jax.shard_map(
        lambda *args: body(sizes, *args),
        mesh=mesh,
        in_specs=(images, images, P(None, "tok", None), P(None, "tok", None)) + weights * 3,
        out_specs=(images, images, P()) + tuple(spec for spec in weights for _ in range(3)),
        check_vma=False,
    )
```

```python
import functools
import math

import jax
import jax.numpy as jnp
import numpy as np
from jax import lax
from jax.experimental import pallas as pl
from jax.experimental.pallas import tpu as pltpu
from jax.sharding import PartitionSpec as P

C = 384
NH = 12
HD = 32
FF = 1536
WS = 7
SHIFT = 3
STEP = 10
GRID = 14
CELLS = WS * WS
REL = (2 * WS - 1) ** 2
MICRO = 5

WIN = 64
IMG = 4 * WIN
PAD = 16 * GRID
ROWS = MICRO * IMG
GROUP = 4
GROUPS = NH // GROUP
LANES = GROUP * HD
BLOCKS = 32
PIECE = 48

EPS_NORM = 1e-05
BETA_ONE = 0.9
BETA_TWO = 0.999
ADAM_EPS = 1e-08
RATE_MATRIX = 0.08
RATE_VECTOR = 1.0
DECAY_MATRIX = 0.05
CLIP_NORM = 0.05
NEG_FILL = -1e30
HIGH = lax.Precision.HIGHEST
LOW = jnp.bfloat16
F32 = jnp.float32
NEVER = 99.0
BOTH = ("tok", "head")
MASKS = (16, 8, 2, 4, 1)
CORE, PLANE, LINE = 1, (2, 4, 6), (16, 8, 24)
PIECES = 8
ME, SLOT, EXTENT, ROUTE = 0, 1, 2, 12


def swap_bits(position):
    return sum((position & mask) // mask << bit for bit, mask in enumerate(MASKS))


def block_at(place):
    return sum(((place >> bit) & 1) * mask for bit, mask in enumerate(MASKS))


def window_tables():
    cell = np.arange(WIN)
    real = cell < CELLS
    rolled_row = np.stack([WS * (w // 2) + cell // WS for w in range(4)])
    rolled_col = np.stack([WS * (w % 2) + cell % WS for w in range(4)])
    source_row = (rolled_row + SHIFT) % GRID
    source_col = (rolled_col + SHIFT) % GRID

    def band(position):
        return np.where(position < GRID - WS, 0, np.where(position < GRID - SHIFT, 1, 2))

    label_row = (rolled_row + SHIFT) % GRID
    label_col = (rolled_col + SHIFT) % GRID
    region = 3 * band(label_row) + band(label_col)
    label_row = (label_row + SHIFT) % GRID
    label_col = (label_col + SHIFT) % GRID
    deal = np.zeros((IMG, PAD), np.float32)
    for w in range(4):
        for c in range(CELLS):
            deal[w * WIN + c, 16 * source_row[w, c] + source_col[w, c]] = 1.0
    place = np.full((2, IMG, 128), NEVER, np.float32)
    place[0] = np.where(real[None], source_row, NEVER).reshape(IMG, 1)
    place[1] = np.where(real[None], source_col, NEVER).reshape(IMG, 1)
    reach = np.full((2, 2, WIN, 128), NEVER, np.float32)
    for pair in range(2):
        for side in range(2):
            w = 2 * pair + side
            same = (region[w][:, None] == region[w][None, :]) & real[:, None] & real[None, :]
            for kind, source in enumerate((label_row, label_col)):
                far = np.where(same, np.maximum(source[w][:, None], source[w][None, :]), NEVER)
                far = np.where(np.eye(WIN, dtype=bool) & real[:, None], -1.0, far)
                reach[pair, kind, :, side * WIN : (side + 1) * WIN] = far
    row, col = cell // WS, cell % WS
    offset = (row[None, :] - row[:, None] + WS - 1) * (2 * WS - 1) + col[None, :] - col[:, None] + WS - 1
    offset = np.where(real[None, :] & real[:, None], offset, -1)
    lookup = (offset.reshape(1, -1) == np.arange(REL)[:, None]).astype(np.float32)
    heads = (np.arange(LANES)[None, :] // HD == np.arange(GROUP)[:, None]).astype(np.float32)
    heads = np.repeat(np.concatenate([heads, heads], axis=1), WIN, axis=0)
    return deal, place, reach, lookup, heads


DEAL, PLACE, REACH, LOOKUP, HEADS = window_tables()


def dot_nn(a, b):
    return lax.dot_general(a, b, (((1,), (0,)), ((), ())), preferred_element_type=F32)


def dot_nt(a, b):
    return lax.dot_general(a, b, (((1,), (1,)), ((), ())), preferred_element_type=F32)


def dot_tn(a, b):
    return lax.dot_general(a, b, (((0,), (0,)), ((), ())), preferred_element_type=F32)


def norm_parts(rows):
    average = jnp.mean(rows, axis=-1, keepdims=True)
    centered = rows - average
    inverse = lax.rsqrt(jnp.mean(centered * centered, axis=-1, keepdims=True) + EPS_NORM)
    return centered * inverse, inverse


def norm_back(gradient, normed, inverse, gain):
    scaled = gradient * gain
    return inverse * (
        scaled
        - jnp.mean(scaled, axis=-1, keepdims=True)
        - normed * jnp.mean(scaled * normed, axis=-1, keepdims=True)
    )


def gelu_parts(pre_act):
    size = jnp.abs(pre_act) * 2.0 ** (-0.5)
    bell = jnp.exp(-size * size)
    t = 1.0 / (1.0 + 0.3275911 * size)
    poly = t * (0.254829592 + t * (-0.284496736 + t * (1.421413741 + t * (-1.453152027 + t * 1.061405429))))
    tail = 0.5 * poly * bell
    return jnp.where(pre_act < 0.0, tail, 1.0 - tail), bell * (2.0 * math.pi) ** (-0.5)


SCALARS = pl.BlockSpec(memory_space=pltpu.SMEM)
HELD = pl.BlockSpec(memory_space=pltpu.VMEM)


def call(body, outs, inputs, name, limit=16, scratch=(), flops=1e9, scalars=0):
    return pl.pallas_call(
        body,
        in_specs=[SCALARS] * scalars + [HELD] * (len(inputs) - scalars),
        out_specs=[HELD] * len(outs),
        out_shape=[jax.ShapeDtypeStruct(shape, dtype) for shape, dtype in outs],
        scratch_shapes=list(scratch),
        compiler_params=whole(limit),
        cost_estimate=pl.CostEstimate(flops=int(flops), bytes_accessed=4000000, transcendentals=0),
        name=name,
    )(*inputs)


def image_rows(image):
    return pl.ds(pl.multiple_of(image * IMG, IMG), IMG)


def whole(limit):
    return pltpu.CompilerParams(vmem_limit_bytes=limit * 1024 * 1024)


def sds(shape, dtype):
    return jax.ShapeDtypeStruct(shape, dtype)


def streamed(*arrays):
    return [pltpu.with_memory_space_constraint(array, pltpu.HBM) for array in arrays]


def row_mask(place_ref, table_ref, image):
    parts = []
    for w in range(4):
        rows = slice(w * WIN, (w + 1) * WIN)
        high = jnp.where(table_ref[ROUTE + 4 * image + w] >= 0, table_ref[EXTENT + 2 * image], -1).astype(F32)
        wide = table_ref[EXTENT + 2 * image + 1].astype(F32)
        inside = (place_ref[0, rows] < high) & (place_ref[1, rows] < wide)
        parts.append(jnp.where(inside, 1.0, 0.0))
    return jnp.concatenate(parts, axis=0)


def pack_body(qkv_ref, proj_ref, fc1_ref, fc2_ref, near_ref, far_ref):
    near_ref[...] = jnp.concatenate([qkv_ref[0], qkv_ref[1], qkv_ref[2], proj_ref[...]], axis=1).astype(LOW)
    depth = fc1_ref.shape[0]
    far_ref[:depth] = fc1_ref[...].astype(LOW)
    far_ref[depth:] = fc2_ref[...].astype(LOW)


def first_sum_body(keep_ref, got_ref, stays_ref, *goes_refs):
    stays_ref[...] = keep_ref[:4].astype(F32) + got_ref[:4].astype(F32)
    for index, goes in enumerate(goes_refs):
        at = 4 * (index + 1)
        goes[...] = (keep_ref[at : at + 4].astype(F32) + got_ref[at : at + 4].astype(F32)).astype(LOW)


def plane_sum_body(stays_ref, *refs):
    got, (rest, *goes) = refs[:3], refs[3:]
    for at in range(4):
        total = stays_ref[at : at + 1] + got[0][at : at + 1].astype(F32)
        total = total + (got[1][at : at + 1].astype(F32) + got[2][at : at + 1].astype(F32))
        if at == 0:
            rest[...] = total
        else:
            goes[at - 1][...] = total.astype(LOW)


def finish_body(patches, near_ref, far_ref, vec_ref, table_ref, *refs):
    near_got, far_got, (near_grad, far_grad, spare) = refs[:3], refs[3:6], refs[6:]
    squares = jnp.zeros((1, 1), F32)
    for stays, got, target in ((near_ref, near_got, near_grad), (far_ref, far_got, far_grad)):
        total = stays[0] + got[0][0].astype(F32) + (got[1][0].astype(F32) + got[2][0].astype(F32))
        total = total * (1.0 / patches)
        target[...] = total
        squares = squares + jnp.sum(jnp.sum(total * total, axis=1, keepdims=True), axis=0, keepdims=True)
    spare[0:12] = vec_ref[...] * (1.0 / patches)
    spare[12:24] = jnp.zeros((12, C), F32)
    spare[12:24, :REL] = table_ref[...] * (1.0 / patches)
    spare[24:32] = jnp.broadcast_to(squares, (8, C))


def prep_body(tok_ref, cot_ref, deal_ref, vec_ref, x_ref, g_ref, n_ref, pad):
    pad[...] = jnp.zeros_like(pad)

    @pl.loop(0, MICRO)
    def _(image):
        at = image_rows(image)
        for source, target in ((cot_ref, g_ref), (tok_ref, x_ref)):
            for r in range(GRID):
                pad[16 * r : 16 * r + GRID, :] = source[image, 0, r]
            rows = dot_nn(deal_ref[...], pad[...])
            target[at, :] = rows.astype(LOW)
        unit, _ = norm_parts(rows)
        n_ref[at, :] = (unit * vec_ref[0:1] + vec_ref[1:2]).astype(LOW)


def put_back(rows, back_ref, target, image):
    grid = dot_nn(back_ref[...], rows.astype(LOW)).astype(LOW)
    for r in range(GRID):
        target[image, 0, r] = grid[16 * r : 16 * r + GRID]


def spread_keys(part, heads_ref):
    wide = jnp.concatenate([part[:WIN], part[WIN:]], axis=1)
    return jnp.concatenate([wide] * GROUP, axis=0) * heads_ref[...]


def spread_rows(part):
    zero = jnp.zeros((WIN, LANES), part.dtype)
    top = jnp.concatenate([part[:WIN], zero], axis=1)
    return jnp.concatenate([top, jnp.concatenate([zero, part[WIN:]], axis=1)], axis=0)


def own_rows(product):
    return jnp.concatenate([product[:WIN, :LANES], product[WIN:, LANES:]], axis=0)


def own_keys(product, heads_ref):
    kept = product * heads_ref[...].astype(F32)
    total = kept[:WIN]
    for h in range(1, GROUP):
        total = total + kept[h * WIN : (h + 1) * WIN]
    return jnp.concatenate([total[:, :LANES], total[:, LANES:]], axis=0)


def attend_body(
    direct, table_ref, n_ref, vec_ref, bias_ref, reach_ref, place_ref, heads_ref, *refs,
):
    near_refs, (packed_ref, soft_ref, attn_ref, wq_ref, wp_ref, parts) = refs[:PIECES], refs[PIECES:]
    for j in range(BLOCKS):
        at = table_ref[ME] ^ block_at(j) if direct else (j % 8) * 4 + j // 8
        row = at // 4 * PIECE if not direct else pl.multiple_of((at >> 2) * PIECE, PIECE)
        parts[at & 3, pl.ds(row, PIECE), :] = near_refs[j // 4][j % 4]
    for w in range(3):
        wq_ref[:, w * C : (w + 1) * C] = jnp.concatenate([parts[h, :, w * 96 : (w + 1) * 96] for h in range(4)], axis=1)
    wp_ref[...] = jnp.concatenate([parts[h, :, 288:] for h in range(4)], axis=1)

    @pl.loop(0, MICRO)
    def _(image):
        at_image = image_rows(image)
        made = dot_nn(n_ref[at_image, :], wq_ref[...])
        packed_ref[at_image, :C] = (made[:, :C] + vec_ref[2:3]).astype(LOW)
        packed_ref[at_image, C : 2 * C] = made[:, C : 2 * C].astype(LOW)
        packed_ref[at_image, 2 * C :] = (made[:, 2 * C :] + vec_ref[3:4]).astype(LOW)
        mask = row_mask(place_ref, table_ref, image)
        high = table_ref[EXTENT + 2 * image].astype(F32)
        wide = table_ref[EXTENT + 2 * image + 1].astype(F32)
        for pair in range(2):
            rows = slice(pair * 2 * WIN, (pair + 1) * 2 * WIN)
            at_pair = pl.ds(pl.multiple_of(image * IMG + pair * 2 * WIN, 2 * WIN), 2 * WIN)
            allowed = (reach_ref[pair, 0] < high) & (reach_ref[pair, 1] < wide)
            for g in range(GROUPS):
                at = g * LANES
                queries = packed_ref[at_pair, at : at + LANES]
                keys = packed_ref[at_pair, C + at : C + at + LANES]
                values = packed_ref[at_pair, 2 * C + at : 2 * C + at + LANES]
                raw = dot_nt(spread_keys(keys, heads_ref), spread_rows(queries))
                raw = (raw * HD ** (-0.5) + bias_ref[g]).reshape(GROUP, WIN, 128)
                scores = jnp.where(allowed[None], raw, NEG_FILL)
                exponent = jnp.exp(scores - jnp.max(scores, axis=1, keepdims=True))
                soft = exponent * (1.0 / jnp.sum(exponent, axis=1, keepdims=True))
                soft = soft.reshape(GROUP * WIN, 128)
                soft_ref[image, pair * GROUPS + g] = soft
                result = own_rows(dot_tn(soft.astype(LOW), spread_keys(values, heads_ref)))
                attn_ref[at_pair, at : at + LANES] = (result * mask[rows]).astype(LOW)


def middle_body(attn_ref, x_ref, wp_ref, vec_ref, middle_ref, n_ref):
    @pl.loop(0, MICRO)
    def _(image):
        at = image_rows(image)
        middle = x_ref[at, :].astype(F32) + dot_nt(attn_ref[at, :], wp_ref[...]) + vec_ref[4:5]
        middle_ref[at, :] = middle
        unit, _ = norm_parts(middle)
        n_ref[at, :] = (unit * vec_ref[5:6] + vec_ref[6:7]).astype(LOW)


def mlp_body(
    direct, table_ref, middle_ref, n_ref, g_ref, vec_ref, *refs,
):
    far_refs, (hidden_ref, grad_hidden_ref, grad_ref, sums_ref, w2_ref, w1, bias) = refs[:PIECES], refs[PIECES:]
    for j in range(BLOCKS):
        at = table_ref[ME] ^ block_at(j) if direct else (j % 8) * 4 + j // 8
        row = at // 4 * PIECE if not direct else pl.multiple_of((at >> 2) * PIECE, PIECE)
        col = at % 4 * C if not direct else pl.multiple_of((at & 3) * C, C)
        w1[pl.ds(row, PIECE), pl.ds(col, C)] = far_refs[j // 4][j % 4, :PIECE]
        w2_ref[pl.ds(row, PIECE), pl.ds(col, C)] = far_refs[j // 4][j % 4, PIECE:]
    for r in range(4):
        bias[:, r * C : (r + 1) * C] = vec_ref[8 + r : 9 + r]
    sums_ref[...] = jnp.zeros_like(sums_ref)

    @pl.loop(0, MICRO)
    def _(image):
        at = image_rows(image)
        unit, inverse = norm_parts(middle_ref[at, :])
        normed = n_ref[at, :]
        g_low = g_ref[at, :]
        g = g_low.astype(F32)
        for part in range(4):
            cols = slice(part * C, (part + 1) * C)
            pre_act = dot_nn(normed, w1[:, cols]) + bias[:, cols]
            grad_post = dot_nn(g_low, w2_ref[:, cols])
            below, density = gelu_parts(pre_act)
            hidden_ref[at, cols] = (pre_act * below).astype(LOW)
            grad_pre = grad_post * (below + pre_act * density)
            grad_hidden_ref[at, cols] = grad_pre.astype(LOW)
            sums_ref[8 + part : 9 + part] += jnp.sum(grad_pre, axis=0, keepdims=True)
        back = dot_nt(grad_hidden_ref[at, :], w1[...])
        sums_ref[5:6] += jnp.sum(back * unit, axis=0, keepdims=True)
        sums_ref[6:7] += jnp.sum(back, axis=0, keepdims=True)
        grad_middle = g + norm_back(back, unit, inverse, vec_ref[5:6])
        grad_ref[at, :] = grad_middle
        sums_ref[4:5] += jnp.sum(grad_middle, axis=0, keepdims=True)
        sums_ref[7:8] += jnp.sum(g, axis=0, keepdims=True)


def place_of(direct, table_ref, t, h):
    if not direct:
        return h * 8 + t
    return table_ref[SLOT] ^ swap_bits(4 * t) ^ ((h & 1) * 16 + (h >> 1) * 4)


def mlp_weights_body(direct, table_ref, n_ref, g_ref, hidden_ref, grad_hidden_ref, keep_ref, send_ref, n_turned, g_turned, made):
    n_turned[...] = n_ref[...].T
    g_turned[...] = g_ref[...].T
    for part in range(4):
        cols = slice(part * C, (part + 1) * C)
        first = dot_nn(n_turned[...], grad_hidden_ref[:, cols]).astype(LOW)
        second = dot_nn(g_turned[...], hidden_ref[:, cols]).astype(LOW)
        for t in range(8):
            at = place_of(direct, table_ref, t, part)
            made[at, :PIECE] = first[t * PIECE : (t + 1) * PIECE]
            made[at, PIECE:] = second[t * PIECE : (t + 1) * PIECE]
    keep_ref[...] = made[: BLOCKS // 2]
    send_ref[...] = made[BLOCKS // 2 :]


def output_body(hidden_ref, w2_ref, middle_ref, vec_ref, back_ref, out_ref):
    @pl.loop(0, MICRO)
    def _(image):
        at = image_rows(image)
        put_back(middle_ref[at, :] + dot_nt(hidden_ref[at, :], w2_ref[...]) + vec_ref[7:8], back_ref, out_ref, image)


def attend_back_body(
    table_ref, grad_ref, packed_ref, soft_ref, wp_ref, place_ref, heads_ref,
    packed_grad_ref, grad_low_ref, bias_sum_ref, sums_ref,
):
    bias_sum_ref[...] = jnp.zeros_like(bias_sum_ref)
    sums_ref[...] = jnp.zeros_like(sums_ref)

    @pl.loop(0, MICRO)
    def _(image):
        at_image = image_rows(image)
        grad_low = grad_ref[at_image, :].astype(LOW)
        grad_low_ref[at_image, :] = grad_low
        mask = row_mask(place_ref, table_ref, image)
        grad_attn = dot_nn(grad_low, wp_ref[...])
        grad_attn = (grad_attn * jnp.concatenate([mask] * 3, axis=1)).astype(LOW)
        for pair in range(2):
            rows = slice(pair * 2 * WIN, (pair + 1) * 2 * WIN)
            at_pair = pl.ds(pl.multiple_of(image * IMG + pair * 2 * WIN, 2 * WIN), 2 * WIN)
            for g in range(GROUPS):
                at = g * LANES
                queries = packed_ref[at_pair, at : at + LANES]
                keys = packed_ref[at_pair, C + at : C + at + LANES]
                values = packed_ref[at_pair, 2 * C + at : 2 * C + at + LANES]
                incoming = spread_rows(grad_attn[rows, at : at + LANES])
                soft = soft_ref[image, pair * GROUPS + g]
                grad_soft = dot_nt(spread_keys(values, heads_ref), incoming)
                joint = (soft * grad_soft).reshape(GROUP, WIN, 128)
                inner = jnp.sum(joint, axis=1, keepdims=True)
                grad_scores = (joint - soft.reshape(GROUP, WIN, 128) * inner).reshape(GROUP * WIN, 128)
                grad_low_scores = grad_scores.astype(LOW)
                bias_sum_ref[g] += grad_low_scores.astype(F32)
                grad_values = own_keys(dot_nn(soft.astype(LOW), incoming), heads_ref)
                grad_keys = own_keys(dot_nn(grad_low_scores, spread_rows(queries)), heads_ref)
                grad_queries = own_rows(dot_tn(grad_low_scores, spread_keys(keys, heads_ref)))
                packed_grad_ref[at_pair, at : at + LANES] = (grad_queries * HD ** (-0.5)).astype(LOW)
                packed_grad_ref[at_pair, C + at : C + at + LANES] = (grad_keys * HD ** (-0.5)).astype(LOW)
                packed_grad_ref[at_pair, 2 * C + at : 2 * C + at + LANES] = grad_values.astype(LOW)
        sums_ref[0:1] += jnp.sum(packed_grad_ref[at_image, :C].astype(F32), axis=0, keepdims=True)
        sums_ref[1:2] += jnp.sum(packed_grad_ref[at_image, 2 * C :].astype(F32), axis=0, keepdims=True)


def attend_weights_body(direct, table_ref, n_ref, grad_low_ref, packed_grad_ref, attn_ref, keep_ref, send_ref, made):
    n_turned = n_ref[...].T
    parts = [dot_nn(n_turned, packed_grad_ref[:, w * C : (w + 1) * C]).astype(LOW) for w in range(3)]
    parts.append(dot_nn(grad_low_ref[...].T, attn_ref[...]).astype(LOW))
    for h in range(4):
        block = jnp.concatenate([part[:, h * 96 : (h + 1) * 96] for part in parts], axis=1)
        for t in range(8):
            made[place_of(direct, table_ref, t, h)] = block[t * PIECE : (t + 1) * PIECE]
    keep_ref[...] = made[: BLOCKS // 2]
    send_ref[...] = made[BLOCKS // 2 :]


def input_body(packed_grad_ref, wq_ref, x_ref, grad_ref, vec_ref, back_ref, out_ref, sums_ref):
    sums_ref[...] = jnp.zeros_like(sums_ref)

    @pl.loop(0, MICRO)
    def _(image):
        at = image_rows(image)
        back = dot_nt(packed_grad_ref[at, :], wq_ref[...])
        unit, inverse = norm_parts(x_ref[at, :].astype(F32))
        sums_ref[0:1] += jnp.sum(back * unit, axis=0, keepdims=True)
        sums_ref[1:2] += jnp.sum(back, axis=0, keepdims=True)
        put_back(grad_ref[at, :] + norm_back(back, unit, inverse, vec_ref[0:1]), back_ref, out_ref, image)


def adam_update(weight, first, second, gradient, rate, decay):
    first_new = BETA_ONE * first + (1.0 - BETA_ONE) * gradient
    second_new = BETA_TWO * second + (1.0 - BETA_TWO) * gradient * gradient
    first_hat = first_new / (1.0 - BETA_ONE**STEP)
    second_hat = second_new / (1.0 - BETA_TWO**STEP)
    weight_new = weight * (1.0 - rate * decay) - rate * first_hat / (jnp.sqrt(second_hat) + ADAM_EPS)
    return (weight_new, first_new, second_new)


def adam_body(near_ref, far_ref, spare_ref, *refs):
    olds, news = refs[:18], refs[18:]
    vec, table = spare_ref[0:12], spare_ref[12:24, :REL]
    total = spare_ref[24:25, 0:1]
    total = total + jnp.sum(jnp.sum(vec * vec, axis=1, keepdims=True), axis=0, keepdims=True)
    total = total + jnp.sum(jnp.sum(table * table, axis=1, keepdims=True), axis=0, keepdims=True)
    grad_norm = jnp.sqrt(total)
    factor = jnp.minimum(1.0, CLIP_NORM / (grad_norm + 1e-06))
    news[0][...] = grad_norm
    depth = far_ref.shape[0] // 2
    grads = [None, near_ref[:, 288:], far_ref[:depth], far_ref[depth:], vec, table]
    for index in range(6):
        weight, first, second = olds[index], olds[6 + index], olds[12 + index]
        rate, decay = (RATE_MATRIX, DECAY_MATRIX) if index < 4 else (RATE_VECTOR, 0.0)
        for w in range(3 if index == 0 else 1):
            pick = (w,) if index == 0 else (Ellipsis,)
            gradient = near_ref[:, w * 96 : (w + 1) * 96] if index == 0 else grads[index]
            made = adam_update(weight[pick], first[pick], second[pick], gradient * factor, rate, decay)
            for kind in range(3):
                news[1 + 3 * index + kind][pick] = made[kind]


def body(
    mesh_sizes, tokens_in, cotangent, route, extent, qkv_weight, proj_weight, fc1_weight, fc2_weight, vectors, rel_table,
    qkv_first, proj_first, fc1_first, fc2_first, vectors_first, table_first,
    qkv_second, proj_second, fc1_second, fc2_second, vectors_second, table_second,
):
    toks, heads = mesh_sizes
    devices = toks * heads
    direct = toks == 8 and heads == 4
    micro = tokens_in.shape[0]
    patches = micro * devices * GRID * GRID
    head_at = lax.axis_index("head")
    me = lax.axis_index("tok") * heads + head_at
    def tie(*arrays):
        return lax.optimization_barrier(arrays)

    def passed(rows, mask):
        return lax.ppermute(rows, BOTH, [(i, i ^ mask) for i in range(devices)])

    depth = fc1_weight.shape[0]
    near, far = pl.pallas_call(
        pack_body, out_shape=(sds((depth, C), LOW), sds((2 * depth, C), LOW)), compiler_params=whole(8), name="pack"
    )(*streamed(qkv_weight, proj_weight.T, fc1_weight, fc2_weight.T))

    def gather_plain(piece):
        spread = lax.all_gather(lax.all_gather(piece, "tok", axis=0), "head", axis=0)
        half = piece.shape[0] // depth
        spread = spread.reshape(heads, toks, half, depth, C).transpose(0, 2, 1, 3, 4)
        spread = spread.reshape(heads, half, 8, PIECE, C).transpose(0, 2, 1, 3, 4)
        spread = spread.reshape(BLOCKS, half * PIECE, C)
        return [spread[at : at + 4] for at in range(0, BLOCKS, 4)]

    def share_plain(keep, send):
        both = jnp.concatenate([keep, send], axis=0)
        half = both.shape[1] // PIECE
        both = both.reshape(heads, 8, half, PIECE, C).transpose(0, 2, 1, 3, 4)
        both = both.reshape(heads, half, toks, depth, C).transpose(0, 2, 1, 3, 4).reshape(devices, half * depth, C)
        both = lax.psum_scatter(both.astype(F32), "head", scatter_dimension=0, tiled=True)
        return lax.psum_scatter(both, "tok", scatter_dimension=0, tiled=True)[0]

    def join(*arrays):
        return jnp.concatenate(arrays, axis=0)

    def first_sum(keep, got):
        shape = (4,) + keep.shape[1:]
        stays, *goes = pl.pallas_call(
            first_sum_body, out_shape=[sds(shape, F32)] + [sds(shape, LOW)] * 3, compiler_params=whole(2), name="first_sum"
        )(keep, got)
        return stays, goes

    def plane_sum(stays, got):
        shape = (1,) + stays.shape[1:]
        rest, *goes = pl.pallas_call(
            plane_sum_body, out_shape=[sds(shape, F32)] + [sds(shape, LOW)] * 3, compiler_params=whole(2), name="plane_sum"
        )(stays, *got)
        return rest, goes

    def spread(rows, masks):
        return [passed(rows, mask) for mask in masks]

    def sent(parts, masks):
        return [passed(part, mask) for part, mask in zip(parts, masks)]

    def total_of(rows, masks):
        one, two, three = spread(rows, masks)
        return (rows + one) + (two + three)

    back = jnp.asarray(DEAL.T, LOW)
    deal = jnp.asarray(DEAL, LOW)
    place = jnp.asarray(PLACE)
    reach = jnp.asarray(REACH)
    heads_low = jnp.asarray(HEADS, LOW)
    x_rows, g_rows, n_rows = call(
        prep_body,
        [((ROWS, C), LOW)] * 3,
        (tokens_in, cotangent, deal, vectors),
        "prep",
        limit=4,
        scratch=[pltpu.VMEM((PAD, C), LOW)],
    )

    def product_of(values, lookup):
        first = lax.reduce_precision(values, 8, 7)
        second = lax.reduce_precision(values - first, 8, 7)
        parts = jnp.concatenate([first, second, values - first - second], axis=0).astype(LOW)
        made = jnp.dot(parts, jnp.asarray(lookup, LOW), preferred_element_type=F32).reshape(3, values.shape[0], -1)
        return made[0] + (made[1] + made[2])

    def make_bias(values):
        made = product_of(values.T, LOOKUP).reshape(GROUPS, GROUP * WIN, WIN)
        return jnp.concatenate([made, made], axis=2)

    if direct:
        near, extent, route, rel_bias = tie(near[None], extent, route, rel_table)
        near_got, far_got = spread(near, LINE), spread(far[None], LINE)
        near_all = join(near, *near_got)
        near_all, x_rows, g_rows, n_rows, rel_bias = tie(near_all, x_rows, g_rows, n_rows, rel_bias)
        near_all = [near_all] + spread(near_all, PLANE)
        table = jnp.concatenate(
            [
                jnp.stack([me, swap_bits(me)]).astype(jnp.int32),
                lax.dynamic_index_in_dim(extent, head_at, 1, False).reshape(-1),
                lax.dynamic_index_in_dim(route, head_at, 1, False).reshape(-1),
            ]
        )
        bias = make_bias(rel_bias)
        far_got[0], bias, table, *near_all = tie(far_got[0], bias, table, *near_all)
        far_all = join(far[None], *far_got)
        near_all = near_all + [passed(piece, CORE) for piece in near_all]
        far_got = [far_all] + spread(far_all, PLANE)
    else:
        table = jnp.concatenate(
            [
                jnp.stack([me, swap_bits(me)]).astype(jnp.int32),
                lax.dynamic_index_in_dim(extent, head_at, 1, False).reshape(-1),
                lax.dynamic_index_in_dim(route, head_at, 1, False).reshape(-1),
            ]
        )
        bias = make_bias(rel_table)
        near_all, far_all = gather_plain(near), gather_plain(far)

    packed, soft, attn, w_qkv, w_proj = call(
        functools.partial(attend_body, direct),
        [
            ((ROWS, 3 * C), LOW), ((MICRO, 2 * GROUPS, GROUP * WIN, 128), F32), ((ROWS, C), LOW), ((C, 3 * C), LOW), ((C, C), LOW),
        ],
        (table, n_rows, vectors, bias, reach, place, heads_low, *near_all),
        "attend",
        limit=8,
        scratch=[pltpu.VMEM((4, C, C), LOW)],
        flops=8e9,
        scalars=1,
    )

    if direct:
        attn, *far_got = tie(attn, *far_got)
        far_core = [passed(piece, CORE) for piece in far_got]

    middle, n_two = call(middle_body, [((ROWS, C), F32), ((ROWS, C), LOW)], (attn, x_rows, w_proj, vectors), "middle",
        limit=4)

    if direct:
        middle, *far_core = tie(middle, *far_core)
        far_all = far_got + far_core

    hidden, grad_hidden, grad_middle, sums_mlp, w_fc2 = call(
        functools.partial(mlp_body, direct),
        [((ROWS, FF), LOW), ((ROWS, FF), LOW), ((ROWS, C), F32), ((12, C), F32), ((C, FF), LOW)],
        (table, middle, n_two, g_rows, vectors, *far_all),
        "mlp",
        limit=8,
        scratch=[pltpu.VMEM((C, FF), LOW), pltpu.VMEM((1, FF), F32)],
        flops=10e9,
        scalars=1,
    )

    half = BLOCKS // 2
    far_keep, far_send = call(
        functools.partial(mlp_weights_body, direct),
        [((half, 2 * PIECE, C), LOW)] * 2,
        (table, n_two, g_rows, hidden, grad_hidden),
        "mlp_weights",
        limit=10,
        scratch=[pltpu.VMEM((C, ROWS), LOW), pltpu.VMEM((C, ROWS), LOW), pltpu.VMEM((BLOCKS, 2 * PIECE, C), LOW)],
        flops=4e9,
        scalars=1,
    )

    if direct:
        far_got = passed(far_send, CORE)

    (block_out,) = call(output_body, [(tokens_in.shape, LOW)], (hidden, w_fc2, middle, vectors, back), "output",
        limit=5, flops=2e9)

    if direct:
        block_out, far_got, grad_middle = tie(block_out, far_got, grad_middle)
        far_stays, far_goes = first_sum(far_keep, far_got)
        far_got = sent(far_goes, PLANE)

    packed_grad, grad_low, bias_sum, sums_attend = call(
        attend_back_body,
        [((ROWS, 3 * C), LOW), ((ROWS, C), LOW), ((GROUPS, GROUP * WIN, 128), F32), ((2, C), F32)],
        (table, grad_middle, packed, soft, w_proj, place, heads_low),
        "attend_back",
        limit=6,
        flops=8e9,
        scalars=1,
    )

    near_keep, near_send = call(
        functools.partial(attend_weights_body, direct),
        [((half, PIECE, C), LOW)] * 2,
        (table, n_rows, grad_low, packed_grad, attn),
        "attend_weights",
        limit=8,
        scratch=[pltpu.VMEM((BLOCKS, PIECE, C), LOW)],
        flops=2e9,
        scalars=1,
    )

    if direct:
        near_send, *far_got = tie(near_send, *far_got)
        near_got = passed(near_send, CORE)
        near_stays, near_goes = first_sum(near_keep, near_got)
        near_goes[0], packed_grad, bias_sum, *far_got = tie(near_goes[0], packed_grad, bias_sum, *far_got)
        near_got = sent(near_goes, PLANE)
        far_stays, far_goes = plane_sum(far_stays, far_got)
        far_got = sent(far_goes, LINE)

    grad_block, sums_input = call(
        input_body,
        [(tokens_in.shape, LOW), ((2, C), F32)],
        (packed_grad, w_qkv, x_rows, grad_middle, vectors, back),
        "input_grad",
        limit=5,
        flops=4e9,
    )

    vec_grad = jnp.concatenate([sums_input, sums_attend, sums_mlp[4:]], axis=0)
    bias_sum = (bias_sum[:, :, :WIN] + bias_sum[:, :, WIN:]).reshape(NH, WIN * WIN)
    table_grad = product_of(bias_sum, LOOKUP.T)
    if direct:
        grad_block, vec_grad, table_grad, *near_got = tie(grad_block, vec_grad, table_grad, *near_got)
        near_stays, near_goes = plane_sum(near_stays, near_got)
        near_got = sent(near_goes, LINE)
        near_grad, far_grad, spare = pl.pallas_call(
            functools.partial(finish_body, patches),
            out_shape=[sds((depth, C), F32), sds((2 * depth, C), F32), sds((32, C), F32)],
            compiler_params=whole(2),
            name="finish",
        )(near_stays, far_stays, vec_grad, table_grad, *near_got, *far_got)
        spare = spare + passed(spare, CORE)
        spare = total_of(spare, PLANE)
        spare = total_of(spare, LINE)
    else:
        near_grad, far_grad = share_plain(near_keep, near_send) / patches, share_plain(far_keep, far_send) / patches
        squares = jnp.sum(near_grad * near_grad) + jnp.sum(far_grad * far_grad)
        vec_grad, table_grad, squares = lax.psum((vec_grad, table_grad, squares), BOTH)
        table_grad = jnp.concatenate([table_grad, jnp.zeros((12, C - REL), F32)], axis=1)
        spare = jnp.concatenate([vec_grad / patches, table_grad / patches, jnp.broadcast_to(squares, (8, C))], axis=0)

    olds = (
        qkv_weight, proj_weight.T, fc1_weight, fc2_weight.T, vectors, rel_table.T,
        qkv_first, proj_first.T, fc1_first, fc2_first.T, vectors_first, table_first.T,
        qkv_second, proj_second.T, fc1_second, fc2_second.T, vectors_second, table_second.T,
    )
    shapes = [sds((1, 1), F32)] + [sds(olds[index].shape, F32) for index in range(6) for _ in range(3)]
    news = pl.pallas_call(
        adam_body,
        out_shape=shapes,
        compiler_params=whole(8),
        name="adam",
    )(near_grad, far_grad, spare, *olds)
    turned = [new.T if index // 3 in (1, 3, 5) else new for index, new in enumerate(news[1:])]
    return (block_out, grad_block, news[0][0, 0], *turned)


def solution(mesh):
    sizes = (mesh.shape["tok"], mesh.shape["head"])
    weights = (P(None, "tok", "head"), P("head", "tok"), P("tok", "head"), P("head", "tok"), P(), P())
    images = P(None, ("tok", "head"), None, None, None)
    return jax.shard_map(
        lambda *args: body(sizes, *args),
        mesh=mesh,
        in_specs=(images, images, P(None, "tok", None), P(None, "tok", None)) + weights * 3,
        out_specs=(images, images, P()) + tuple(spec for spec in weights for _ in range(3)),
        check_vma=False,
    )
```

```python
import functools
import math

import jax
import jax.numpy as jnp
import numpy as np
from jax import lax
from jax.experimental import pallas as pl
from jax.experimental.pallas import tpu as pltpu
from jax.sharding import PartitionSpec as P

C = 384
NH = 12
HD = 32
FF = 1536
WS = 7
SHIFT = 3
STEP = 10
GRID = 14
CELLS = WS * WS
REL = (2 * WS - 1) ** 2
MICRO = 5

WIN = 64
IMG = 4 * WIN
PAD = 16 * GRID
ROWS = MICRO * IMG
GROUP = 4
GROUPS = NH // GROUP
LANES = GROUP * HD
BLOCKS = 32
PIECE = 48
TALL, WIDE = 320, 256

EPS_NORM = 1e-05
BETA_ONE = 0.9
BETA_TWO = 0.999
ADAM_EPS = 1e-08
RATE_MATRIX = 0.08
RATE_VECTOR = 1.0
DECAY_MATRIX = 0.05
CLIP_NORM = 0.05
NEG_FILL = -1e30
HIGH = lax.Precision.HIGHEST
LOW = jnp.bfloat16
F32 = jnp.float32
NEVER = 99.0
BOTH = ("tok", "head")
MASKS = (16, 8, 2, 4, 1)
CORE, PLANE, LINE = 1, (2, 4, 6), (16, 8, 24)
PIECES = 8
ME, SLOT, EXTENT, ROUTE = 0, 1, 2, 12


def swap_bits(position):
    return sum((position & mask) // mask << bit for bit, mask in enumerate(MASKS))


def block_at(place):
    return sum(((place >> bit) & 1) * mask for bit, mask in enumerate(MASKS))


def window_tables():
    cell = np.arange(WIN)
    real = cell < CELLS
    rolled_row = np.stack([WS * (w // 2) + cell // WS for w in range(4)])
    rolled_col = np.stack([WS * (w % 2) + cell % WS for w in range(4)])
    source_row = (rolled_row + SHIFT) % GRID
    source_col = (rolled_col + SHIFT) % GRID

    def band(position):
        return np.where(position < GRID - WS, 0, np.where(position < GRID - SHIFT, 1, 2))

    label_row = (rolled_row + SHIFT) % GRID
    label_col = (rolled_col + SHIFT) % GRID
    region = 3 * band(label_row) + band(label_col)
    label_row = (label_row + SHIFT) % GRID
    label_col = (label_col + SHIFT) % GRID
    deal = np.zeros((IMG, PAD), np.float32)
    for w in range(4):
        for c in range(CELLS):
            deal[w * WIN + c, 16 * source_row[w, c] + source_col[w, c]] = 1.0
    place = np.full((2, IMG, 128), NEVER, np.float32)
    place[0] = np.where(real[None], source_row, NEVER).reshape(IMG, 1)
    place[1] = np.where(real[None], source_col, NEVER).reshape(IMG, 1)
    reach = np.full((2, 2, WIN, 128), NEVER, np.float32)
    for pair in range(2):
        for side in range(2):
            w = 2 * pair + side
            same = (region[w][:, None] == region[w][None, :]) & real[:, None] & real[None, :]
            for kind, source in enumerate((label_row, label_col)):
                far = np.where(same, np.maximum(source[w][:, None], source[w][None, :]), NEVER)
                far = np.where(np.eye(WIN, dtype=bool) & real[:, None], -1.0, far)
                reach[pair, kind, :, side * WIN : (side + 1) * WIN] = far
    row, col = cell // WS, cell % WS
    offset = (row[None, :] - row[:, None] + WS - 1) * (2 * WS - 1) + col[None, :] - col[:, None] + WS - 1
    offset = np.where(real[None, :] & real[:, None], offset, -1)
    lookup = (offset.reshape(1, -1) == np.arange(REL)[:, None]).astype(np.float32)
    heads = (np.arange(LANES)[None, :] // HD == np.arange(GROUP)[:, None]).astype(np.float32)
    heads = np.repeat(np.concatenate([heads, heads], axis=1), WIN, axis=0)
    return deal, place, reach, lookup, heads


DEAL, PLACE, REACH, LOOKUP, HEADS = window_tables()


def dot_nn(a, b):
    return lax.dot_general(a, b, (((1,), (0,)), ((), ())), preferred_element_type=F32)


def dot_nt(a, b):
    return lax.dot_general(a, b, (((1,), (1,)), ((), ())), preferred_element_type=F32)


def dot_tn(a, b):
    return lax.dot_general(a, b, (((0,), (0,)), ((), ())), preferred_element_type=F32)


def turned(a, eye):
    return dot_nt(eye, a).astype(LOW)


def identity():
    row = lax.broadcasted_iota(jnp.int32, (128, 128), 0)
    return jnp.where(row == lax.broadcasted_iota(jnp.int32, (128, 128), 1), 1.0, 0.0).astype(LOW)


def norm_parts(rows):
    average = jnp.mean(rows, axis=-1, keepdims=True)
    centered = rows - average
    inverse = lax.rsqrt(jnp.mean(centered * centered, axis=-1, keepdims=True) + EPS_NORM)
    return centered * inverse, inverse


def norm_back(gradient, normed, inverse, gain):
    scaled = gradient * gain
    return inverse * (
        scaled
        - jnp.mean(scaled, axis=-1, keepdims=True)
        - normed * jnp.mean(scaled * normed, axis=-1, keepdims=True)
    )


def gelu_parts(pre_act):
    below = 0.5 + 0.5 * lax.erf(pre_act * 2.0 ** (-0.5))
    return below, jnp.exp(-0.5 * pre_act * pre_act) * (2.0 * math.pi) ** (-0.5)


SCALARS = pl.BlockSpec(memory_space=pltpu.SMEM)
HELD = pl.BlockSpec(memory_space=pltpu.VMEM)


def call(body, outs, inputs, name, limit=16, scratch=(), flops=1e9, scalars=0, fetched=0, stored=0):
    inputs = list(inputs)
    remote = slice(scalars, scalars + fetched)
    inputs[remote] = [pltpu.with_memory_space_constraint(array, pltpu.HBM) for array in inputs[remote]]
    far = pl.BlockSpec(memory_space=pltpu.HBM)
    return pl.pallas_call(
        body,
        in_specs=[SCALARS] * scalars + [far] * fetched + [HELD] * (len(inputs) - scalars - fetched),
        out_specs=[far] * stored + [HELD] * (len(outs) - stored),
        out_shape=[
            pltpu.HBM(shape, dtype) if index < stored else jax.ShapeDtypeStruct(shape, dtype)
            for index, (shape, dtype) in enumerate(outs)
        ],
        scratch_shapes=list(scratch),
        compiler_params=whole(limit),
        cost_estimate=pl.CostEstimate(flops=int(flops), bytes_accessed=4000000, transcendentals=0),
        name=name,
    )(*inputs)


def image_rows(image):
    return pl.ds(pl.multiple_of(image * IMG, IMG), IMG)


def whole(limit):
    return pltpu.CompilerParams(vmem_limit_bytes=limit * 1024 * 1024)


def sds(shape, dtype):
    return jax.ShapeDtypeStruct(shape, dtype)


def streamed(*arrays):
    return [pltpu.with_memory_space_constraint(array, pltpu.HBM) for array in arrays]


def row_mask(place_ref, table_ref, image):
    parts = []
    for w in range(4):
        rows = slice(w * WIN, (w + 1) * WIN)
        high = jnp.where(table_ref[ROUTE + 4 * image + w] >= 0, table_ref[EXTENT + 2 * image], -1).astype(F32)
        wide = table_ref[EXTENT + 2 * image + 1].astype(F32)
        inside = (place_ref[0, rows] < high) & (place_ref[1, rows] < wide)
        parts.append(jnp.where(inside, 1.0, 0.0))
    return jnp.concatenate(parts, axis=0)


def pack_body(qkv_ref, proj_ref, fc1_ref, fc2_ref, near_ref, far_ref):
    near_ref[...] = jnp.concatenate([qkv_ref[0], qkv_ref[1], qkv_ref[2], proj_ref[...]], axis=1).astype(LOW)
    depth = fc1_ref.shape[0]
    far_ref[:depth] = fc1_ref[...].astype(LOW)
    far_ref[depth:] = fc2_ref[...].astype(LOW)


def first_sum_body(keep_ref, got_ref, stays_ref, *goes_refs):
    stays_ref[...] = keep_ref[:4].astype(F32) + got_ref[:4].astype(F32)
    for index, goes in enumerate(goes_refs):
        at = 4 * (index + 1)
        goes[...] = (keep_ref[at : at + 4].astype(F32) + got_ref[at : at + 4].astype(F32)).astype(LOW)


def plane_sum_body(stays_ref, *refs):
    got, (rest, *goes) = refs[:3], refs[3:]
    for at in range(4):
        total = stays_ref[at : at + 1] + got[0][at : at + 1].astype(F32)
        total = total + (got[1][at : at + 1].astype(F32) + got[2][at : at + 1].astype(F32))
        if at == 0:
            rest[...] = total
        else:
            goes[at - 1][...] = total.astype(LOW)


def finish_body(patches, near_ref, far_ref, vec_ref, table_ref, *refs):
    near_got, far_got, (near_grad, far_grad, spare) = refs[:3], refs[3:6], refs[6:]
    squares = jnp.zeros((1, 1), F32)
    for stays, got, target in ((near_ref, near_got, near_grad), (far_ref, far_got, far_grad)):
        total = stays[0] + got[0][0].astype(F32) + (got[1][0].astype(F32) + got[2][0].astype(F32))
        total = total * (1.0 / patches)
        target[...] = total
        squares = squares + jnp.sum(jnp.sum(total * total, axis=1, keepdims=True), axis=0, keepdims=True)
    spare[0:12] = vec_ref[...] * (1.0 / patches)
    spare[12:24] = jnp.zeros((12, C), F32)
    spare[12:24, :REL] = table_ref[...] * (1.0 / patches)
    spare[24:32] = jnp.broadcast_to(squares, (8, C))


def prep_body(
    tok_hbm, cot_hbm, deal_hbm, vec_hbm, x_hbm, g_hbm, n_ref, tok, cot, deal, vec, x_all, g_all, pad, sems, out_sems
):
    copies = [
        pltpu.make_async_copy(source, target, sems.at[index])
        for index, (source, target) in enumerate(((vec_hbm, vec), (deal_hbm, deal), (tok_hbm, tok), (cot_hbm, cot)))
    ]
    for copy in copies:
        copy.start()
    pad[...] = jnp.zeros_like(pad)
    for copy in copies:
        copy.wait()
    for image in range(MICRO):
        for r in range(GRID):
            pad[image, 0, 16 * r : 16 * r + GRID, :] = tok[image, 0, r]
            pad[image, 1, 16 * r : 16 * r + GRID, :] = cot[image, 0, r]
    stores, made = [], []
    for image in range(MICRO):
        at = slice(image * IMG, (image + 1) * IMG)
        made.append(dot_nn(deal[...], pad[image, 0]))
        x_all[at, :] = made[-1].astype(LOW)
        g_all[at, :] = dot_nn(deal[...], pad[image, 1]).astype(LOW)
        for index, (source, target) in enumerate(((x_all, x_hbm), (g_all, g_hbm))):
            stores.append(pltpu.make_async_copy(source.at[at], target.at[at], out_sems.at[image, index]))
            stores[-1].start()
    for image in range(MICRO):
        unit, _ = norm_parts(made[image])
        n_ref[image * IMG : (image + 1) * IMG, :] = (unit * vec[0:1] + vec[1:2]).astype(LOW)
    for store in stores:
        store.wait()


def put_back(rows, back_ref, target, image):
    grid = dot_nn(back_ref[...], rows.astype(LOW)).astype(LOW)
    for r in range(GRID):
        target[image, 0, r] = grid[16 * r : 16 * r + GRID]


def spread_keys(part, heads_ref):
    wide = jnp.concatenate([part[:WIN], part[WIN:]], axis=1)
    return jnp.concatenate([wide] * GROUP, axis=0) * heads_ref[...]


def spread_rows(part):
    zero = jnp.zeros((WIN, LANES), part.dtype)
    top = jnp.concatenate([part[:WIN], zero], axis=1)
    return jnp.concatenate([top, jnp.concatenate([zero, part[WIN:]], axis=1)], axis=0)


def own_rows(product):
    return jnp.concatenate([product[:WIN, :LANES], product[WIN:, LANES:]], axis=0)


def own_keys(product, heads_ref):
    kept = product * heads_ref[...].astype(F32)
    total = kept[:WIN]
    for h in range(1, GROUP):
        total = total + kept[h * WIN : (h + 1) * WIN]
    return jnp.concatenate([total[:, :LANES], total[:, LANES:]], axis=0)


def attend_body(
    direct, table_ref, n_ref, vec_ref, bias_ref, reach_ref, place_ref, heads_ref, *refs,
):
    near_refs, (packed_ref, soft_ref, attn_ref, wq_ref, wp_ref, parts) = refs[:PIECES], refs[PIECES:]
    for j in range(BLOCKS):
        at = table_ref[ME] ^ block_at(j) if direct else (j % 8) * 4 + j // 8
        row = at // 4 * PIECE if not direct else pl.multiple_of((at >> 2) * PIECE, PIECE)
        parts[at & 3, pl.ds(row, PIECE), :] = near_refs[j // 4][j % 4]
    for w in range(3):
        wq_ref[:, w * C : (w + 1) * C] = jnp.concatenate([parts[h, :, w * 96 : (w + 1) * 96] for h in range(4)], axis=1)
    wp_ref[...] = jnp.concatenate([parts[h, :, 288:] for h in range(4)], axis=1)

    @pl.loop(0, MICRO)
    def _(image):
        at_image = image_rows(image)
        made = dot_nn(n_ref[at_image, :], wq_ref[...])
        packed_ref[at_image, :C] = (made[:, :C] + vec_ref[2:3]).astype(LOW)
        packed_ref[at_image, C : 2 * C] = made[:, C : 2 * C].astype(LOW)
        packed_ref[at_image, 2 * C :] = (made[:, 2 * C :] + vec_ref[3:4]).astype(LOW)
        mask = row_mask(place_ref, table_ref, image)
        high = table_ref[EXTENT + 2 * image].astype(F32)
        wide = table_ref[EXTENT + 2 * image + 1].astype(F32)
        eye = identity()
        units = [(pair, g) for pair in range(2) for g in range(GROUPS)]
        at_pair = [pl.ds(pl.multiple_of(image * IMG + pair * 2 * WIN, 2 * WIN), 2 * WIN) for pair in range(2)]
        raws = []
        for pair, g in units:
            at = g * LANES
            queries = packed_ref[at_pair[pair], at : at + LANES]
            keys = packed_ref[at_pair[pair], C + at : C + at + LANES]
            raws.append(dot_nt(spread_keys(keys, heads_ref), spread_rows(queries)))
        softs = []
        for (pair, g), raw in zip(units, raws):
            allowed = (reach_ref[pair, 0] < high) & (reach_ref[pair, 1] < wide)
            raw = (raw * HD ** (-0.5) + bias_ref[g]).reshape(GROUP, WIN, 128)
            scores = jnp.where(allowed[None], raw, NEG_FILL)
            exponent = jnp.exp(scores - jnp.max(scores, axis=1, keepdims=True))
            soft = exponent * (1.0 / jnp.sum(exponent, axis=1, keepdims=True))
            soft = soft.reshape(GROUP * WIN, 128).astype(LOW)
            soft_ref[image, pair * GROUPS + g] = soft
            softs.append(soft)
        softs = [turned(soft, eye) for soft in softs]
        for (pair, g), soft in zip(units, softs):
            at = g * LANES
            values = packed_ref[at_pair[pair], 2 * C + at : 2 * C + at + LANES]
            result = own_rows(dot_nn(soft, spread_keys(values, heads_ref)))
            rows = slice(pair * 2 * WIN, (pair + 1) * 2 * WIN)
            attn_ref[at_pair[pair], at : at + LANES] = (result * mask[rows]).astype(LOW)


def middle_body(attn_ref, x_ref, wp_ref, vec_ref, middle_ref, n_ref):
    for image in range(MICRO):
        at = slice(image * IMG, (image + 1) * IMG)
        middle = x_ref[at, :].astype(F32) + dot_nt(attn_ref[at, :], wp_ref[...]) + vec_ref[4:5]
        middle_ref[at, :] = middle
        unit, _ = norm_parts(middle)
        n_ref[at, :] = (unit * vec_ref[5:6] + vec_ref[6:7]).astype(LOW)


def mlp_body(
    direct, table_ref, middle_ref, n_ref, g_ref, vec_ref, *refs,
):
    far_refs, (hidden_ref, grad_hidden_ref, grad_ref, sums_ref, w2_ref, w1, bias, bias_sum) = refs[:PIECES], refs[PIECES:]
    for j in range(BLOCKS):
        at = table_ref[ME] ^ block_at(j) if direct else (j % 8) * 4 + j // 8
        row = at // 4 * PIECE if not direct else pl.multiple_of((at >> 2) * PIECE, PIECE)
        col = at % 4 * C if not direct else pl.multiple_of((at & 3) * C, C)
        w1[pl.ds(row, PIECE), pl.ds(col, C)] = far_refs[j // 4][j % 4, :PIECE]
        w2_ref[pl.ds(row, PIECE), pl.ds(col, C)] = far_refs[j // 4][j % 4, PIECE:]
    for r in range(4):
        bias[:, r * C : (r + 1) * C] = vec_ref[8 + r : 9 + r]
    sums_ref[...] = jnp.zeros_like(sums_ref)

    bias_sum[...] = jnp.zeros_like(bias_sum)
    for part in range(FF // WIDE):
        cols = slice(part * WIDE, (part + 1) * WIDE)
        for block in range(ROWS // TALL):
            at = slice(block * TALL, (block + 1) * TALL)
            pre_act = dot_nn(n_ref[at, :], w1[:, cols]) + bias[:, cols]
            grad_post = dot_nn(g_ref[at, :], w2_ref[:, cols])
            below, density = gelu_parts(pre_act)
            hidden_ref[at, cols] = (pre_act * below).astype(LOW)
            grad_pre = grad_post * (below + pre_act * density)
            grad_hidden_ref[at, cols] = grad_pre.astype(LOW)
            bias_sum[:, cols] += jnp.sum(grad_pre, axis=0, keepdims=True)
    for block in range(ROWS // TALL):
        at = slice(block * TALL, (block + 1) * TALL)
        back = dot_nt(grad_hidden_ref[at, :], w1[...])
        unit, inverse = norm_parts(middle_ref[at, :])
        g = g_ref[at, :].astype(F32)
        grad_middle = g + norm_back(back, unit, inverse, vec_ref[5:6])
        grad_ref[at, :] = grad_middle
        sums_ref[4:5] += jnp.sum(grad_middle, axis=0, keepdims=True)
        sums_ref[5:6] += jnp.sum(back * unit, axis=0, keepdims=True)
        sums_ref[6:7] += jnp.sum(back, axis=0, keepdims=True)
        sums_ref[7:8] += jnp.sum(g, axis=0, keepdims=True)
    for r in range(4):
        sums_ref[8 + r : 9 + r] = bias_sum[:, r * C : (r + 1) * C]


def place_of(direct, table_ref, t, h):
    if not direct:
        return h * 8 + t
    return table_ref[SLOT] ^ swap_bits(4 * t) ^ ((h & 1) * 16 + (h >> 1) * 4)


def mlp_weights_body(direct, table_ref, n_ref, g_ref, hidden_ref, grad_hidden_ref, keep_ref, send_ref, n_turned, g_turned, made, first, second):
    n_turned[...] = n_ref[...].T
    g_turned[...] = g_ref[...].T
    for part in range(3):
        cols = slice(part * 2 * WIDE, (part + 1) * 2 * WIDE)
        first[:, cols] = dot_nn(n_turned[...], grad_hidden_ref[:, cols]).astype(LOW)
        second[:, cols] = dot_nn(g_turned[...], hidden_ref[:, cols]).astype(LOW)
    for h in range(4):
        cols = slice(h * C, (h + 1) * C)
        for t in range(8):
            at = place_of(direct, table_ref, t, h)
            made[at, :PIECE] = first[t * PIECE : (t + 1) * PIECE, cols]
            made[at, PIECE:] = second[t * PIECE : (t + 1) * PIECE, cols]
    keep_ref[...] = made[: BLOCKS // 2]
    send_ref[...] = made[BLOCKS // 2 :]


def output_body(hidden_ref, w2_ref, middle_ref, vec_ref, back_ref, out_ref):
    made = []
    for image in range(MICRO):
        at = slice(image * IMG, (image + 1) * IMG)
        made.append((middle_ref[at, :] + dot_nt(hidden_ref[at, :], w2_ref[...]) + vec_ref[7:8]).astype(LOW))
    for image in range(MICRO):
        put_back(made[image], back_ref, out_ref, image)


def attend_back_body(
    table_ref, grad_ref, packed_ref, soft_ref, wp_ref, place_ref, heads_ref,
    packed_grad_ref, grad_low_ref, bias_sum_ref, sums_ref,
):
    bias_sum_ref[...] = jnp.zeros_like(bias_sum_ref)
    sums_ref[...] = jnp.zeros_like(sums_ref)

    @pl.loop(0, MICRO)
    def _(image):
        at_image = image_rows(image)
        grad_low = grad_ref[at_image, :].astype(LOW)
        grad_low_ref[at_image, :] = grad_low
        mask = row_mask(place_ref, table_ref, image)
        grad_attn = dot_nn(grad_low, wp_ref[...])
        grad_attn = (grad_attn * jnp.concatenate([mask] * 3, axis=1)).astype(LOW)
        eye = identity()
        units = [(pair, g) for pair in range(2) for g in range(GROUPS)]
        at_pair = [pl.ds(pl.multiple_of(image * IMG + pair * 2 * WIN, 2 * WIN), 2 * WIN) for pair in range(2)]
        incomings, grad_softs = [], []
        for pair, g in units:
            at = g * LANES
            values = packed_ref[at_pair[pair], 2 * C + at : 2 * C + at + LANES]
            incomings.append(spread_rows(grad_attn[pair * 2 * WIN : (pair + 1) * 2 * WIN, at : at + LANES]))
            grad_softs.append(dot_nt(spread_keys(values, heads_ref), incomings[-1]))
        grads = []
        for (pair, g), grad_soft in zip(units, grad_softs):
            soft = soft_ref[image, pair * GROUPS + g].astype(F32)
            joint = (soft * grad_soft).reshape(GROUP, WIN, 128)
            inner = jnp.sum(joint, axis=1, keepdims=True)
            grad_scores = (joint - soft.reshape(GROUP, WIN, 128) * inner).reshape(GROUP * WIN, 128)
            grads.append(grad_scores.astype(LOW))
            bias_sum_ref[g] += grads[-1].astype(F32)
        values_made = [dot_nn(soft_ref[image, pair * GROUPS + g], incoming) for (pair, g), incoming in zip(units, incomings)]
        turns = [turned(grad, eye) for grad in grads]
        keys_made, queries_made = [], []
        for (pair, g), grad, turn in zip(units, grads, turns):
            at = g * LANES
            queries = packed_ref[at_pair[pair], at : at + LANES]
            keys = packed_ref[at_pair[pair], C + at : C + at + LANES]
            keys_made.append(dot_nn(grad, spread_rows(queries)))
            queries_made.append(dot_nn(turn, spread_keys(keys, heads_ref)))
        for (pair, g), grad_values, grad_keys, grad_queries in zip(units, values_made, keys_made, queries_made):
            at = g * LANES
            rows = at_pair[pair]
            packed_grad_ref[rows, at : at + LANES] = (own_rows(grad_queries) * HD ** (-0.5)).astype(LOW)
            packed_grad_ref[rows, C + at : C + at + LANES] = (own_keys(grad_keys, heads_ref) * HD ** (-0.5)).astype(LOW)
            packed_grad_ref[rows, 2 * C + at : 2 * C + at + LANES] = own_keys(grad_values, heads_ref).astype(LOW)
        sums_ref[0:1] += jnp.sum(packed_grad_ref[at_image, :C].astype(F32), axis=0, keepdims=True)
        sums_ref[1:2] += jnp.sum(packed_grad_ref[at_image, 2 * C :].astype(F32), axis=0, keepdims=True)


def attend_weights_body(direct, table_ref, n_ref, grad_low_ref, packed_grad_ref, attn_ref, keep_ref, send_ref, made):
    n_turned = n_ref[...].T
    parts = [dot_nn(n_turned, packed_grad_ref[:, w * C : (w + 1) * C]).astype(LOW) for w in range(3)]
    parts.append(dot_nn(grad_low_ref[...].T, attn_ref[...]).astype(LOW))
    for h in range(4):
        block = jnp.concatenate([part[:, h * 96 : (h + 1) * 96] for part in parts], axis=1)
        for t in range(8):
            made[place_of(direct, table_ref, t, h)] = block[t * PIECE : (t + 1) * PIECE]
    keep_ref[...] = made[: BLOCKS // 2]
    send_ref[...] = made[BLOCKS // 2 :]


def input_body(
    wq_hbm, packed_grad_hbm, x_hbm, grad_hbm, vec_ref, back_ref, out_ref, sums_ref, wq, packed_grad, x_all, grad_all, wq_sem, sems
):
    sums_ref[...] = jnp.zeros_like(sums_ref)
    whole_copy = pltpu.make_async_copy(wq_hbm, wq, wq_sem)
    whole_copy.start()
    copies = []
    for image in range(MICRO):
        at = slice(image * IMG, (image + 1) * IMG)
        for index, (source, target) in enumerate(((packed_grad_hbm, packed_grad), (x_hbm, x_all), (grad_hbm, grad_all))):
            copies.append(pltpu.make_async_copy(source.at[at], target.at[at], sems.at[image, index]))
            copies[-1].start()
    whole_copy.wait()
    backs = []
    for image in range(MICRO):
        for copy in copies[3 * image : 3 * image + 3]:
            copy.wait()
        backs.append(dot_nt(packed_grad[image * IMG : (image + 1) * IMG, :], wq[...]))
    made = []
    for image, back in enumerate(backs):
        at = slice(image * IMG, (image + 1) * IMG)
        unit, inverse = norm_parts(x_all[at, :].astype(F32))
        sums_ref[0:1] += jnp.sum(back * unit, axis=0, keepdims=True)
        sums_ref[1:2] += jnp.sum(back, axis=0, keepdims=True)
        made.append((grad_all[at, :] + norm_back(back, unit, inverse, vec_ref[0:1])).astype(LOW))
    for image in range(MICRO):
        put_back(made[image], back_ref, out_ref, image)


def adam_update(weight, first, second, gradient, rate, decay):
    first_new = BETA_ONE * first + (1.0 - BETA_ONE) * gradient
    second_new = BETA_TWO * second + (1.0 - BETA_TWO) * gradient * gradient
    first_hat = first_new / (1.0 - BETA_ONE**STEP)
    second_hat = second_new / (1.0 - BETA_TWO**STEP)
    weight_new = weight * (1.0 - rate * decay) - rate * first_hat / (jnp.sqrt(second_hat) + ADAM_EPS)
    return (weight_new, first_new, second_new)


def adam_body(near_ref, far_ref, spare_ref, *refs):
    olds, news = refs[:18], refs[18:]
    vec, table = spare_ref[0:12], spare_ref[12:24, :REL]
    total = spare_ref[24:25, 0:1]
    total = total + jnp.sum(jnp.sum(vec * vec, axis=1, keepdims=True), axis=0, keepdims=True)
    total = total + jnp.sum(jnp.sum(table * table, axis=1, keepdims=True), axis=0, keepdims=True)
    grad_norm = jnp.sqrt(total)
    factor = jnp.minimum(1.0, CLIP_NORM / (grad_norm + 1e-06))
    news[0][...] = grad_norm
    depth = far_ref.shape[0] // 2
    grads = [None, near_ref[:, 288:], far_ref[:depth], far_ref[depth:], vec, table]
    for index in range(6):
        weight, first, second = olds[index], olds[6 + index], olds[12 + index]
        rate, decay = (RATE_MATRIX, DECAY_MATRIX) if index < 4 else (RATE_VECTOR, 0.0)
        for w in range(3 if index == 0 else 1):
            pick = (w,) if index == 0 else (Ellipsis,)
            gradient = near_ref[:, w * 96 : (w + 1) * 96] if index == 0 else grads[index]
            made = adam_update(weight[pick], first[pick], second[pick], gradient * factor, rate, decay)
            for kind in range(3):
                news[1 + 3 * index + kind][pick] = made[kind]


def body(
    mesh_sizes, tokens_in, cotangent, route, extent, qkv_weight, proj_weight, fc1_weight, fc2_weight, vectors, rel_table,
    qkv_first, proj_first, fc1_first, fc2_first, vectors_first, table_first,
    qkv_second, proj_second, fc1_second, fc2_second, vectors_second, table_second,
):
    toks, heads = mesh_sizes
    devices = toks * heads
    direct = toks == 8 and heads == 4
    micro = tokens_in.shape[0]
    patches = micro * devices * GRID * GRID
    head_at = lax.axis_index("head")
    me = lax.axis_index("tok") * heads + head_at
    def tie(*arrays):
        return lax.optimization_barrier(arrays)

    def passed(rows, mask):
        return lax.ppermute(rows, BOTH, [(i, i ^ mask) for i in range(devices)])

    depth = fc1_weight.shape[0]
    near, far = pl.pallas_call(
        pack_body, out_shape=(sds((depth, C), LOW), sds((2 * depth, C), LOW)), compiler_params=whole(8), name="pack"
    )(*streamed(qkv_weight, proj_weight.T, fc1_weight, fc2_weight.T))

    def gather_plain(piece):
        spread = lax.all_gather(lax.all_gather(piece, "tok", axis=0), "head", axis=0)
        half = piece.shape[0] // depth
        spread = spread.reshape(heads, toks, half, depth, C).transpose(0, 2, 1, 3, 4)
        spread = spread.reshape(heads, half, 8, PIECE, C).transpose(0, 2, 1, 3, 4)
        spread = spread.reshape(BLOCKS, half * PIECE, C)
        return [spread[at : at + 4] for at in range(0, BLOCKS, 4)]

    def share_plain(keep, send):
        both = jnp.concatenate([keep, send], axis=0)
        half = both.shape[1] // PIECE
        both = both.reshape(heads, 8, half, PIECE, C).transpose(0, 2, 1, 3, 4)
        both = both.reshape(heads, half, toks, depth, C).transpose(0, 2, 1, 3, 4).reshape(devices, half * depth, C)
        both = lax.psum_scatter(both.astype(F32), "head", scatter_dimension=0, tiled=True)
        return lax.psum_scatter(both, "tok", scatter_dimension=0, tiled=True)[0]

    def join(*arrays):
        return jnp.concatenate(arrays, axis=0)

    def first_sum(keep, got):
        shape = (4,) + keep.shape[1:]
        stays, *goes = pl.pallas_call(
            first_sum_body, out_shape=[sds(shape, F32)] + [sds(shape, LOW)] * 3, compiler_params=whole(2), name="first_sum"
        )(keep, got)
        return stays, goes

    def plane_sum(stays, got):
        shape = (1,) + stays.shape[1:]
        rest, *goes = pl.pallas_call(
            plane_sum_body, out_shape=[sds(shape, F32)] + [sds(shape, LOW)] * 3, compiler_params=whole(2), name="plane_sum"
        )(stays, *got)
        return rest, goes

    def spread(rows, masks):
        return [passed(rows, mask) for mask in masks]

    def sent(parts, masks):
        return [passed(part, mask) for part, mask in zip(parts, masks)]

    def total_of(rows, masks):
        one, two, three = spread(rows, masks)
        return (rows + one) + (two + three)

    back = jnp.asarray(DEAL.T, LOW)
    deal = jnp.asarray(DEAL, LOW)
    place = jnp.asarray(PLACE)
    reach = jnp.asarray(REACH)
    heads_low = jnp.asarray(HEADS, LOW)
    def prepare(tokens, cotangents):
        image = (MICRO, 1, GRID, GRID, C)
        return call(
            prep_body,
            [((ROWS, C), LOW)] * 3,
            (tokens, cotangents, deal, vectors),
            "prep",
            scratch=[
                pltpu.VMEM(image, LOW), pltpu.VMEM(image, LOW), pltpu.VMEM((IMG, PAD), LOW), pltpu.VMEM((12, C), F32),
                pltpu.VMEM((ROWS, C), LOW), pltpu.VMEM((ROWS, C), LOW), pltpu.VMEM((MICRO, 2, PAD, C), LOW),
                pltpu.SemaphoreType.DMA((4,)), pltpu.SemaphoreType.DMA((MICRO, 2)),
            ],
            fetched=4,
            stored=2,
        )

    def product_of(values, lookup):
        first = lax.reduce_precision(values, 8, 7)
        second = lax.reduce_precision(values - first, 8, 7)
        parts = jnp.concatenate([first, second, values - first - second], axis=0).astype(LOW)
        made = jnp.dot(parts, jnp.asarray(lookup, LOW), preferred_element_type=F32).reshape(3, values.shape[0], -1)
        return made[0] + (made[1] + made[2])

    def make_bias(values):
        made = product_of(values.T, LOOKUP).reshape(GROUPS, GROUP * WIN, WIN)
        return jnp.concatenate([made, made], axis=2)

    if direct:
        near = near[None]
        near_got, far_got = spread(near, LINE), spread(far[None], LINE)
        near_all = join(near, *near_got)
        near_all, tokens, cotangents, extent, route, rel_bias = tie(near_all, tokens_in, cotangent, extent, route, rel_table)
        near_all = [near_all] + spread(near_all, PLANE)
        x_rows, g_rows, n_rows = prepare(tokens, cotangents)
        table = jnp.concatenate(
            [
                jnp.stack([me, swap_bits(me)]).astype(jnp.int32),
                lax.dynamic_index_in_dim(extent, head_at, 1, False).reshape(-1),
                lax.dynamic_index_in_dim(route, head_at, 1, False).reshape(-1),
            ]
        )
        bias = make_bias(rel_bias)
        bias, table, n_rows, *near_all = tie(bias, table, n_rows, *near_all)
        far_got[0], near_all[0] = tie(far_got[0], near_all[0])
        far_all = join(far[None], *far_got)
        near_all = near_all + [passed(piece, CORE) for piece in near_all]
        far_got = [far_all] + spread(far_all, PLANE)
    else:
        x_rows, g_rows, n_rows = prepare(tokens_in, cotangent)
        table = jnp.concatenate(
            [
                jnp.stack([me, swap_bits(me)]).astype(jnp.int32),
                lax.dynamic_index_in_dim(extent, head_at, 1, False).reshape(-1),
                lax.dynamic_index_in_dim(route, head_at, 1, False).reshape(-1),
            ]
        )
        bias = make_bias(rel_table)
        near_all, far_all = gather_plain(near), gather_plain(far)

    packed, soft, attn, w_qkv, w_proj = call(
        functools.partial(attend_body, direct),
        [
            ((ROWS, 3 * C), LOW), ((MICRO, 2 * GROUPS, GROUP * WIN, 128), LOW), ((ROWS, C), LOW), ((C, 3 * C), LOW), ((C, C), LOW),
        ],
        (table, n_rows, vectors, bias, reach, place, heads_low, *near_all),
        "attend",
        limit=8,
        scratch=[pltpu.VMEM((4, C, C), LOW)],
        flops=8e9,
        scalars=1,
    )

    if direct:
        attn, *far_got = tie(attn, *far_got)
        far_core = [passed(piece, CORE) for piece in far_got]

    middle, n_two = call(middle_body, [((ROWS, C), F32), ((ROWS, C), LOW)], (attn, x_rows, w_proj, vectors), "middle",
        limit=4)

    if direct:
        middle, *far_core = tie(middle, *far_core)
        far_all = far_got + far_core

    hidden, grad_hidden, grad_middle, sums_mlp, w_fc2 = call(
        functools.partial(mlp_body, direct),
        [((ROWS, FF), LOW), ((ROWS, FF), LOW), ((ROWS, C), F32), ((12, C), F32), ((C, FF), LOW)],
        (table, middle, n_two, g_rows, vectors, *far_all),
        "mlp",
        limit=8,
        scratch=[pltpu.VMEM((C, FF), LOW), pltpu.VMEM((1, FF), F32), pltpu.VMEM((1, FF), F32)],
        flops=10e9,
        scalars=1,
    )

    half = BLOCKS // 2
    far_keep, far_send = call(
        functools.partial(mlp_weights_body, direct),
        [((half, 2 * PIECE, C), LOW)] * 2,
        (table, n_two, g_rows, hidden, grad_hidden),
        "mlp_weights",
        limit=14,
        scratch=[
            pltpu.VMEM((C, ROWS), LOW), pltpu.VMEM((C, ROWS), LOW), pltpu.VMEM((BLOCKS, 2 * PIECE, C), LOW),
            pltpu.VMEM((C, FF), LOW), pltpu.VMEM((C, FF), LOW),
        ],
        flops=4e9,
        scalars=1,
    )

    if direct:
        far_got = passed(far_send, CORE)

    (block_out,) = call(output_body, [(tokens_in.shape, LOW)], (hidden, w_fc2, middle, vectors, back), "output",
        limit=5, flops=2e9)

    if direct:
        block_out, far_got, grad_middle = tie(block_out, far_got, grad_middle)
        far_stays, far_goes = first_sum(far_keep, far_got)
        far_got = sent(far_goes, PLANE)

    packed_grad, grad_low, bias_sum, sums_attend = call(
        attend_back_body,
        [((ROWS, 3 * C), LOW), ((ROWS, C), LOW), ((GROUPS, GROUP * WIN, 128), F32), ((2, C), F32)],
        (table, grad_middle, packed, soft, w_proj, place, heads_low),
        "attend_back",
        limit=6,
        flops=8e9,
        scalars=1,
    )

    near_keep, near_send = call(
        functools.partial(attend_weights_body, direct),
        [((half, PIECE, C), LOW)] * 2,
        (table, n_rows, grad_low, packed_grad, attn),
        "attend_weights",
        limit=8,
        scratch=[pltpu.VMEM((BLOCKS, PIECE, C), LOW)],
        flops=2e9,
        scalars=1,
    )

    if direct:
        near_send, *far_got = tie(near_send, *far_got)
        near_got = passed(near_send, CORE)
        near_stays, near_goes = first_sum(near_keep, near_got)
        near_goes[0], packed_grad, bias_sum = tie(near_goes[0], packed_grad, bias_sum)
        near_got = sent(near_goes, PLANE)

    bias_sum = (bias_sum[:, :, :WIN] + bias_sum[:, :, WIN:]).reshape(NH, WIN * WIN)
    table_grad = product_of(bias_sum, LOOKUP.T)
    if direct:
        table_grad, *far_got = tie(table_grad, *far_got)
        far_stays, far_goes = plane_sum(far_stays, far_got)
        far_got = sent(far_goes, LINE)

    grad_block, sums_input = call(
        input_body,
        [(tokens_in.shape, LOW), ((2, C), F32)],
        (w_qkv, packed_grad, x_rows, grad_middle, vectors, back),
        "input_grad",
        scratch=[
            pltpu.VMEM((C, 3 * C), LOW), pltpu.VMEM((ROWS, 3 * C), LOW), pltpu.VMEM((ROWS, C), LOW), pltpu.VMEM((ROWS, C), F32),
            pltpu.SemaphoreType.DMA, pltpu.SemaphoreType.DMA((MICRO, 3)),
        ],
        flops=4e9,
        fetched=4,
    )

    vec_grad = jnp.concatenate([sums_input, sums_attend, sums_mlp[4:]], axis=0)
    if direct:
        grad_block, vec_grad, table_grad, *near_got = tie(grad_block, vec_grad, table_grad, *near_got)
        near_stays, near_goes = plane_sum(near_stays, near_got)
        near_got = sent(near_goes, LINE)
        near_grad, far_grad, spare = pl.pallas_call(
            functools.partial(finish_body, patches),
            out_shape=[sds((depth, C), F32), sds((2 * depth, C), F32), sds((32, C), F32)],
            compiler_params=whole(2),
            name="finish",
        )(near_stays, far_stays, vec_grad, table_grad, *near_got, *far_got)
        spare = spare + passed(spare, CORE)
        spare = total_of(spare, PLANE)
        spare = total_of(spare, LINE)
    else:
        near_grad, far_grad = share_plain(near_keep, near_send) / patches, share_plain(far_keep, far_send) / patches
        squares = jnp.sum(near_grad * near_grad) + jnp.sum(far_grad * far_grad)
        vec_grad, table_grad, squares = lax.psum((vec_grad, table_grad, squares), BOTH)
        table_grad = jnp.concatenate([table_grad, jnp.zeros((12, C - REL), F32)], axis=1)
        spare = jnp.concatenate([vec_grad / patches, table_grad / patches, jnp.broadcast_to(squares, (8, C))], axis=0)

    olds = (
        qkv_weight, proj_weight.T, fc1_weight, fc2_weight.T, vectors, rel_table.T,
        qkv_first, proj_first.T, fc1_first, fc2_first.T, vectors_first, table_first.T,
        qkv_second, proj_second.T, fc1_second, fc2_second.T, vectors_second, table_second.T,
    )
    shapes = [sds((1, 1), F32)] + [sds(olds[index].shape, F32) for index in range(6) for _ in range(3)]
    news = pl.pallas_call(
        adam_body,
        out_shape=shapes,
        compiler_params=whole(8),
        name="adam",
    )(near_grad, far_grad, spare, *olds)
    turned = [new.T if index // 3 in (1, 3, 5) else new for index, new in enumerate(news[1:])]
    return (block_out, grad_block, news[0][0, 0], *turned)


def solution(mesh):
    sizes = (mesh.shape["tok"], mesh.shape["head"])
    weights = (P(None, "tok", "head"), P("head", "tok"), P("tok", "head"), P("head", "tok"), P(), P())
    images = P(None, ("tok", "head"), None, None, None)
    return jax.shard_map(
        lambda *args: body(sizes, *args),
        mesh=mesh,
        in_specs=(images, images, P(None, "tok", None), P(None, "tok", None)) + weights * 3,
        out_specs=(images, images, P()) + tuple(spec for spec in weights for _ in range(3)),
        check_vma=False,
    )
```

```python
import functools
import math

import jax
import jax.numpy as jnp
import numpy as np
from jax import lax
from jax.experimental import pallas as pl
from jax.experimental.pallas import tpu as pltpu
from jax.sharding import PartitionSpec as P

C = 384
NH = 12
HD = 32
FF = 1536
WS = 7
SHIFT = 3
STEP = 10
GRID = 14
CELLS = WS * WS
REL = (2 * WS - 1) ** 2
MICRO = 5

WIN = 64
IMG = 4 * WIN
PAD = 16 * GRID
ROWS = MICRO * IMG
GROUP = 4
GROUPS = NH // GROUP
LANES = GROUP * HD
BLOCKS = 32
PIECE = 48
EARLY = 16
TALL, WIDE = 320, 256

EPS_NORM = 1e-05
BETA_ONE = 0.9
BETA_TWO = 0.999
ADAM_EPS = 1e-08
RATE_MATRIX = 0.08
RATE_VECTOR = 1.0
DECAY_MATRIX = 0.05
CLIP_NORM = 0.05
NEG_FILL = -1e30
HIGH = lax.Precision.HIGHEST
LOW = jnp.bfloat16
F32 = jnp.float32
NEVER = 99.0
BOTH = ("tok", "head")
MASKS = (16, 8, 2, 4, 1)
CORE, PLANE, LINE = 1, (2, 4, 6), (16, 8, 24)
PIECES = 8
ME, SLOT, EXTENT, ROUTE = 0, 1, 2, 12


def swap_bits(position):
    return sum((position & mask) // mask << bit for bit, mask in enumerate(MASKS))


def block_at(place):
    return sum(((place >> bit) & 1) * mask for bit, mask in enumerate(MASKS))


def window_tables():
    cell = np.arange(WIN)
    real = cell < CELLS
    rolled_row = np.stack([WS * (w // 2) + cell // WS for w in range(4)])
    rolled_col = np.stack([WS * (w % 2) + cell % WS for w in range(4)])
    source_row = (rolled_row + SHIFT) % GRID
    source_col = (rolled_col + SHIFT) % GRID

    def band(position):
        return np.where(position < GRID - WS, 0, np.where(position < GRID - SHIFT, 1, 2))

    label_row = (rolled_row + SHIFT) % GRID
    label_col = (rolled_col + SHIFT) % GRID
    region = 3 * band(label_row) + band(label_col)
    label_row = (label_row + SHIFT) % GRID
    label_col = (label_col + SHIFT) % GRID
    deal = np.zeros((IMG, PAD), np.float32)
    for w in range(4):
        for c in range(CELLS):
            deal[w * WIN + c, 16 * source_row[w, c] + source_col[w, c]] = 1.0
    place = np.full((2, IMG, 128), NEVER, np.float32)
    place[0] = np.where(real[None], source_row, NEVER).reshape(IMG, 1)
    place[1] = np.where(real[None], source_col, NEVER).reshape(IMG, 1)
    reach = np.full((2, 2, WIN, 128), NEVER, np.float32)
    for pair in range(2):
        for side in range(2):
            w = 2 * pair + side
            same = (region[w][:, None] == region[w][None, :]) & real[:, None] & real[None, :]
            for kind, source in enumerate((label_row, label_col)):
                far = np.where(same, np.maximum(source[w][:, None], source[w][None, :]), NEVER)
                far = np.where(np.eye(WIN, dtype=bool) & real[:, None], -1.0, far)
                reach[pair, kind, :, side * WIN : (side + 1) * WIN] = far
    offset = (2 * WS - 1) * (cell // WS) + cell % WS
    shifts = [int(value) for value in offset[:CELLS]]
    wanted = np.where(real, offset + REL // 2, -1)
    lookup = (np.arange(256)[:, None] == np.concatenate([wanted, wanted])[None, :]).astype(np.float32)
    heads = (np.arange(LANES)[None, :] // HD == np.arange(GROUP)[:, None]).astype(np.float32)
    heads = np.repeat(np.concatenate([heads, heads], axis=1), WIN, axis=0)
    return deal, place, reach, lookup, heads, shifts


DEAL, PLACE, REACH, LOOKUP, HEADS, SHIFTS = window_tables()


def dot_nn(a, b):
    return lax.dot_general(a, b, (((1,), (0,)), ((), ())), preferred_element_type=F32)


def dot_nt(a, b):
    return lax.dot_general(a, b, (((1,), (1,)), ((), ())), preferred_element_type=F32)


def dot_tn(a, b):
    return lax.dot_general(a, b, (((0,), (0,)), ((), ())), preferred_element_type=F32)


def turned(a, eye):
    return dot_nt(eye, a).astype(LOW)


def identity():
    row = lax.broadcasted_iota(jnp.int32, (128, 128), 0)
    return jnp.where(row == lax.broadcasted_iota(jnp.int32, (128, 128), 1), 1.0, 0.0).astype(LOW)


def norm_parts(rows):
    average = jnp.mean(rows, axis=-1, keepdims=True)
    centered = rows - average
    inverse = lax.rsqrt(jnp.mean(centered * centered, axis=-1, keepdims=True) + EPS_NORM)
    return centered * inverse, inverse


def norm_back(gradient, normed, inverse, gain):
    scaled = gradient * gain
    return inverse * (
        scaled
        - jnp.mean(scaled, axis=-1, keepdims=True)
        - normed * jnp.mean(scaled * normed, axis=-1, keepdims=True)
    )


def gelu_parts(pre_act):
    below = 0.5 + 0.5 * lax.erf(pre_act * 2.0 ** (-0.5))
    return below, jnp.exp(-0.5 * pre_act * pre_act) * (2.0 * math.pi) ** (-0.5)


SCALARS = pl.BlockSpec(memory_space=pltpu.SMEM)
HELD = pl.BlockSpec(memory_space=pltpu.VMEM)


def call(body, outs, inputs, name, limit=16, scratch=(), flops=1e9, scalars=0, fetched=0, stored=0):
    inputs = list(inputs)
    remote = slice(scalars, scalars + fetched)
    inputs[remote] = [pltpu.with_memory_space_constraint(array, pltpu.HBM) for array in inputs[remote]]
    far = pl.BlockSpec(memory_space=pltpu.HBM)
    return pl.pallas_call(
        body,
        in_specs=[SCALARS] * scalars + [far] * fetched + [HELD] * (len(inputs) - scalars - fetched),
        out_specs=[far] * stored + [HELD] * (len(outs) - stored),
        out_shape=[
            pltpu.HBM(shape, dtype) if index < stored else jax.ShapeDtypeStruct(shape, dtype)
            for index, (shape, dtype) in enumerate(outs)
        ],
        scratch_shapes=list(scratch),
        compiler_params=whole(limit),
        cost_estimate=pl.CostEstimate(flops=int(flops), bytes_accessed=4000000, transcendentals=0),
        name=name,
    )(*inputs)


def image_rows(image):
    return pl.ds(pl.multiple_of(image * IMG, IMG), IMG)


def whole(limit):
    return pltpu.CompilerParams(vmem_limit_bytes=limit * 1024 * 1024)


def sds(shape, dtype):
    return jax.ShapeDtypeStruct(shape, dtype)


def streamed(*arrays):
    return [pltpu.with_memory_space_constraint(array, pltpu.HBM) for array in arrays]


def row_mask(place_ref, table_ref, image):
    parts = []
    for w in range(4):
        rows = slice(w * WIN, (w + 1) * WIN)
        high = jnp.where(table_ref[ROUTE + 4 * image + w] >= 0, table_ref[EXTENT + 2 * image], -1).astype(F32)
        wide = table_ref[EXTENT + 2 * image + 1].astype(F32)
        inside = (place_ref[0, rows] < high) & (place_ref[1, rows] < wide)
        parts.append(jnp.where(inside, 1.0, 0.0))
    return jnp.concatenate(parts, axis=0)


def pack_body(qkv_ref, proj_ref, fc1_ref, fc2_ref, near_ref, far_ref):
    depth = fc1_ref.shape[0]
    early = near_ref.shape[0] - depth
    near_ref[:depth] = jnp.concatenate([qkv_ref[0], qkv_ref[1], qkv_ref[2], proj_ref[...]], axis=1).astype(LOW)
    near_ref[depth:] = fc1_ref[:early].astype(LOW)
    far_ref[: depth - early] = fc1_ref[early:].astype(LOW)
    far_ref[depth - early :] = fc2_ref[...].astype(LOW)


def first_sum_body(keep_ref, got_ref, stays_ref, *goes_refs):
    stays_ref[...] = keep_ref[:4].astype(F32) + got_ref[:4].astype(F32)
    for index, goes in enumerate(goes_refs):
        at = 4 * (index + 1)
        goes[...] = (keep_ref[at : at + 4].astype(F32) + got_ref[at : at + 4].astype(F32)).astype(LOW)


def plane_sum_body(stays_ref, *refs):
    got, (rest, *goes) = refs[:3], refs[3:]
    for at in range(4):
        total = stays_ref[at : at + 1] + got[0][at : at + 1].astype(F32)
        total = total + (got[1][at : at + 1].astype(F32) + got[2][at : at + 1].astype(F32))
        if at == 0:
            rest[...] = total
        else:
            goes[at - 1][...] = total.astype(LOW)


def finish_body(patches, near_ref, far_ref, vec_ref, table_ref, *refs):
    near_got, far_got, (near_grad, far_grad, spare) = refs[:3], refs[3:6], refs[6:]
    squares = jnp.zeros((1, 1), F32)
    for stays, got, target in ((near_ref, near_got, near_grad), (far_ref, far_got, far_grad)):
        total = stays[0] + got[0][0].astype(F32) + (got[1][0].astype(F32) + got[2][0].astype(F32))
        total = total * (1.0 / patches)
        target[...] = total
        squares = squares + jnp.sum(jnp.sum(total * total, axis=1, keepdims=True), axis=0, keepdims=True)
    spare[0:12] = vec_ref[...] * (1.0 / patches)
    spare[12:24] = jnp.zeros((12, C), F32)
    spare[12:24, :REL] = table_ref[...] * (1.0 / patches)
    spare[24:32] = jnp.broadcast_to(squares, (8, C))


def three_parts(values):
    first = values.astype(LOW).astype(F32)
    second = (values - first).astype(LOW).astype(F32)
    return jnp.concatenate([first, second, values - first - second], axis=0)


def fetch(pairs, sems):
    copies = [pltpu.make_async_copy(source, target, sems.at[index]) for index, (source, target) in enumerate(pairs)]
    for copy in copies:
        copy.start()
    return copies


def deal_rows(source, deal, pad, image):
    for r in range(GRID):
        pad[image, 16 * r : 16 * r + GRID, :] = source[image, 0, r]
    return dot_nn(deal[...], pad[image])


def prep_body(
    table_hbm, lookup_hbm, vec_hbm, deal_hbm, tok_hbm, x_hbm, unit_hbm, n_ref, bias_ref,
    table, lookup, vec, deal, tok, x_all, unit_all, padded, pad, sems, out_sems
):
    copies = fetch(
        ((table_hbm, table), (lookup_hbm, lookup), (vec_hbm, vec), (deal_hbm, deal), (tok_hbm, tok)), sems
    )
    padded[...] = jnp.zeros_like(padded)
    pad[...] = jnp.zeros_like(pad)
    bias_ref[...] = jnp.zeros_like(bias_ref)
    copies[0].wait()
    padded[:NH, :REL] = table[...]
    parts = three_parts(padded[...])
    moved = [pltpu.roll(parts, shift, 1) if shift else parts for shift in SHIFTS]
    copies[1].wait()
    spread = dot_nn(jnp.concatenate(moved, axis=0).astype(LOW), lookup[...])
    for k in range(CELLS):
        rows = spread[48 * k : 48 * k + 48]
        bias_ref[pl.ds(k, NH, stride=WIN), :] = (rows[:16] + (rows[16:32] + rows[32:]))[:NH]
    for copy in copies[2:]:
        copy.wait()
    stores, made = [], []
    for image in range(MICRO):
        at = slice(image * IMG, (image + 1) * IMG)
        made.append(deal_rows(tok, deal, pad, image))
        x_all[at, :] = made[-1].astype(LOW)
        stores.append(pltpu.make_async_copy(x_all.at[at], x_hbm.at[at], out_sems.at[image, 0]))
        stores[-1].start()
    for image in range(MICRO):
        at = slice(image * IMG, (image + 1) * IMG)
        unit, _ = norm_parts(made[image])
        unit_all[at, :] = unit.astype(LOW)
        stores.append(pltpu.make_async_copy(unit_all.at[at], unit_hbm.at[at], out_sems.at[image, 1]))
        stores[-1].start()
        n_ref[at, :] = (unit * vec[0:1] + vec[1:2]).astype(LOW)
    for store in stores:
        store.wait()


def prep_grad_body(deal_hbm, cot_hbm, g_ref, deal, cot, pad, sems):
    copies = fetch(((deal_hbm, deal), (cot_hbm, cot)), sems)
    pad[...] = jnp.zeros_like(pad)
    for copy in copies:
        copy.wait()
    for image in range(MICRO):
        g_ref[image * IMG : (image + 1) * IMG, :] = deal_rows(cot, deal, pad, image).astype(LOW)


def table_body(sums_ref, lookup_ref, table_ref, padded):
    padded[...] = jnp.zeros_like(padded)
    slabs = []
    for k in range(CELLS):
        padded[:NH, :] = sums_ref[pl.ds(k, NH, stride=WIN), :]
        slabs.append(three_parts(padded[...]))
    made = dot_nt(jnp.concatenate(slabs, axis=0).astype(LOW), lookup_ref[...])
    total = jnp.zeros((16, 256), F32)
    for k, shift in enumerate(SHIFTS):
        rows = made[48 * k : 48 * k + 48]
        rows = rows[:16] + (rows[16:32] + rows[32:])
        total = total + (pltpu.roll(rows, 256 - shift, 1) if shift else rows)
    table_ref[...] = total[:NH, :REL]


def put_back(rows, back_ref, target, image):
    grid = dot_nn(back_ref[...], rows.astype(LOW)).astype(LOW)
    for r in range(GRID):
        target[image, 0, r] = grid[16 * r : 16 * r + GRID]


def spread_keys(part, heads_ref):
    wide = jnp.concatenate([part[:WIN], part[WIN:]], axis=1)
    return jnp.concatenate([wide] * GROUP, axis=0) * heads_ref[...]


def spread_rows(part):
    zero = jnp.zeros((WIN, LANES), part.dtype)
    top = jnp.concatenate([part[:WIN], zero], axis=1)
    return jnp.concatenate([top, jnp.concatenate([zero, part[WIN:]], axis=1)], axis=0)


def own_rows(product):
    return jnp.concatenate([product[:WIN, :LANES], product[WIN:, LANES:]], axis=0)


def own_keys(product, heads_ref):
    kept = product * heads_ref[...].astype(F32)
    total = kept[:WIN]
    for h in range(1, GROUP):
        total = total + kept[h * WIN : (h + 1) * WIN]
    return jnp.concatenate([total[:, :LANES], total[:, LANES:]], axis=0)


def attend_body(
    direct, table_ref, n_ref, vec_ref, bias_ref, reach_ref, place_ref, heads_ref, *refs,
):
    near_refs, (packed_ref, soft_ref, attn_ref, wq_ref, wp_ref, parts) = refs[:PIECES], refs[PIECES:]
    for j in range(BLOCKS):
        at = table_ref[ME] ^ block_at(j) if direct else (j % 8) * 4 + j // 8
        row = at // 4 * PIECE if not direct else pl.multiple_of((at >> 2) * PIECE, PIECE)
        parts[at & 3, pl.ds(row, PIECE), :] = near_refs[j // 4][j % 4, :PIECE]
    for w in range(3):
        wq_ref[:, w * C : (w + 1) * C] = jnp.concatenate([parts[h, :, w * 96 : (w + 1) * 96] for h in range(4)], axis=1)
    wp_ref[...] = jnp.concatenate([parts[h, :, 288:] for h in range(4)], axis=1)

    @pl.loop(0, MICRO)
    def _(image):
        at_image = image_rows(image)
        made = dot_nn(n_ref[at_image, :], wq_ref[...])
        packed_ref[at_image, :C] = (made[:, :C] + vec_ref[2:3]).astype(LOW)
        packed_ref[at_image, C : 2 * C] = made[:, C : 2 * C].astype(LOW)
        packed_ref[at_image, 2 * C :] = (made[:, 2 * C :] + vec_ref[3:4]).astype(LOW)
        mask = row_mask(place_ref, table_ref, image)
        high = table_ref[EXTENT + 2 * image].astype(F32)
        wide = table_ref[EXTENT + 2 * image + 1].astype(F32)
        eye = identity()
        units = [(pair, g) for pair in range(2) for g in range(GROUPS)]
        at_pair = [pl.ds(pl.multiple_of(image * IMG + pair * 2 * WIN, 2 * WIN), 2 * WIN) for pair in range(2)]
        raws = []
        for pair, g in units:
            at = g * LANES
            queries = packed_ref[at_pair[pair], at : at + LANES]
            keys = packed_ref[at_pair[pair], C + at : C + at + LANES]
            raws.append(dot_nt(spread_keys(keys, heads_ref), spread_rows(queries)))
        softs = []
        for (pair, g), raw in zip(units, raws):
            allowed = (reach_ref[pair, 0] < high) & (reach_ref[pair, 1] < wide)
            raw = (raw * HD ** (-0.5) + bias_ref[g]).reshape(GROUP, WIN, 128)
            scores = jnp.where(allowed[None], raw, NEG_FILL)
            exponent = jnp.exp(scores - jnp.max(scores, axis=1, keepdims=True))
            soft = exponent * (1.0 / jnp.sum(exponent, axis=1, keepdims=True))
            soft = soft.reshape(GROUP * WIN, 128).astype(LOW)
            soft_ref[image, pair * GROUPS + g] = soft
            softs.append(soft)
        softs = [turned(soft, eye) for soft in softs]
        for (pair, g), soft in zip(units, softs):
            at = g * LANES
            values = packed_ref[at_pair[pair], 2 * C + at : 2 * C + at + LANES]
            result = own_rows(dot_nn(soft, spread_keys(values, heads_ref)))
            rows = slice(pair * 2 * WIN, (pair + 1) * 2 * WIN)
            attn_ref[at_pair[pair], at : at + LANES] = (result * mask[rows]).astype(LOW)


def middle_body(attn_ref, x_ref, wp_ref, vec_ref, middle_ref, n_ref):
    for image in range(MICRO):
        at = slice(image * IMG, (image + 1) * IMG)
        middle = x_ref[at, :].astype(F32) + dot_nt(attn_ref[at, :], wp_ref[...]) + vec_ref[4:5]
        middle_ref[at, :] = middle
        unit, _ = norm_parts(middle)
        n_ref[at, :] = (unit * vec_ref[5:6] + vec_ref[6:7]).astype(LOW)


def mlp_body(
    direct, table_ref, middle_ref, n_ref, g_ref, vec_ref, *refs,
):
    near_refs, far_refs, refs = refs[:PIECES], refs[PIECES : 2 * PIECES], refs[2 * PIECES :]
    (hidden_ref, grad_hidden_ref, grad_ref, sums_ref, w2_ref, w1, bias, bias_sum) = refs
    for j in range(BLOCKS):
        at = table_ref[ME] ^ block_at(j) if direct else (j % 8) * 4 + j // 8
        row = at // 4 * PIECE if not direct else pl.multiple_of((at >> 2) * PIECE, PIECE)
        col = at % 4 * C if not direct else pl.multiple_of((at & 3) * C, C)
        w1[pl.ds(row, EARLY), pl.ds(col, C)] = near_refs[j // 4][j % 4, PIECE:]
        w1[pl.ds(row + EARLY, PIECE - EARLY), pl.ds(col, C)] = far_refs[j // 4][j % 4, : PIECE - EARLY]
        w2_ref[pl.ds(row, PIECE), pl.ds(col, C)] = far_refs[j // 4][j % 4, PIECE - EARLY :]
    for r in range(4):
        bias[:, r * C : (r + 1) * C] = vec_ref[8 + r : 9 + r]
    sums_ref[...] = jnp.zeros_like(sums_ref)

    bias_sum[...] = jnp.zeros_like(bias_sum)
    for part in range(FF // WIDE):
        cols = slice(part * WIDE, (part + 1) * WIDE)
        for block in range(ROWS // TALL):
            at = slice(block * TALL, (block + 1) * TALL)
            pre_act = dot_nn(n_ref[at, :], w1[:, cols]) + bias[:, cols]
            grad_post = dot_nn(g_ref[at, :], w2_ref[:, cols])
            below, density = gelu_parts(pre_act)
            hidden_ref[at, cols] = (pre_act * below).astype(LOW)
            grad_pre = grad_post * (below + pre_act * density)
            grad_hidden_ref[at, cols] = grad_pre.astype(LOW)
            bias_sum[:, cols] += jnp.sum(grad_pre, axis=0, keepdims=True)
    for block in range(ROWS // TALL):
        at = slice(block * TALL, (block + 1) * TALL)
        back = dot_nt(grad_hidden_ref[at, :], w1[...])
        unit, inverse = norm_parts(middle_ref[at, :])
        g = g_ref[at, :].astype(F32)
        grad_middle = g + norm_back(back, unit, inverse, vec_ref[5:6])
        grad_ref[at, :] = grad_middle
        sums_ref[4:5] += jnp.sum(grad_middle, axis=0, keepdims=True)
        sums_ref[5:6] += jnp.sum(back * unit, axis=0, keepdims=True)
        sums_ref[6:7] += jnp.sum(back, axis=0, keepdims=True)
        sums_ref[7:8] += jnp.sum(g, axis=0, keepdims=True)
    for r in range(4):
        sums_ref[8 + r : 9 + r] = bias_sum[:, r * C : (r + 1) * C]


def place_of(direct, table_ref, t, h):
    if not direct:
        return h * 8 + t
    return table_ref[SLOT] ^ swap_bits(4 * t) ^ ((h & 1) * 16 + (h >> 1) * 4)


def mlp_weights_body(direct, table_ref, n_ref, g_ref, hidden_ref, grad_hidden_ref, keep_ref, send_ref, n_turned, g_turned, made, first, second):
    n_turned[...] = n_ref[...].T
    g_turned[...] = g_ref[...].T
    for part in range(3):
        cols = slice(part * 2 * WIDE, (part + 1) * 2 * WIDE)
        first[:, cols] = dot_nn(n_turned[...], grad_hidden_ref[:, cols]).astype(LOW)
        second[:, cols] = dot_nn(g_turned[...], hidden_ref[:, cols]).astype(LOW)
    for h in range(4):
        cols = slice(h * C, (h + 1) * C)
        for t in range(8):
            at = place_of(direct, table_ref, t, h)
            made[at, :PIECE] = first[t * PIECE : (t + 1) * PIECE, cols]
            made[at, PIECE:] = second[t * PIECE : (t + 1) * PIECE, cols]
    keep_ref[...] = made[: BLOCKS // 2]
    send_ref[...] = made[BLOCKS // 2 :]


def output_body(hidden_ref, w2_ref, middle_ref, vec_ref, back_ref, out_ref):
    made = []
    for image in range(MICRO):
        at = slice(image * IMG, (image + 1) * IMG)
        made.append((middle_ref[at, :] + dot_nt(hidden_ref[at, :], w2_ref[...]) + vec_ref[7:8]).astype(LOW))
    for image in range(MICRO):
        put_back(made[image], back_ref, out_ref, image)


def attend_back_body(
    table_ref, grad_ref, packed_ref, soft_ref, wp_ref, place_ref, heads_ref,
    packed_grad_ref, grad_low_ref, bias_sum_ref, sums_ref,
):
    bias_sum_ref[...] = jnp.zeros_like(bias_sum_ref)
    sums_ref[...] = jnp.zeros_like(sums_ref)

    @pl.loop(0, MICRO)
    def _(image):
        at_image = image_rows(image)
        grad_low = grad_ref[at_image, :].astype(LOW)
        grad_low_ref[at_image, :] = grad_low
        mask = row_mask(place_ref, table_ref, image)
        grad_attn = dot_nn(grad_low, wp_ref[...])
        grad_attn = (grad_attn * jnp.concatenate([mask] * 3, axis=1)).astype(LOW)
        eye = identity()
        units = [(pair, g) for pair in range(2) for g in range(GROUPS)]
        at_pair = [pl.ds(pl.multiple_of(image * IMG + pair * 2 * WIN, 2 * WIN), 2 * WIN) for pair in range(2)]
        incomings, grad_softs = [], []
        for pair, g in units:
            at = g * LANES
            values = packed_ref[at_pair[pair], 2 * C + at : 2 * C + at + LANES]
            incomings.append(spread_rows(grad_attn[pair * 2 * WIN : (pair + 1) * 2 * WIN, at : at + LANES]))
            grad_softs.append(dot_nt(spread_keys(values, heads_ref), incomings[-1]))
        grads = []
        for (pair, g), grad_soft in zip(units, grad_softs):
            soft = soft_ref[image, pair * GROUPS + g].astype(F32)
            joint = (soft * grad_soft).reshape(GROUP, WIN, 128)
            inner = jnp.sum(joint, axis=1, keepdims=True)
            grad_scores = (joint - soft.reshape(GROUP, WIN, 128) * inner).reshape(GROUP * WIN, 128)
            grads.append(grad_scores.astype(LOW))
            bias_sum_ref[g] += grads[-1].astype(F32)
        values_made = [dot_nn(soft_ref[image, pair * GROUPS + g], incoming) for (pair, g), incoming in zip(units, incomings)]
        turns = [turned(grad, eye) for grad in grads]
        keys_made, queries_made = [], []
        for (pair, g), grad, turn in zip(units, grads, turns):
            at = g * LANES
            queries = packed_ref[at_pair[pair], at : at + LANES]
            keys = packed_ref[at_pair[pair], C + at : C + at + LANES]
            keys_made.append(dot_nn(grad, spread_rows(queries)))
            queries_made.append(dot_nn(turn, spread_keys(keys, heads_ref)))
        for (pair, g), grad_values, grad_keys, grad_queries in zip(units, values_made, keys_made, queries_made):
            at = g * LANES
            rows = at_pair[pair]
            packed_grad_ref[rows, at : at + LANES] = (own_rows(grad_queries) * HD ** (-0.5)).astype(LOW)
            packed_grad_ref[rows, C + at : C + at + LANES] = (own_keys(grad_keys, heads_ref) * HD ** (-0.5)).astype(LOW)
            packed_grad_ref[rows, 2 * C + at : 2 * C + at + LANES] = own_keys(grad_values, heads_ref).astype(LOW)
        sums_ref[...] += jnp.sum(packed_grad_ref[at_image, :].astype(F32), axis=0, keepdims=True)


def attend_weights_body(
    direct, table_ref, unit_ref, grad_low_ref, packed_grad_ref, attn_ref, wq_ref, sums_ref, vec_ref, keep_ref, send_ref, norm_ref, made
):
    unit_turned = unit_ref[...].T
    turned_vec = vec_ref[...].T
    gain, shift = turned_vec[:, 0:1], turned_vec[:, 1:2]
    parts = []
    gain_grad = jnp.zeros((C, 1), F32)
    shift_grad = jnp.zeros((C, 1), F32)
    for w in range(3):
        cols = slice(w * C, (w + 1) * C)
        product = dot_nn(unit_turned, packed_grad_ref[:, cols])
        weight, sums = wq_ref[:, cols].astype(F32), sums_ref[:, cols]
        parts.append((product * gain + shift * sums).astype(LOW))
        gain_grad = gain_grad + jnp.sum(product * weight, axis=1, keepdims=True)
        shift_grad = shift_grad + jnp.sum(weight * sums, axis=1, keepdims=True)
    norm_ref[0:1] = jnp.broadcast_to(gain_grad, (C, 128)).T[0:1]
    norm_ref[1:2] = jnp.broadcast_to(shift_grad, (C, 128)).T[0:1]
    parts.append(dot_nn(grad_low_ref[...].T, attn_ref[...]).astype(LOW))
    for h in range(4):
        block = jnp.concatenate([part[:, h * 96 : (h + 1) * 96] for part in parts], axis=1)
        for t in range(8):
            made[place_of(direct, table_ref, t, h)] = block[t * PIECE : (t + 1) * PIECE]
    keep_ref[...] = made[: BLOCKS // 2]
    send_ref[...] = made[BLOCKS // 2 :]


def input_body(first, last, *refs):
    wq_hbm, packed_grad_hbm, x_hbm, grad_hbm = refs[:4]
    refs = refs[4 + (first > 0) :]
    vec_ref, back_ref, out_hbm, wq, packed_grad, x_all, grad_all, made, wq_sem, sems, out_sems = refs
    images = range(last - first)
    whole_copy = pltpu.make_async_copy(wq_hbm, wq, wq_sem)
    whole_copy.start()
    copies = []
    for image in images:
        source_at = slice((first + image) * IMG, (first + image + 1) * IMG)
        at = slice(image * IMG, (image + 1) * IMG)
        for index, (source, target) in enumerate(((packed_grad_hbm, packed_grad), (x_hbm, x_all), (grad_hbm, grad_all))):
            copies.append(pltpu.make_async_copy(source.at[source_at], target.at[at], sems.at[image, index]))
            copies[-1].start()
    whole_copy.wait()
    stores = []
    for image in images:
        at = slice(image * IMG, (image + 1) * IMG)
        for copy in copies[3 * image : 3 * image + 3]:
            copy.wait()
        back = dot_nt(packed_grad[at, :], wq[...])
        unit, inverse = norm_parts(x_all[at, :].astype(F32))
        rows = grad_all[at, :] + norm_back(back, unit, inverse, vec_ref[0:1])
        put_back(rows, back_ref, made, image)
        stores.append(pltpu.make_async_copy(made.at[image], out_hbm.at[first + image], out_sems.at[image]))
        stores[-1].start()
    for store in stores:
        store.wait()


def adam_update(weight, first, second, gradient, rate, decay):
    first_new = BETA_ONE * first + (1.0 - BETA_ONE) * gradient
    second_new = BETA_TWO * second + (1.0 - BETA_TWO) * gradient * gradient
    first_hat = first_new / (1.0 - BETA_ONE**STEP)
    second_hat = second_new / (1.0 - BETA_TWO**STEP)
    weight_new = weight * (1.0 - rate * decay) - rate * first_hat / (jnp.sqrt(second_hat) + ADAM_EPS)
    return (weight_new, first_new, second_new)


def adam_body(near_ref, far_ref, spare_ref, *refs):
    olds, news = refs[:18], refs[18:]
    vec, table = spare_ref[0:12], spare_ref[12:24, :REL]
    total = spare_ref[24:25, 0:1]
    total = total + jnp.sum(jnp.sum(vec * vec, axis=1, keepdims=True), axis=0, keepdims=True)
    total = total + jnp.sum(jnp.sum(table * table, axis=1, keepdims=True), axis=0, keepdims=True)
    grad_norm = jnp.sqrt(total)
    factor = jnp.minimum(1.0, CLIP_NORM / (grad_norm + 1e-06))
    news[0][...] = grad_norm
    depth = far_ref.shape[0] // 2
    grads = [None, near_ref[:, 288:], far_ref[:depth], far_ref[depth:], vec, table]
    for index in range(6):
        weight, first, second = olds[index], olds[6 + index], olds[12 + index]
        rate, decay = (RATE_MATRIX, DECAY_MATRIX) if index < 4 else (RATE_VECTOR, 0.0)
        for w in range(3 if index == 0 else 1):
            pick = (w,) if index == 0 else (Ellipsis,)
            gradient = near_ref[:, w * 96 : (w + 1) * 96] if index == 0 else grads[index]
            made = adam_update(weight[pick], first[pick], second[pick], gradient * factor, rate, decay)
            for kind in range(3):
                news[1 + 3 * index + kind][pick] = made[kind]


def body(
    mesh_sizes, tokens_in, cotangent, route, extent, qkv_weight, proj_weight, fc1_weight, fc2_weight, vectors, rel_table,
    qkv_first, proj_first, fc1_first, fc2_first, vectors_first, table_first,
    qkv_second, proj_second, fc1_second, fc2_second, vectors_second, table_second,
):
    toks, heads = mesh_sizes
    devices = toks * heads
    direct = toks == 8 and heads == 4
    micro = tokens_in.shape[0]
    patches = micro * devices * GRID * GRID
    head_at = lax.axis_index("head")
    me = lax.axis_index("tok") * heads + head_at
    def tie(*arrays):
        return lax.optimization_barrier(arrays)

    def passed(rows, mask):
        return lax.ppermute(rows, BOTH, [(i, i ^ mask) for i in range(devices)])

    depth = fc1_weight.shape[0]
    early = depth * EARLY // PIECE
    near, far = pl.pallas_call(
        pack_body, out_shape=(sds((depth + early, C), LOW), sds((2 * depth - early, C), LOW)), compiler_params=whole(8), name="pack"
    )(*streamed(qkv_weight, proj_weight.T, fc1_weight, fc2_weight.T))

    def gather_plain(piece):
        spread = lax.all_gather(lax.all_gather(piece, "tok", axis=0), "head", axis=0)
        return spread.reshape(BLOCKS, PIECE, C)

    def plain_pieces(near, far):
        one = gather_plain(near[:depth])
        two = gather_plain(jnp.concatenate([near[depth:], far[: depth - early]], axis=0))
        three = gather_plain(far[depth - early :])
        near = jnp.concatenate([one, two[:, :EARLY]], axis=1)
        far = jnp.concatenate([two[:, EARLY:], three], axis=1)
        return [[array[at : at + 4] for at in range(0, BLOCKS, 4)] for array in (near, far)]

    def share_plain(keep, send):
        both = jnp.concatenate([keep, send], axis=0)
        half = both.shape[1] // PIECE
        both = both.reshape(heads, 8, half, PIECE, C).transpose(0, 2, 1, 3, 4)
        both = both.reshape(heads, half, toks, depth, C).transpose(0, 2, 1, 3, 4).reshape(devices, half * depth, C)
        both = lax.psum_scatter(both.astype(F32), "head", scatter_dimension=0, tiled=True)
        return lax.psum_scatter(both, "tok", scatter_dimension=0, tiled=True)[0]

    def join(*arrays):
        return jnp.concatenate(arrays, axis=0)

    def first_sum(keep, got):
        shape = (4,) + keep.shape[1:]
        stays, *goes = pl.pallas_call(
            first_sum_body, out_shape=[sds(shape, F32)] + [sds(shape, LOW)] * 3, compiler_params=whole(2), name="first_sum"
        )(keep, got)
        return stays, goes

    def plane_sum(stays, got):
        shape = (1,) + stays.shape[1:]
        rest, *goes = pl.pallas_call(
            plane_sum_body, out_shape=[sds(shape, F32)] + [sds(shape, LOW)] * 3, compiler_params=whole(2), name="plane_sum"
        )(stays, *got)
        return rest, goes

    def spread(rows, masks):
        return [passed(rows, mask) for mask in masks]

    def sent(parts, masks):
        return [passed(part, mask) for part, mask in zip(parts, masks)]

    back = jnp.asarray(DEAL.T, LOW)
    deal = jnp.asarray(DEAL, LOW)
    lookup = jnp.asarray(LOOKUP, LOW)
    place = jnp.asarray(PLACE)
    reach = jnp.asarray(REACH)
    heads_low = jnp.asarray(HEADS, LOW)
    whole_images = pltpu.VMEM((MICRO, 1, GRID, GRID, C), LOW)

    def prepare(tokens, values):
        x_rows, unit_rows, n_rows, bias = call(
            prep_body,
            [((ROWS, C), LOW)] * 3 + [((NH * WIN, 128), F32)],
            (values.T, lookup, vectors, deal, tokens),
            "prep",
            scratch=[
                pltpu.VMEM((NH, REL), F32), pltpu.VMEM((256, 128), LOW), pltpu.VMEM((12, C), F32), pltpu.VMEM((IMG, PAD), LOW),
                whole_images, pltpu.VMEM((ROWS, C), LOW), pltpu.VMEM((ROWS, C), LOW), pltpu.VMEM((16, 256), F32),
                pltpu.VMEM((MICRO, PAD, C), LOW), pltpu.SemaphoreType.DMA((5,)), pltpu.SemaphoreType.DMA((MICRO, 2)),
            ],
            flops=1e9,
            fetched=5,
            stored=2,
        )
        return x_rows, unit_rows, n_rows, bias.reshape(GROUPS, GROUP * WIN, 128)

    def prepare_grad(cotangents):
        (g_rows,) = call(
            prep_grad_body,
            [((ROWS, C), LOW)],
            (deal, cotangents),
            "prep_grad",
            limit=8,
            scratch=[pltpu.VMEM((IMG, PAD), LOW), whole_images, pltpu.VMEM((MICRO, PAD, C), LOW), pltpu.SemaphoreType.DMA((2,))],
            fetched=2,
        )
        return g_rows

    if direct:
        near = near[None]
        near_got, far_got = spread(near, LINE), spread(far[None], LINE)
        near_all = join(near, *near_got)
        near_all = [near_all] + spread(near_all, PLANE)
        far_all = join(far[None], *far_got)
        far_all, tokens, extent, route, rel_bias = tie(far_all, tokens_in, extent, route, rel_table)
        x_rows, unit_rows, n_rows, bias = prepare(tokens, rel_bias)
        table = jnp.concatenate(
            [
                jnp.stack([me, swap_bits(me)]).astype(jnp.int32),
                lax.dynamic_index_in_dim(extent, head_at, 1, False).reshape(-1),
                lax.dynamic_index_in_dim(route, head_at, 1, False).reshape(-1),
            ]
        )
        bias, table, n_rows, *near_all = tie(bias, table, n_rows, *near_all)
        far_all, near_all[0] = tie(far_all, near_all[0])
        near_all = near_all + [passed(piece, CORE) for piece in near_all]
        far_got = [far_all] + spread(far_all, PLANE)
    else:
        x_rows, unit_rows, n_rows, bias = prepare(tokens_in, rel_table)
        table = jnp.concatenate(
            [
                jnp.stack([me, swap_bits(me)]).astype(jnp.int32),
                lax.dynamic_index_in_dim(extent, head_at, 1, False).reshape(-1),
                lax.dynamic_index_in_dim(route, head_at, 1, False).reshape(-1),
            ]
        )
        near_all, far_all = plain_pieces(near, far)

    packed, soft, attn, w_qkv, w_proj = call(
        functools.partial(attend_body, direct),
        [
            ((ROWS, 3 * C), LOW), ((MICRO, 2 * GROUPS, GROUP * WIN, 128), LOW), ((ROWS, C), LOW), ((C, 3 * C), LOW), ((C, C), LOW),
        ],
        (table, n_rows, vectors, bias, reach, place, heads_low, *near_all),
        "attend",
        limit=8,
        scratch=[pltpu.VMEM((4, C, C), LOW)],
        flops=8e9,
        scalars=1,
    )

    middle, n_two = call(middle_body, [((ROWS, C), F32), ((ROWS, C), LOW)], (attn, x_rows, w_proj, vectors), "middle",
        limit=4)

    late = cotangent
    if direct:
        middle, late, *far_got = tie(middle, late, *far_got)
        far_core = [passed(piece, CORE) for piece in far_got]
    g_rows = prepare_grad(late)
    if direct:
        g_rows, *far_core = tie(g_rows, *far_core)
        far_all = far_got + far_core

    hidden, grad_hidden, grad_middle, sums_mlp, w_fc2 = call(
        functools.partial(mlp_body, direct),
        [((ROWS, FF), LOW), ((ROWS, FF), LOW), ((ROWS, C), F32), ((12, C), F32), ((C, FF), LOW)],
        (table, middle, n_two, g_rows, vectors, *near_all, *far_all),
        "mlp",
        limit=8,
        scratch=[pltpu.VMEM((C, FF), LOW), pltpu.VMEM((1, FF), F32), pltpu.VMEM((1, FF), F32)],
        flops=10e9,
        scalars=1,
    )

    half = BLOCKS // 2
    far_keep, far_send = call(
        functools.partial(mlp_weights_body, direct),
        [((half, 2 * PIECE, C), LOW)] * 2,
        (table, n_two, g_rows, hidden, grad_hidden),
        "mlp_weights",
        limit=14,
        scratch=[
            pltpu.VMEM((C, ROWS), LOW), pltpu.VMEM((C, ROWS), LOW), pltpu.VMEM((BLOCKS, 2 * PIECE, C), LOW),
            pltpu.VMEM((C, FF), LOW), pltpu.VMEM((C, FF), LOW),
        ],
        flops=4e9,
        scalars=1,
    )

    if direct:
        far_got = passed(far_send, CORE)

    (block_out,) = call(output_body, [(tokens_in.shape, LOW)], (hidden, w_fc2, middle, vectors, back), "output",
        limit=5, flops=2e9)

    if direct:
        block_out, far_got, grad_middle = tie(block_out, far_got, grad_middle)
        far_stays, far_goes = first_sum(far_keep, far_got)
        far_got = sent(far_goes, PLANE)

    packed_grad, grad_low, bias_sum, sums_attend = call(
        attend_back_body,
        [((ROWS, 3 * C), LOW), ((ROWS, C), LOW), ((GROUPS, GROUP * WIN, 128), F32), ((1, 3 * C), F32)],
        (table, grad_middle, packed, soft, w_proj, place, heads_low),
        "attend_back",
        limit=6,
        flops=8e9,
        scalars=1,
    )

    vec_square = jnp.concatenate([vectors, jnp.zeros((4, C), F32)], axis=0)
    near_keep, near_send, sums_input = call(
        functools.partial(attend_weights_body, direct),
        [((half, PIECE, C), LOW)] * 2 + [((2, C), F32)],
        (table, unit_rows, grad_low, packed_grad, attn, w_qkv, sums_attend, vec_square),
        "attend_weights",
        limit=8,
        scratch=[pltpu.VMEM((BLOCKS, PIECE, C), LOW)],
        flops=2e9,
        scalars=1,
    )

    if direct:
        near_send, *far_got = tie(near_send, *far_got)
        near_got = passed(near_send, CORE)
        near_stays, near_goes = first_sum(near_keep, near_got)
        near_goes[0], bias_sum = tie(near_goes[0], bias_sum)
        near_got = sent(near_goes, PLANE)

    (table_grad,) = call(
        table_body,
        [((NH, REL), F32)],
        (bias_sum.reshape(NH * WIN, 128), lookup),
        "table_grad",
        limit=8,
        scratch=[pltpu.VMEM((16, 128), F32)],
        flops=1e8,
    )
    if direct:
        table_grad, *far_got = tie(table_grad, *far_got)
        far_stays, far_goes = plane_sum(far_stays, far_got)
        far_got = sent(far_goes, LINE)

    def input_piece(first, last, packed_grad, grad_block):
        count = last - first
        sources = [pltpu.with_memory_space_constraint(array, pltpu.HBM) for array in (w_qkv, packed_grad, x_rows, grad_middle)]
        sources += [] if grad_block is None else [pltpu.with_memory_space_constraint(grad_block, pltpu.HBM)]
        far = pl.BlockSpec(memory_space=pltpu.HBM)
        return pl.pallas_call(
            functools.partial(input_body, first, last),
            in_specs=[far] * len(sources) + [HELD] * 2,
            out_specs=far,
            out_shape=pltpu.HBM(tokens_in.shape, LOW),
            input_output_aliases={} if grad_block is None else {4: 0},
            scratch_shapes=[
                pltpu.VMEM((C, 3 * C), LOW), pltpu.VMEM((count * IMG, 3 * C), LOW), pltpu.VMEM((count * IMG, C), LOW),
                pltpu.VMEM((count * IMG, C), F32), pltpu.VMEM((count, 1, GRID, GRID, C), LOW),
                pltpu.SemaphoreType.DMA, pltpu.SemaphoreType.DMA((count, 3)), pltpu.SemaphoreType.DMA((count,)),
            ],
            compiler_params=whole(16),
            cost_estimate=pl.CostEstimate(flops=int(4e8 * count), bytes_accessed=2000000, transcendentals=0),
            name="input_grad",
        )(*sources, vectors, back)

    vec_grad = jnp.concatenate([sums_input, sums_attend[:, :C], sums_attend[:, 2 * C :], sums_mlp[4:]], axis=0)
    if direct:
        vec_grad, table_grad, far_got[0], *near_got = tie(vec_grad, table_grad, far_got[0], *near_got)
        near_stays, near_goes = plane_sum(near_stays, near_got)
        near_goes[0], packed_grad = tie(near_goes[0], packed_grad)
        near_got = sent(near_goes, LINE)
        grad_block = input_piece(0, 2, packed_grad, None)
        grad_block, *near_got = tie(grad_block, *near_got)
        near_grad, far_grad, spare = pl.pallas_call(
            functools.partial(finish_body, patches),
            out_shape=[sds((depth, C), F32), sds((2 * depth, C), F32), sds((32, C), F32)],
            compiler_params=whole(2),
            name="finish",
        )(near_stays, far_stays, vec_grad, table_grad, *near_got, *far_got)
        spare = spare + passed(spare, CORE)
        for masks, first, last in ((PLANE, 2, 4), (LINE, 4, 5)):
            spare, packed_grad = tie(spare, packed_grad)
            one, two, three = spread(spare, masks)
            grad_block = input_piece(first, last, packed_grad, grad_block)
            grad_block, one, two, three = tie(grad_block, one, two, three)
            spare = (spare + one) + (two + three)
    else:
        grad_block = input_piece(0, MICRO, packed_grad, None)
        near_grad, far_grad = share_plain(near_keep, near_send) / patches, share_plain(far_keep, far_send) / patches
        squares = jnp.sum(near_grad * near_grad) + jnp.sum(far_grad * far_grad)
        vec_grad, table_grad, squares = lax.psum((vec_grad, table_grad, squares), BOTH)
        table_grad = jnp.concatenate([table_grad, jnp.zeros((12, C - REL), F32)], axis=1)
        spare = jnp.concatenate([vec_grad / patches, table_grad / patches, jnp.broadcast_to(squares, (8, C))], axis=0)

    olds = (
        qkv_weight, proj_weight.T, fc1_weight, fc2_weight.T, vectors, rel_table.T,
        qkv_first, proj_first.T, fc1_first, fc2_first.T, vectors_first, table_first.T,
        qkv_second, proj_second.T, fc1_second, fc2_second.T, vectors_second, table_second.T,
    )
    shapes = [sds((1, 1), F32)] + [sds(olds[index].shape, F32) for index in range(6) for _ in range(3)]
    news = pl.pallas_call(
        adam_body,
        out_shape=shapes,
        compiler_params=whole(8),
        name="adam",
    )(near_grad, far_grad, spare, *olds)
    turned = [new.T if index // 3 in (1, 3, 5) else new for index, new in enumerate(news[1:])]
    return (block_out, grad_block, news[0][0, 0], *turned)


def solution(mesh):
    sizes = (mesh.shape["tok"], mesh.shape["head"])
    weights = (P(None, "tok", "head"), P("head", "tok"), P("tok", "head"), P("head", "tok"), P(), P())
    images = P(None, ("tok", "head"), None, None, None)
    return jax.shard_map(
        lambda *args: body(sizes, *args),
        mesh=mesh,
        in_specs=(images, images, P(None, "tok", None), P(None, "tok", None)) + weights * 3,
        out_specs=(images, images, P()) + tuple(spec for spec in weights for _ in range(3)),
        check_vma=False,
    )
```

```python
import functools
import math

import jax
import jax.numpy as jnp
import numpy as np
from jax import lax
from jax.experimental import pallas as pl
from jax.experimental.pallas import tpu as pltpu
from jax.sharding import PartitionSpec as P

C = 384
NH = 12
HD = 32
FF = 1536
WS = 7
SHIFT = 3
STEP = 10
GRID = 14
CELLS = WS * WS
REL = (2 * WS - 1) ** 2
MICRO = 5

WIN = 64
IMG = 4 * WIN
PAD = 16 * GRID
ROWS = MICRO * IMG
GROUP = 4
GROUPS = NH // GROUP
LANES = GROUP * HD
BLOCKS = 32
PIECE = 48
EARLY = 16
TALL, WIDE = 320, 256

EPS_NORM = 1e-05
BETA_ONE = 0.9
BETA_TWO = 0.999
ADAM_EPS = 1e-08
RATE_MATRIX = 0.08
RATE_VECTOR = 1.0
DECAY_MATRIX = 0.05
CLIP_NORM = 0.05
NEG_FILL = -1e30
HIGH = lax.Precision.HIGHEST
LOW = jnp.bfloat16
F32 = jnp.float32
NEVER = 99.0
BOTH = ("tok", "head")
MASKS = (16, 8, 2, 4, 1)
CORE, PLANE, LINE = 1, (2, 4, 6), (16, 8, 24)
PIECES = 8
ME, SLOT, IMAGE = 0, 1, 2


def swap_bits(position):
    return sum((position & mask) // mask << bit for bit, mask in enumerate(MASKS))


def block_at(place):
    return sum(((place >> bit) & 1) * mask for bit, mask in enumerate(MASKS))


def window_tables():
    cell = np.arange(WIN)
    real = cell < CELLS
    rolled_row = np.stack([WS * (w // 2) + cell // WS for w in range(4)])
    rolled_col = np.stack([WS * (w % 2) + cell % WS for w in range(4)])
    source_row = (rolled_row + SHIFT) % GRID
    source_col = (rolled_col + SHIFT) % GRID

    def band(position):
        return np.where(position < GRID - WS, 0, np.where(position < GRID - SHIFT, 1, 2))

    label_row = (rolled_row + SHIFT) % GRID
    label_col = (rolled_col + SHIFT) % GRID
    region = 3 * band(label_row) + band(label_col)
    label_row = (label_row + SHIFT) % GRID
    label_col = (label_col + SHIFT) % GRID
    deal = np.zeros((IMG, PAD), np.float32)
    for w in range(4):
        for c in range(CELLS):
            deal[w * WIN + c, 16 * source_row[w, c] + source_col[w, c]] = 1.0
    place = np.full((2, IMG, 128), NEVER, np.float32)
    place[0] = np.where(real[None], source_row, NEVER).reshape(IMG, 1)
    place[1] = np.where(real[None], source_col, NEVER).reshape(IMG, 1)
    reach = np.full((2, 2, WIN, 128), NEVER, np.float32)
    for pair in range(2):
        for side in range(2):
            w = 2 * pair + side
            same = (region[w][:, None] == region[w][None, :]) & real[:, None] & real[None, :]
            for kind, source in enumerate((label_row, label_col)):
                far = np.where(same, np.maximum(source[w][:, None], source[w][None, :]), NEVER)
                far = np.where(np.eye(WIN, dtype=bool) & real[:, None], -1.0, far)
                reach[pair, kind, :, side * WIN : (side + 1) * WIN] = far
    offset = (2 * WS - 1) * (cell // WS) + cell % WS
    shifts = [int(value) for value in offset[:CELLS]]
    wanted = np.where(real, offset + REL // 2, -1)
    lookup = (np.arange(256)[:, None] == np.concatenate([wanted, wanted])[None, :]).astype(np.float32)
    heads = (np.arange(LANES)[None, :] // HD == np.arange(GROUP)[:, None]).astype(np.float32)
    heads = np.repeat(np.concatenate([heads, heads], axis=1), WIN, axis=0)
    return deal, place, reach, lookup, heads, shifts


DEAL, PLACE, REACH, LOOKUP, HEADS, SHIFTS = window_tables()


def dot_nn(a, b):
    return lax.dot_general(a, b, (((1,), (0,)), ((), ())), preferred_element_type=F32)


def dot_nt(a, b):
    return lax.dot_general(a, b, (((1,), (1,)), ((), ())), preferred_element_type=F32)


def dot_tn(a, b):
    return lax.dot_general(a, b, (((0,), (0,)), ((), ())), preferred_element_type=F32)


def turned(a, eye):
    return dot_nt(eye, a).astype(LOW)


def identity():
    row = lax.broadcasted_iota(jnp.int32, (128, 128), 0)
    return jnp.where(row == lax.broadcasted_iota(jnp.int32, (128, 128), 1), 1.0, 0.0).astype(LOW)


def norm_parts(rows):
    average = jnp.mean(rows, axis=-1, keepdims=True)
    centered = rows - average
    inverse = lax.rsqrt(jnp.mean(centered * centered, axis=-1, keepdims=True) + EPS_NORM)
    return centered * inverse, inverse


def norm_back(gradient, normed, inverse, gain):
    scaled = gradient * gain
    return inverse * (
        scaled
        - jnp.mean(scaled, axis=-1, keepdims=True)
        - normed * jnp.mean(scaled * normed, axis=-1, keepdims=True)
    )


def gelu_parts(pre_act):
    below = 0.5 + 0.5 * lax.erf(pre_act * 2.0 ** (-0.5))
    return below, jnp.exp(-0.5 * pre_act * pre_act) * (2.0 * math.pi) ** (-0.5)


SCALARS = pl.BlockSpec(memory_space=pltpu.SMEM)
HELD = pl.BlockSpec(memory_space=pltpu.VMEM)


def call(body, outs, inputs, name, limit=16, scratch=(), flops=1e9, scalars=0, fetched=0, stored=0):
    inputs = list(inputs)
    remote = slice(scalars, scalars + fetched)
    inputs[remote] = [pltpu.with_memory_space_constraint(array, pltpu.HBM) for array in inputs[remote]]
    far = pl.BlockSpec(memory_space=pltpu.HBM)
    return pl.pallas_call(
        body,
        in_specs=[SCALARS] * scalars + [far] * fetched + [HELD] * (len(inputs) - scalars - fetched),
        out_specs=[far] * stored + [HELD] * (len(outs) - stored),
        out_shape=[
            pltpu.HBM(shape, dtype) if index < stored else jax.ShapeDtypeStruct(shape, dtype)
            for index, (shape, dtype) in enumerate(outs)
        ],
        scratch_shapes=list(scratch),
        compiler_params=whole(limit),
        cost_estimate=pl.CostEstimate(flops=int(flops), bytes_accessed=4000000, transcendentals=0),
        name=name,
    )(*inputs)


def image_rows(image):
    return pl.ds(pl.multiple_of(image * IMG, IMG), IMG)


def whole(limit):
    return pltpu.CompilerParams(vmem_limit_bytes=limit * 1024 * 1024)


def sds(shape, dtype):
    return jax.ShapeDtypeStruct(shape, dtype)


def streamed(*arrays):
    return [pltpu.with_memory_space_constraint(array, pltpu.HBM) for array in arrays]


def row_mask(place_ref, table_ref, extent_ref, route_ref, image):
    parts = []
    own = table_ref[IMAGE]
    for w in range(4):
        rows = slice(w * WIN, (w + 1) * WIN)
        high = jnp.where(route_ref[own, w, image] >= 0, extent_ref[own, 0, image], -1).astype(F32)
        wide = extent_ref[own, 1, image].astype(F32)
        inside = (place_ref[0, rows] < high) & (place_ref[1, rows] < wide)
        parts.append(jnp.where(inside, 1.0, 0.0))
    return jnp.concatenate(parts, axis=0)


def pack_body(qkv_ref, proj_ref, fc1_ref, fc2_ref, near_ref, far_ref):
    depth = fc1_ref.shape[0]
    early = near_ref.shape[0] - depth
    near_ref[:depth] = jnp.concatenate([qkv_ref[0], qkv_ref[1], qkv_ref[2], proj_ref[...]], axis=1).astype(LOW)
    near_ref[depth:] = fc1_ref[:early].astype(LOW)
    far_ref[: depth - early] = fc1_ref[early:].astype(LOW)
    far_ref[depth - early :] = fc2_ref[...].astype(LOW)


def first_sum_body(keep_ref, got_ref, stays_ref, *goes_refs):
    stays_ref[...] = keep_ref[:4].astype(F32) + got_ref[:4].astype(F32)
    for index, goes in enumerate(goes_refs):
        at = 4 * (index + 1)
        goes[...] = (keep_ref[at : at + 4].astype(F32) + got_ref[at : at + 4].astype(F32)).astype(LOW)


def plane_sum_body(stays_ref, *refs):
    got, (rest, *goes) = refs[:3], refs[3:]
    for at in range(4):
        total = stays_ref[at : at + 1] + got[0][at : at + 1].astype(F32)
        total = total + (got[1][at : at + 1].astype(F32) + got[2][at : at + 1].astype(F32))
        if at == 0:
            rest[...] = total
        else:
            goes[at - 1][...] = total.astype(LOW)


def finish_body(patches, near_ref, far_ref, vec_ref, table_ref, *refs):
    near_got, far_got, (near_grad, far_grad, spare) = refs[:3], refs[3:6], refs[6:]
    squares = jnp.zeros((1, 1), F32)
    for stays, got, target in ((near_ref, near_got, near_grad), (far_ref, far_got, far_grad)):
        total = stays[0] + got[0][0].astype(F32) + (got[1][0].astype(F32) + got[2][0].astype(F32))
        total = total * (1.0 / patches)
        target[...] = total
        squares = squares + jnp.sum(jnp.sum(total * total, axis=1, keepdims=True), axis=0, keepdims=True)
    spare[0:12] = vec_ref[...] * (1.0 / patches)
    spare[12:24] = jnp.broadcast_to(squares, (12, C))
    spare[12:18, :REL] = table_ref[: NH // 2] * (1.0 / patches)
    spare[12:18, C // 2 : C // 2 + REL] = table_ref[NH // 2 :] * (1.0 / patches)


def three_parts(values):
    first = values.astype(LOW).astype(F32)
    second = (values - first).astype(LOW).astype(F32)
    return jnp.concatenate([first, second, values - first - second], axis=0)


def fetch(pairs, sems):
    copies = [pltpu.make_async_copy(source, target, sems.at[index]) for index, (source, target) in enumerate(pairs)]
    for copy in copies:
        copy.start()
    return copies


def deal_rows(source, deal, pad, image):
    for r in range(GRID):
        pad[image, 16 * r : 16 * r + GRID, :] = source[image, 0, r]
    return dot_nn(deal[...], pad[image])


def prep_body(
    table_hbm, lookup_hbm, vec_hbm, deal_hbm, tok_hbm, x_hbm, unit_hbm, n_ref, bias_ref,
    table, lookup, vec, deal, tok, x_all, unit_all, padded, pad, sems, out_sems
):
    copies = fetch(
        ((table_hbm, table), (lookup_hbm, lookup), (vec_hbm, vec), (deal_hbm, deal), (tok_hbm, tok)), sems
    )
    padded[...] = jnp.zeros_like(padded)
    pad[...] = jnp.zeros_like(pad)
    bias_ref[...] = jnp.zeros_like(bias_ref)
    copies[0].wait()
    padded[:NH, :REL] = table[...]
    parts = three_parts(padded[...])
    moved = [pltpu.roll(parts, shift, 1) if shift else parts for shift in SHIFTS]
    copies[1].wait()
    spread = dot_nn(jnp.concatenate(moved, axis=0).astype(LOW), lookup[...])
    for k in range(CELLS):
        rows = spread[48 * k : 48 * k + 48]
        bias_ref[pl.ds(k, NH, stride=WIN), :] = (rows[:16] + (rows[16:32] + rows[32:]))[:NH]
    for copy in copies[2:]:
        copy.wait()
    stores, made = [], []
    for image in range(MICRO):
        at = slice(image * IMG, (image + 1) * IMG)
        made.append(deal_rows(tok, deal, pad, image))
        x_all[at, :] = made[-1].astype(LOW)
        stores.append(pltpu.make_async_copy(x_all.at[at], x_hbm.at[at], out_sems.at[image, 0]))
        stores[-1].start()
    for image in range(MICRO):
        at = slice(image * IMG, (image + 1) * IMG)
        unit, _ = norm_parts(made[image])
        unit_all[:, at] = unit.astype(LOW).T
        stores.append(pltpu.make_async_copy(unit_all.at[:, at], unit_hbm.at[:, at], out_sems.at[image, 1]))
        stores[-1].start()
        n_ref[at, :] = (unit * vec[0:1] + vec[1:2]).astype(LOW)
    for store in stores:
        store.wait()


def prep_grad_body(deal_hbm, cot_hbm, g_ref, turned_ref, deal, cot, pad, sems):
    copies = fetch(((deal_hbm, deal), (cot_hbm, cot)), sems)
    pad[...] = jnp.zeros_like(pad)
    for copy in copies:
        copy.wait()
    for image in range(MICRO):
        at = slice(image * IMG, (image + 1) * IMG)
        rows = deal_rows(cot, deal, pad, image).astype(LOW)
        g_ref[at, :] = rows
        turned_ref[:, at] = rows.T


def table_body(sums_ref, lookup_ref, table_ref, padded):
    padded[...] = jnp.zeros_like(padded)
    slabs = []
    for k in range(CELLS):
        padded[:NH, :] = sums_ref[pl.ds(k, NH, stride=WIN), :]
        slabs.append(three_parts(padded[...]))
    made = dot_nt(jnp.concatenate(slabs, axis=0).astype(LOW), lookup_ref[...])
    total = jnp.zeros((16, 256), F32)
    for k, shift in enumerate(SHIFTS):
        rows = made[48 * k : 48 * k + 48]
        rows = rows[:16] + (rows[16:32] + rows[32:])
        total = total + (pltpu.roll(rows, 256 - shift, 1) if shift else rows)
    table_ref[...] = total[:NH, :REL]


def put_back(rows, back_ref, target, image):
    grid = dot_nn(back_ref[...], rows.astype(LOW)).astype(LOW)
    for r in range(GRID):
        target[image, 0, r] = grid[16 * r : 16 * r + GRID]


def spread_keys(part, heads_ref):
    wide = jnp.concatenate([part[:WIN], part[WIN:]], axis=1)
    return jnp.concatenate([wide] * GROUP, axis=0) * heads_ref[...]


def spread_rows(part):
    zero = jnp.zeros((WIN, LANES), part.dtype)
    top = jnp.concatenate([part[:WIN], zero], axis=1)
    return jnp.concatenate([top, jnp.concatenate([zero, part[WIN:]], axis=1)], axis=0)


def own_rows(product):
    return jnp.concatenate([product[:WIN, :LANES], product[WIN:, LANES:]], axis=0)


def own_keys(product, heads_ref):
    kept = product * heads_ref[...].astype(F32)
    total = kept[:WIN]
    for h in range(1, GROUP):
        total = total + kept[h * WIN : (h + 1) * WIN]
    return jnp.concatenate([total[:, :LANES], total[:, LANES:]], axis=0)


def attend_body(
    direct, table_ref, extent_ref, route_ref, n_ref, vec_ref, bias_ref, reach_ref, place_ref, heads_ref, *refs,
):
    near_refs, (packed_ref, soft_ref, attn_ref, wq_ref, wp_ref, parts) = refs[:PIECES], refs[PIECES:]
    for j in range(BLOCKS):
        at = table_ref[ME] ^ block_at(j) if direct else (j % 8) * 4 + j // 8
        row = at // 4 * PIECE if not direct else pl.multiple_of((at >> 2) * PIECE, PIECE)
        parts[at & 3, pl.ds(row, PIECE), :] = near_refs[j // 4][j % 4, :PIECE]
    for w in range(3):
        wq_ref[:, w * C : (w + 1) * C] = jnp.concatenate([parts[h, :, w * 96 : (w + 1) * 96] for h in range(4)], axis=1)
    wp_ref[...] = jnp.concatenate([parts[h, :, 288:] for h in range(4)], axis=1)

    @pl.loop(0, MICRO)
    def _(image):
        at_image = image_rows(image)
        made = dot_nn(n_ref[at_image, :], wq_ref[...])
        packed_ref[at_image, :C] = (made[:, :C] + vec_ref[2:3]).astype(LOW)
        packed_ref[at_image, C : 2 * C] = made[:, C : 2 * C].astype(LOW)
        packed_ref[at_image, 2 * C :] = (made[:, 2 * C :] + vec_ref[3:4]).astype(LOW)
        mask = row_mask(place_ref, table_ref, extent_ref, route_ref, image)
        high = extent_ref[table_ref[IMAGE], 0, image].astype(F32)
        wide = extent_ref[table_ref[IMAGE], 1, image].astype(F32)
        eye = identity()
        units = [(pair, g) for pair in range(2) for g in range(GROUPS)]
        at_pair = [pl.ds(pl.multiple_of(image * IMG + pair * 2 * WIN, 2 * WIN), 2 * WIN) for pair in range(2)]
        raws = []
        for pair, g in units:
            at = g * LANES
            queries = packed_ref[at_pair[pair], at : at + LANES]
            keys = packed_ref[at_pair[pair], C + at : C + at + LANES]
            raws.append(dot_nt(spread_keys(keys, heads_ref), spread_rows(queries)))
        softs = []
        for (pair, g), raw in zip(units, raws):
            allowed = (reach_ref[pair, 0] < high) & (reach_ref[pair, 1] < wide)
            raw = (raw * HD ** (-0.5) + bias_ref[g]).reshape(GROUP, WIN, 128)
            scores = jnp.where(allowed[None], raw, NEG_FILL)
            exponent = jnp.exp(scores - jnp.max(scores, axis=1, keepdims=True))
            soft = exponent * (1.0 / jnp.sum(exponent, axis=1, keepdims=True))
            soft = soft.reshape(GROUP * WIN, 128).astype(LOW)
            soft_ref[image, pair * GROUPS + g] = soft
            softs.append(soft)
        softs = [turned(soft, eye) for soft in softs]
        for (pair, g), soft in zip(units, softs):
            at = g * LANES
            values = packed_ref[at_pair[pair], 2 * C + at : 2 * C + at + LANES]
            result = own_rows(dot_nn(soft, spread_keys(values, heads_ref)))
            rows = slice(pair * 2 * WIN, (pair + 1) * 2 * WIN)
            attn_ref[at_pair[pair], at : at + LANES] = (result * mask[rows]).astype(LOW)


def middle_body(attn_ref, x_ref, wp_ref, vec_ref, middle_ref, n_ref, turned_ref):
    for image in range(MICRO):
        at = slice(image * IMG, (image + 1) * IMG)
        middle = x_ref[at, :].astype(F32) + dot_nt(attn_ref[at, :], wp_ref[...]) + vec_ref[4:5]
        middle_ref[at, :] = middle
        unit, _ = norm_parts(middle)
        normed = (unit * vec_ref[5:6] + vec_ref[6:7]).astype(LOW)
        n_ref[at, :] = normed
        turned_ref[:, at] = normed.T


def mlp_body(
    direct, table_ref, middle_ref, n_ref, g_ref, vec_ref, *refs,
):
    near_refs, far_refs, refs = refs[:PIECES], refs[PIECES : 2 * PIECES], refs[2 * PIECES :]
    (hidden_ref, grad_hidden_ref, grad_ref, sums_ref, w2_ref, w1, bias, bias_sum) = refs
    for j in range(BLOCKS):
        at = table_ref[ME] ^ block_at(j) if direct else (j % 8) * 4 + j // 8
        row = at // 4 * PIECE if not direct else pl.multiple_of((at >> 2) * PIECE, PIECE)
        col = at % 4 * C if not direct else pl.multiple_of((at & 3) * C, C)
        w1[pl.ds(row, EARLY), pl.ds(col, C)] = near_refs[j // 4][j % 4, PIECE:]
        w1[pl.ds(row + EARLY, PIECE - EARLY), pl.ds(col, C)] = far_refs[j // 4][j % 4, : PIECE - EARLY]
        w2_ref[pl.ds(row, PIECE), pl.ds(col, C)] = far_refs[j // 4][j % 4, PIECE - EARLY :]
    for r in range(4):
        bias[:, r * C : (r + 1) * C] = vec_ref[8 + r : 9 + r]
    sums_ref[...] = jnp.zeros_like(sums_ref)

    bias_sum[...] = jnp.zeros_like(bias_sum)
    for part in range(FF // WIDE):
        cols = slice(part * WIDE, (part + 1) * WIDE)
        for block in range(ROWS // TALL):
            at = slice(block * TALL, (block + 1) * TALL)
            pre_act = dot_nn(n_ref[at, :], w1[:, cols]) + bias[:, cols]
            grad_post = dot_nn(g_ref[at, :], w2_ref[:, cols])
            below, density = gelu_parts(pre_act)
            hidden_ref[at, cols] = (pre_act * below).astype(LOW)
            grad_pre = grad_post * (below + pre_act * density)
            grad_hidden_ref[at, cols] = grad_pre.astype(LOW)
            bias_sum[:, cols] += jnp.sum(grad_pre, axis=0, keepdims=True)
    for block in range(ROWS // TALL):
        at = slice(block * TALL, (block + 1) * TALL)
        back = dot_nt(grad_hidden_ref[at, :], w1[...])
        unit, inverse = norm_parts(middle_ref[at, :])
        g = g_ref[at, :].astype(F32)
        grad_middle = g + norm_back(back, unit, inverse, vec_ref[5:6])
        grad_ref[at, :] = grad_middle
        sums_ref[4:5] += jnp.sum(grad_middle, axis=0, keepdims=True)
        sums_ref[5:6] += jnp.sum(back * unit, axis=0, keepdims=True)
        sums_ref[6:7] += jnp.sum(back, axis=0, keepdims=True)
        sums_ref[7:8] += jnp.sum(g, axis=0, keepdims=True)
    for r in range(4):
        sums_ref[8 + r : 9 + r] = bias_sum[:, r * C : (r + 1) * C]


def place_of(direct, table_ref, t, h):
    if not direct:
        return h * 8 + t
    return table_ref[SLOT] ^ swap_bits(4 * t) ^ ((h & 1) * 16 + (h >> 1) * 4)


def mlp_weights_body(direct, table_ref, n_turned, g_turned, hidden_ref, grad_hidden_ref, keep_ref, send_ref, made, first, second):
    for part in range(3):
        cols = slice(part * 2 * WIDE, (part + 1) * 2 * WIDE)
        first[:, cols] = dot_nn(n_turned[...], grad_hidden_ref[:, cols]).astype(LOW)
        second[:, cols] = dot_nn(g_turned[...], hidden_ref[:, cols]).astype(LOW)
    for h in range(4):
        cols = slice(h * C, (h + 1) * C)
        for t in range(8):
            at = place_of(direct, table_ref, t, h)
            made[at, :PIECE] = first[t * PIECE : (t + 1) * PIECE, cols]
            made[at, PIECE:] = second[t * PIECE : (t + 1) * PIECE, cols]
    keep_ref[...] = made[: BLOCKS // 2]
    send_ref[...] = made[BLOCKS // 2 :]


def output_body(first, last, hidden_ref, w2_ref, middle_ref, vec_ref, back_ref, *refs):
    out_hbm, made, sems = refs[(first > 0) :]
    rows = []
    for image in range(first, last):
        at = slice(image * IMG, (image + 1) * IMG)
        rows.append((middle_ref[at, :] + dot_nt(hidden_ref[at, :], w2_ref[...]) + vec_ref[7:8]).astype(LOW))
    stores = []
    for index, low in enumerate(rows):
        put_back(low, back_ref, made, index)
        stores.append(pltpu.make_async_copy(made.at[index], out_hbm.at[first + index], sems.at[index]))
        stores[-1].start()
    for store in stores:
        store.wait()


def attend_back_body(
    table_ref, extent_ref, route_ref, grad_ref, packed_ref, soft_ref, wp_ref, place_ref, heads_ref,
    packed_grad_ref, grad_low_ref, bias_sum_ref, sums_ref,
):
    bias_sum_ref[...] = jnp.zeros_like(bias_sum_ref)
    sums_ref[...] = jnp.zeros_like(sums_ref)

    @pl.loop(0, MICRO)
    def _(image):
        at_image = image_rows(image)
        grad_low = grad_ref[at_image, :].astype(LOW)
        grad_low_ref[at_image, :] = grad_low
        mask = row_mask(place_ref, table_ref, extent_ref, route_ref, image)
        grad_attn = dot_nn(grad_low, wp_ref[...])
        grad_attn = (grad_attn * jnp.concatenate([mask] * 3, axis=1)).astype(LOW)
        eye = identity()
        units = [(pair, g) for pair in range(2) for g in range(GROUPS)]
        at_pair = [pl.ds(pl.multiple_of(image * IMG + pair * 2 * WIN, 2 * WIN), 2 * WIN) for pair in range(2)]
        incomings, grad_softs = [], []
        for pair, g in units:
            at = g * LANES
            values = packed_ref[at_pair[pair], 2 * C + at : 2 * C + at + LANES]
            incomings.append(spread_rows(grad_attn[pair * 2 * WIN : (pair + 1) * 2 * WIN, at : at + LANES]))
            grad_softs.append(dot_nt(spread_keys(values, heads_ref), incomings[-1]))
        grads = []
        for (pair, g), grad_soft in zip(units, grad_softs):
            soft = soft_ref[image, pair * GROUPS + g].astype(F32)
            joint = (soft * grad_soft).reshape(GROUP, WIN, 128)
            inner = jnp.sum(joint, axis=1, keepdims=True)
            grad_scores = (joint - soft.reshape(GROUP, WIN, 128) * inner).reshape(GROUP * WIN, 128)
            grads.append(grad_scores.astype(LOW))
            bias_sum_ref[g] += grads[-1].astype(F32)
        values_made = [dot_nn(soft_ref[image, pair * GROUPS + g], incoming) for (pair, g), incoming in zip(units, incomings)]
        turns = [turned(grad, eye) for grad in grads]
        keys_made, queries_made = [], []
        for (pair, g), grad, turn in zip(units, grads, turns):
            at = g * LANES
            queries = packed_ref[at_pair[pair], at : at + LANES]
            keys = packed_ref[at_pair[pair], C + at : C + at + LANES]
            keys_made.append(dot_nn(grad, spread_rows(queries)))
            queries_made.append(dot_nn(turn, spread_keys(keys, heads_ref)))
        for (pair, g), grad_values, grad_keys, grad_queries in zip(units, values_made, keys_made, queries_made):
            at = g * LANES
            rows = at_pair[pair]
            packed_grad_ref[rows, at : at + LANES] = (own_rows(grad_queries) * HD ** (-0.5)).astype(LOW)
            packed_grad_ref[rows, C + at : C + at + LANES] = (own_keys(grad_keys, heads_ref) * HD ** (-0.5)).astype(LOW)
            packed_grad_ref[rows, 2 * C + at : 2 * C + at + LANES] = own_keys(grad_values, heads_ref).astype(LOW)
        sums_ref[...] += jnp.sum(packed_grad_ref[at_image, :].astype(F32), axis=0, keepdims=True)


def attend_weights_body(
    direct, table_ref, unit_turned, grad_low_ref, packed_grad_ref, attn_ref, wq_ref, sums_ref, vec_ref, keep_ref, send_ref, norm_ref, made
):
    turned_vec = vec_ref[...].T
    gain, shift = turned_vec[:, 0:1], turned_vec[:, 1:2]
    parts = []
    gain_grad = jnp.zeros((C, 1), F32)
    shift_grad = jnp.zeros((C, 1), F32)
    for w in range(3):
        cols = slice(w * C, (w + 1) * C)
        product = dot_nn(unit_turned[...], packed_grad_ref[:, cols])
        weight, sums = wq_ref[:, cols].astype(F32), sums_ref[:, cols]
        parts.append((product * gain + shift * sums).astype(LOW))
        gain_grad = gain_grad + jnp.sum(product * weight, axis=1, keepdims=True)
        shift_grad = shift_grad + jnp.sum(weight * sums, axis=1, keepdims=True)
    norm_ref[0:1] = jnp.broadcast_to(gain_grad, (C, 128)).T[0:1]
    norm_ref[1:2] = jnp.broadcast_to(shift_grad, (C, 128)).T[0:1]
    parts.append(dot_nn(grad_low_ref[...].T, attn_ref[...]).astype(LOW))
    for h in range(4):
        block = jnp.concatenate([part[:, h * 96 : (h + 1) * 96] for part in parts], axis=1)
        for t in range(8):
            made[place_of(direct, table_ref, t, h)] = block[t * PIECE : (t + 1) * PIECE]
    keep_ref[...] = made[: BLOCKS // 2]
    send_ref[...] = made[BLOCKS // 2 :]


def input_body(first, last, *refs):
    wq_hbm, packed_grad_hbm, x_hbm, grad_hbm = refs[:4]
    refs = refs[4 + (first > 0) :]
    vec_ref, back_ref, out_hbm, wq, packed_grad, x_all, grad_all, made, wq_sem, sems, out_sems = refs
    images = range(last - first)
    whole_copy = pltpu.make_async_copy(wq_hbm, wq, wq_sem)
    whole_copy.start()
    copies = []
    for image in images:
        source_at = slice((first + image) * IMG, (first + image + 1) * IMG)
        at = slice(image * IMG, (image + 1) * IMG)
        for index, (source, target) in enumerate(((packed_grad_hbm, packed_grad), (x_hbm, x_all), (grad_hbm, grad_all))):
            copies.append(pltpu.make_async_copy(source.at[source_at], target.at[at], sems.at[image, index]))
            copies[-1].start()
    whole_copy.wait()
    stores = []
    for image in images:
        at = slice(image * IMG, (image + 1) * IMG)
        for copy in copies[3 * image : 3 * image + 3]:
            copy.wait()
        back = dot_nt(packed_grad[at, :], wq[...])
        unit, inverse = norm_parts(x_all[at, :].astype(F32))
        rows = grad_all[at, :] + norm_back(back, unit, inverse, vec_ref[0:1])
        put_back(rows, back_ref, made, image)
        stores.append(pltpu.make_async_copy(made.at[image], out_hbm.at[first + image], out_sems.at[image]))
        stores[-1].start()
    for store in stores:
        store.wait()


def adam_update(weight, first, second, gradient, rate, decay):
    first_new = BETA_ONE * first + (1.0 - BETA_ONE) * gradient
    second_new = BETA_TWO * second + (1.0 - BETA_TWO) * gradient * gradient
    first_hat = first_new / (1.0 - BETA_ONE**STEP)
    second_hat = second_new / (1.0 - BETA_TWO**STEP)
    weight_new = weight * (1.0 - rate * decay) - rate * first_hat / (jnp.sqrt(second_hat) + ADAM_EPS)
    return (weight_new, first_new, second_new)


def adam_body(near_ref, far_ref, spare_ref, *refs):
    olds, news, turned = refs[:18], refs[18:-1], refs[-1]
    turned[: NH // 2] = spare_ref[12:18, :REL]
    turned[NH // 2 :] = spare_ref[12:18, C // 2 : C // 2 + REL]
    vec, table = spare_ref[0:12], turned[...]
    total = spare_ref[18:19, 0:1]
    total = total + jnp.sum(jnp.sum(vec * vec, axis=1, keepdims=True), axis=0, keepdims=True)
    total = total + jnp.sum(jnp.sum(table * table, axis=1, keepdims=True), axis=0, keepdims=True)
    grad_norm = jnp.sqrt(total)
    factor = jnp.minimum(1.0, CLIP_NORM / (grad_norm + 1e-06))
    news[0][...] = grad_norm
    depth = far_ref.shape[0] // 2
    grads = [None, near_ref[:, 288:], far_ref[:depth], far_ref[depth:], vec, table]
    for index in range(6):
        weight, first, second = olds[index], olds[6 + index], olds[12 + index]
        rate, decay = (RATE_MATRIX, DECAY_MATRIX) if index < 4 else (RATE_VECTOR, 0.0)
        for w in range(3 if index == 0 else 1):
            pick = (w,) if index == 0 else (Ellipsis,)
            gradient = near_ref[:, w * 96 : (w + 1) * 96] if index == 0 else grads[index]
            made = adam_update(weight[pick], first[pick], second[pick], gradient * factor, rate, decay)
            for kind in range(3):
                news[1 + 3 * index + kind][pick] = made[kind]


def body(
    mesh_sizes, tokens_in, cotangent, route, extent, qkv_weight, proj_weight, fc1_weight, fc2_weight, vectors, rel_table,
    qkv_first, proj_first, fc1_first, fc2_first, vectors_first, table_first,
    qkv_second, proj_second, fc1_second, fc2_second, vectors_second, table_second,
):
    toks, heads = mesh_sizes
    devices = toks * heads
    direct = toks == 8 and heads == 4
    micro = tokens_in.shape[0]
    patches = micro * devices * GRID * GRID
    head_at = lax.axis_index("head")
    me = lax.axis_index("tok") * heads + head_at
    numbers = [me, swap_bits(me), head_at]
    extents, routes = extent.transpose(1, 2, 0), route.transpose(1, 2, 0)

    def tie(*arrays):
        return lax.optimization_barrier(arrays)

    def passed(rows, mask):
        return lax.ppermute(rows, BOTH, [(i, i ^ mask) for i in range(devices)])

    depth = fc1_weight.shape[0]
    early = depth * EARLY // PIECE
    near, far = pl.pallas_call(
        pack_body, out_shape=(sds((depth + early, C), LOW), sds((2 * depth - early, C), LOW)), compiler_params=whole(8), name="pack"
    )(*streamed(qkv_weight, proj_weight.T, fc1_weight, fc2_weight.T))

    def gather_plain(piece):
        spread = lax.all_gather(lax.all_gather(piece, "tok", axis=0), "head", axis=0)
        return spread.reshape(BLOCKS, PIECE, C)

    def plain_pieces(near, far):
        one = gather_plain(near[:depth])
        two = gather_plain(jnp.concatenate([near[depth:], far[: depth - early]], axis=0))
        three = gather_plain(far[depth - early :])
        near = jnp.concatenate([one, two[:, :EARLY]], axis=1)
        far = jnp.concatenate([two[:, EARLY:], three], axis=1)
        return [[array[at : at + 4] for at in range(0, BLOCKS, 4)] for array in (near, far)]

    def share_plain(keep, send):
        both = jnp.concatenate([keep, send], axis=0)
        half = both.shape[1] // PIECE
        both = both.reshape(heads, 8, half, PIECE, C).transpose(0, 2, 1, 3, 4)
        both = both.reshape(heads, half, toks, depth, C).transpose(0, 2, 1, 3, 4).reshape(devices, half * depth, C)
        both = lax.psum_scatter(both.astype(F32), "head", scatter_dimension=0, tiled=True)
        return lax.psum_scatter(both, "tok", scatter_dimension=0, tiled=True)[0]

    def join(*arrays):
        return jnp.concatenate(arrays, axis=0)

    def first_sum(keep, got):
        shape = (4,) + keep.shape[1:]
        stays, *goes = pl.pallas_call(
            first_sum_body, out_shape=[sds(shape, F32)] + [sds(shape, LOW)] * 3, compiler_params=whole(2), name="first_sum"
        )(keep, got)
        return stays, goes

    def plane_sum(stays, got):
        shape = (1,) + stays.shape[1:]
        rest, *goes = pl.pallas_call(
            plane_sum_body, out_shape=[sds(shape, F32)] + [sds(shape, LOW)] * 3, compiler_params=whole(2), name="plane_sum"
        )(stays, *got)
        return rest, goes

    def spread(rows, masks):
        return [passed(rows, mask) for mask in masks]

    def sent(parts, masks):
        return [passed(part, mask) for part, mask in zip(parts, masks)]

    back = jnp.asarray(DEAL.T, LOW)
    deal = jnp.asarray(DEAL, LOW)
    lookup = jnp.asarray(LOOKUP, LOW)
    place = jnp.asarray(PLACE)
    reach = jnp.asarray(REACH)
    heads_low = jnp.asarray(HEADS, LOW)
    whole_images = pltpu.VMEM((MICRO, 1, GRID, GRID, C), LOW)

    def prepare(tokens, values):
        x_rows, unit_turned, n_rows, bias = call(
            prep_body,
            [((ROWS, C), LOW), ((C, ROWS), LOW), ((ROWS, C), LOW), ((NH * WIN, 128), F32)],
            (values.T, lookup, vectors, deal, tokens),
            "prep",
            scratch=[
                pltpu.VMEM((NH, REL), F32), pltpu.VMEM((256, 128), LOW), pltpu.VMEM((12, C), F32), pltpu.VMEM((IMG, PAD), LOW),
                whole_images, pltpu.VMEM((ROWS, C), LOW), pltpu.VMEM((C, ROWS), LOW), pltpu.VMEM((16, 256), F32),
                pltpu.VMEM((MICRO, PAD, C), LOW), pltpu.SemaphoreType.DMA((5,)), pltpu.SemaphoreType.DMA((MICRO, 2)),
            ],
            flops=1e9,
            fetched=5,
            stored=2,
        )
        return x_rows, unit_turned, n_rows, bias.reshape(GROUPS, GROUP * WIN, 128)

    def prepare_grad(cotangents):
        return call(
            prep_grad_body,
            [((ROWS, C), LOW), ((C, ROWS), LOW)],
            (deal, cotangents),
            "prep_grad",
            limit=8,
            scratch=[pltpu.VMEM((IMG, PAD), LOW), whole_images, pltpu.VMEM((MICRO, PAD, C), LOW), pltpu.SemaphoreType.DMA((2,))],
            fetched=2,
        )

    if direct:
        near = near[None]
        near_got, far_got = spread(near, LINE), spread(far[None], LINE)
        near_all = join(near, *near_got)
        near_all = [near_all] + spread(near_all, PLANE)
        far_all = join(far[None], *far_got)
        far_all, tokens, rel_bias, *numbers = tie(far_all, tokens_in, rel_table, *numbers)
        table = jnp.stack(numbers).astype(jnp.int32)
        x_rows, unit_turned, n_rows, bias = prepare(tokens, rel_bias)
        bias, table, n_rows, *near_all = tie(bias, table, n_rows, *near_all)
        far_all, near_all[0] = tie(far_all, near_all[0])
        near_all = near_all + [passed(piece, CORE) for piece in near_all]
        far_got = [far_all] + spread(far_all, PLANE)
    else:
        table = jnp.stack(numbers).astype(jnp.int32)
        x_rows, unit_turned, n_rows, bias = prepare(tokens_in, rel_table)
        near_all, far_all = plain_pieces(near, far)

    packed, soft, attn, w_qkv, w_proj = call(
        functools.partial(attend_body, direct),
        [
            ((ROWS, 3 * C), LOW), ((MICRO, 2 * GROUPS, GROUP * WIN, 128), LOW), ((ROWS, C), LOW), ((C, 3 * C), LOW), ((C, C), LOW),
        ],
        (table, extents, routes, n_rows, vectors, bias, reach, place, heads_low, *near_all),
        "attend",
        limit=8,
        scratch=[pltpu.VMEM((4, C, C), LOW)],
        flops=8e9,
        scalars=3,
    )

    middle, n_two, n_turned = call(
        middle_body, [((ROWS, C), F32), ((ROWS, C), LOW), ((C, ROWS), LOW)], (attn, x_rows, w_proj, vectors), "middle", limit=4
    )

    late = cotangent
    if direct:
        middle, late, *far_got = tie(middle, late, *far_got)
        far_core = [passed(piece, CORE) for piece in far_got]
    g_rows, g_turned = prepare_grad(late)
    if direct:
        g_rows, *far_core = tie(g_rows, *far_core)
        far_all = far_got + far_core

    hidden, grad_hidden, grad_middle, sums_mlp, w_fc2 = call(
        functools.partial(mlp_body, direct),
        [((ROWS, FF), LOW), ((ROWS, FF), LOW), ((ROWS, C), F32), ((12, C), F32), ((C, FF), LOW)],
        (table, middle, n_two, g_rows, vectors, *near_all, *far_all),
        "mlp",
        limit=8,
        scratch=[pltpu.VMEM((C, FF), LOW), pltpu.VMEM((1, FF), F32), pltpu.VMEM((1, FF), F32)],
        flops=10e9,
        scalars=1,
    )

    half = BLOCKS // 2
    far_keep, far_send = call(
        functools.partial(mlp_weights_body, direct),
        [((half, 2 * PIECE, C), LOW)] * 2,
        (table, n_turned, g_turned, hidden, grad_hidden),
        "mlp_weights",
        limit=14,
        scratch=[
            pltpu.VMEM((BLOCKS, 2 * PIECE, C), LOW), pltpu.VMEM((C, FF), LOW), pltpu.VMEM((C, FF), LOW),
        ],
        flops=4e9,
        scalars=1,
    )

    if direct:
        far_got = passed(far_send, CORE)

    def output_piece(first, last, hidden, block_out):
        far = pl.BlockSpec(memory_space=pltpu.HBM)
        before = [] if block_out is None else [pltpu.with_memory_space_constraint(block_out, pltpu.HBM)]
        return pl.pallas_call(
            functools.partial(output_body, first, last),
            in_specs=[HELD] * 5 + [far] * len(before),
            out_specs=far,
            out_shape=pltpu.HBM(tokens_in.shape, LOW),
            input_output_aliases={} if block_out is None else {5: 0},
            scratch_shapes=[pltpu.VMEM((last - first, 1, GRID, GRID, C), LOW), pltpu.SemaphoreType.DMA((last - first,))],
            compiler_params=whole(8),
            cost_estimate=pl.CostEstimate(flops=int(4e8 * (last - first)), bytes_accessed=2000000, transcendentals=0),
            name="output",
        )(hidden, w_fc2, middle, vectors, back, *before)

    early_images = 3 if direct else MICRO
    block_out = output_piece(0, early_images, hidden, None)

    if direct:
        block_out, far_got, grad_middle, hidden = tie(block_out, far_got, grad_middle, hidden)
        far_stays, far_goes = first_sum(far_keep, far_got)
        far_got = sent(far_goes, PLANE)

    packed_grad, grad_low, bias_sum, sums_attend = call(
        attend_back_body,
        [((ROWS, 3 * C), LOW), ((ROWS, C), LOW), ((GROUPS, GROUP * WIN, 128), F32), ((1, 3 * C), F32)],
        (table, extents, routes, grad_middle, packed, soft, w_proj, place, heads_low),
        "attend_back",
        limit=6,
        flops=8e9,
        scalars=3,
    )

    vec_square = jnp.concatenate([vectors, jnp.zeros((4, C), F32)], axis=0)
    near_keep, near_send, sums_input = call(
        functools.partial(attend_weights_body, direct),
        [((half, PIECE, C), LOW)] * 2 + [((2, C), F32)],
        (table, unit_turned, grad_low, packed_grad, attn, w_qkv, sums_attend, vec_square),
        "attend_weights",
        limit=8,
        scratch=[pltpu.VMEM((BLOCKS, PIECE, C), LOW)],
        flops=2e9,
        scalars=1,
    )

    if direct:
        near_send, *far_got = tie(near_send, *far_got)
        near_send, hidden = tie(near_send, hidden)
        near_got = passed(near_send, CORE)
        block_out = output_piece(early_images, MICRO, hidden, block_out)
        near_got, block_out = tie(near_got, block_out)
        near_stays, near_goes = first_sum(near_keep, near_got)
        near_goes[0], bias_sum = tie(near_goes[0], bias_sum)
        near_got = sent(near_goes, PLANE)

    (table_grad,) = call(
        table_body,
        [((NH, REL), F32)],
        (bias_sum.reshape(NH * WIN, 128), lookup),
        "table_grad",
        limit=8,
        scratch=[pltpu.VMEM((16, 128), F32)],
        flops=1e8,
    )
    if direct:
        table_grad, *far_got = tie(table_grad, *far_got)
        far_stays, far_goes = plane_sum(far_stays, far_got)
        far_got = sent(far_goes, LINE)

    def input_piece(first, last, packed_grad, grad_block):
        count = last - first
        sources = [pltpu.with_memory_space_constraint(array, pltpu.HBM) for array in (w_qkv, packed_grad, x_rows, grad_middle)]
        sources += [] if grad_block is None else [pltpu.with_memory_space_constraint(grad_block, pltpu.HBM)]
        far = pl.BlockSpec(memory_space=pltpu.HBM)
        return pl.pallas_call(
            functools.partial(input_body, first, last),
            in_specs=[far] * len(sources) + [HELD] * 2,
            out_specs=far,
            out_shape=pltpu.HBM(tokens_in.shape, LOW),
            input_output_aliases={} if grad_block is None else {4: 0},
            scratch_shapes=[
                pltpu.VMEM((C, 3 * C), LOW), pltpu.VMEM((count * IMG, 3 * C), LOW), pltpu.VMEM((count * IMG, C), LOW),
                pltpu.VMEM((count * IMG, C), F32), pltpu.VMEM((count, 1, GRID, GRID, C), LOW),
                pltpu.SemaphoreType.DMA, pltpu.SemaphoreType.DMA((count, 3)), pltpu.SemaphoreType.DMA((count,)),
            ],
            compiler_params=whole(16),
            cost_estimate=pl.CostEstimate(flops=int(4e8 * count), bytes_accessed=2000000, transcendentals=0),
            name="input_grad",
        )(*sources, vectors, back)

    vec_grad = jnp.concatenate([sums_input, sums_attend[:, :C], sums_attend[:, 2 * C :], sums_mlp[4:]], axis=0)
    if direct:
        vec_grad, table_grad, far_got[0], *near_got = tie(vec_grad, table_grad, far_got[0], *near_got)
        near_stays, near_goes = plane_sum(near_stays, near_got)
        near_goes[0], packed_grad = tie(near_goes[0], packed_grad)
        near_got = sent(near_goes, LINE)
        grad_block = input_piece(0, 2, packed_grad, None)
        grad_block, *near_got = tie(grad_block, *near_got)
        near_grad, far_grad, spare = pl.pallas_call(
            functools.partial(finish_body, patches),
            out_shape=[sds((depth, C), F32), sds((2 * depth, C), F32), sds((24, C), F32)],
            compiler_params=whole(2),
            name="finish",
        )(near_stays, far_stays, vec_grad, table_grad, *near_got, *far_got)
        spare = spare + passed(spare, CORE)
        for masks, first, last in ((PLANE, 2, 4), (LINE, 4, 5)):
            spare, packed_grad = tie(spare, packed_grad)
            one, two, three = spread(spare, masks)
            grad_block = input_piece(first, last, packed_grad, grad_block)
            grad_block, one, two, three = tie(grad_block, one, two, three)
            spare = (spare + one) + (two + three)
    else:
        grad_block = input_piece(0, MICRO, packed_grad, None)
        near_grad, far_grad = share_plain(near_keep, near_send) / patches, share_plain(far_keep, far_send) / patches
        squares = jnp.sum(near_grad * near_grad) + jnp.sum(far_grad * far_grad)
        vec_grad, table_grad, squares = lax.psum((vec_grad, table_grad, squares), BOTH)
        gap = jnp.zeros((6, C // 2 - REL), F32)
        table_grad = jnp.concatenate([table_grad[:6] / patches, gap, table_grad[6:] / patches, gap], axis=1)
        spare = jnp.concatenate([vec_grad / patches, table_grad, jnp.broadcast_to(squares, (6, C))], axis=0)

    olds = (
        qkv_weight, proj_weight.T, fc1_weight, fc2_weight.T, vectors, rel_table.T,
        qkv_first, proj_first.T, fc1_first, fc2_first.T, vectors_first, table_first.T,
        qkv_second, proj_second.T, fc1_second, fc2_second.T, vectors_second, table_second.T,
    )
    shapes = [sds((1, 1), F32)] + [sds(olds[index].shape, F32) for index in range(6) for _ in range(3)]
    news = pl.pallas_call(
        adam_body,
        out_shape=shapes,
        scratch_shapes=[pltpu.VMEM((NH, REL), F32)],
        compiler_params=whole(8),
        name="adam",
    )(near_grad, far_grad, spare, *olds)
    turned = [new.T if index // 3 in (1, 3, 5) else new for index, new in enumerate(news[1:])]
    return (block_out, grad_block, news[0][0, 0], *turned)


def solution(mesh):
    sizes = (mesh.shape["tok"], mesh.shape["head"])
    weights = (P(None, "tok", "head"), P("head", "tok"), P("tok", "head"), P("head", "tok"), P(), P())
    images = P(None, ("tok", "head"), None, None, None)
    return jax.shard_map(
        lambda *args: body(sizes, *args),
        mesh=mesh,
        in_specs=(images, images, P(None, "tok", None), P(None, "tok", None)) + weights * 3,
        out_specs=(images, images, P()) + tuple(spec for spec in weights for _ in range(3)),
        check_vma=False,
    )
```

```python
import functools
import math

import jax
import jax.numpy as jnp
import numpy as np
from jax import lax
from jax.experimental import pallas as pl
from jax.experimental.pallas import tpu as pltpu
from jax.sharding import PartitionSpec as P

C = 384
NH = 12
HD = 32
FF = 1536
WS = 7
SHIFT = 3
STEP = 10
GRID = 14
CELLS = WS * WS
REL = (2 * WS - 1) ** 2
MICRO = 5

WIN = 64
IMG = 4 * WIN
PAD = 16 * GRID
ROWS = MICRO * IMG
GROUP = 4
GROUPS = NH // GROUP
LANES = GROUP * HD
BLOCKS = 32
PIECE = 48
EARLY = 16
TALL, WIDE = 320, 256

EPS_NORM = 1e-05
BETA_ONE = 0.9
BETA_TWO = 0.999
ADAM_EPS = 1e-08
RATE_MATRIX = 0.08
RATE_VECTOR = 1.0
DECAY_MATRIX = 0.05
CLIP_NORM = 0.05
NEG_FILL = -1e30
HIGH = lax.Precision.HIGHEST
LOW = jnp.bfloat16
F32 = jnp.float32
NEVER = 99.0
BOTH = ("tok", "head")
MASKS = (16, 8, 2, 4, 1)
CORE, PLANE, LINE = 1, (2, 4, 6), (16, 8, 24)
PIECES = 8
ME, SLOT, IMAGE = 0, 1, 2


def swap_bits(position):
    return sum((position & mask) // mask << bit for bit, mask in enumerate(MASKS))


def block_at(place):
    return sum(((place >> bit) & 1) * mask for bit, mask in enumerate(MASKS))


def window_tables():
    cell = np.arange(WIN)
    real = cell < CELLS
    rolled_row = np.stack([WS * (w // 2) + cell // WS for w in range(4)])
    rolled_col = np.stack([WS * (w % 2) + cell % WS for w in range(4)])
    source_row = (rolled_row + SHIFT) % GRID
    source_col = (rolled_col + SHIFT) % GRID

    def band(position):
        return np.where(position < GRID - WS, 0, np.where(position < GRID - SHIFT, 1, 2))

    label_row = (rolled_row + SHIFT) % GRID
    label_col = (rolled_col + SHIFT) % GRID
    region = 3 * band(label_row) + band(label_col)
    label_row = (label_row + SHIFT) % GRID
    label_col = (label_col + SHIFT) % GRID
    deal = np.zeros((IMG, PAD), np.float32)
    for w in range(4):
        for c in range(CELLS):
            deal[w * WIN + c, 16 * source_row[w, c] + source_col[w, c]] = 1.0
    place = np.full((2, IMG, 128), NEVER, np.float32)
    place[0] = np.where(real[None], source_row, NEVER).reshape(IMG, 1)
    place[1] = np.where(real[None], source_col, NEVER).reshape(IMG, 1)
    reach = np.full((2, 2, WIN, 128), NEVER, np.float32)
    for pair in range(2):
        for side in range(2):
            w = 2 * pair + side
            same = (region[w][:, None] == region[w][None, :]) & real[:, None] & real[None, :]
            for kind, source in enumerate((label_row, label_col)):
                far = np.where(same, np.maximum(source[w][:, None], source[w][None, :]), NEVER)
                far = np.where(np.eye(WIN, dtype=bool) & real[:, None], -1.0, far)
                reach[pair, kind, :, side * WIN : (side + 1) * WIN] = far
    offset = (2 * WS - 1) * (cell // WS) + cell % WS
    shifts = [int(value) for value in offset[:CELLS]]
    wanted = np.where(real, offset + REL // 2, -1)
    lookup = (np.arange(256)[:, None] == np.concatenate([wanted, wanted])[None, :]).astype(np.float32)
    heads = (np.arange(LANES)[None, :] // HD == np.arange(GROUP)[:, None]).astype(np.float32)
    heads = np.repeat(np.concatenate([heads, heads], axis=1), WIN, axis=0)
    return deal, place, reach, lookup, heads, shifts


DEAL, PLACE, REACH, LOOKUP, HEADS, SHIFTS = window_tables()


def dot_nn(a, b):
    return lax.dot_general(a, b, (((1,), (0,)), ((), ())), preferred_element_type=F32)


def dot_nt(a, b):
    return lax.dot_general(a, b, (((1,), (1,)), ((), ())), preferred_element_type=F32)


def dot_tn(a, b):
    return lax.dot_general(a, b, (((0,), (0,)), ((), ())), preferred_element_type=F32)


def turned(a, eye):
    return dot_nt(eye, a).astype(LOW)


def identity():
    row = lax.broadcasted_iota(jnp.int32, (128, 128), 0)
    return jnp.where(row == lax.broadcasted_iota(jnp.int32, (128, 128), 1), 1.0, 0.0).astype(LOW)


def norm_parts(rows):
    average = jnp.mean(rows, axis=-1, keepdims=True)
    centered = rows - average
    inverse = lax.rsqrt(jnp.mean(centered * centered, axis=-1, keepdims=True) + EPS_NORM)
    return centered * inverse, inverse


def norm_back(gradient, normed, inverse, gain):
    scaled = gradient * gain
    return inverse * (
        scaled
        - jnp.mean(scaled, axis=-1, keepdims=True)
        - normed * jnp.mean(scaled * normed, axis=-1, keepdims=True)
    )


def gelu_parts(pre_act):
    below = 0.5 + 0.5 * lax.erf(pre_act * 2.0 ** (-0.5))
    return below, jnp.exp(-0.5 * pre_act * pre_act) * (2.0 * math.pi) ** (-0.5)


SCALARS = pl.BlockSpec(memory_space=pltpu.SMEM)
HELD = pl.BlockSpec(memory_space=pltpu.VMEM)


def call(body, outs, inputs, name, limit=16, scratch=(), flops=1e9, scalars=0, fetched=0, stored=0):
    inputs = list(inputs)
    remote = slice(scalars, scalars + fetched)
    inputs[remote] = [pltpu.with_memory_space_constraint(array, pltpu.HBM) for array in inputs[remote]]
    far = pl.BlockSpec(memory_space=pltpu.HBM)
    return pl.pallas_call(
        body,
        in_specs=[SCALARS] * scalars + [far] * fetched + [HELD] * (len(inputs) - scalars - fetched),
        out_specs=[far] * stored + [HELD] * (len(outs) - stored),
        out_shape=[
            pltpu.HBM(shape, dtype) if index < stored else jax.ShapeDtypeStruct(shape, dtype)
            for index, (shape, dtype) in enumerate(outs)
        ],
        scratch_shapes=list(scratch),
        compiler_params=whole(limit),
        cost_estimate=pl.CostEstimate(flops=int(flops), bytes_accessed=4000000, transcendentals=0),
        name=name,
    )(*inputs)


def image_rows(image):
    return pl.ds(pl.multiple_of(image * IMG, IMG), IMG)


def whole(limit):
    return pltpu.CompilerParams(vmem_limit_bytes=limit * 1024 * 1024)


def sds(shape, dtype):
    return jax.ShapeDtypeStruct(shape, dtype)


def streamed(*arrays):
    return [pltpu.with_memory_space_constraint(array, pltpu.HBM) for array in arrays]


def row_mask(place_ref, table_ref, extent_ref, route_ref, image):
    parts = []
    own = table_ref[IMAGE]
    for w in range(4):
        rows = slice(w * WIN, (w + 1) * WIN)
        high = jnp.where(route_ref[own, w, image] >= 0, extent_ref[own, 0, image], -1).astype(F32)
        wide = extent_ref[own, 1, image].astype(F32)
        inside = (place_ref[0, rows] < high) & (place_ref[1, rows] < wide)
        parts.append(jnp.where(inside, 1.0, 0.0))
    return jnp.concatenate(parts, axis=0)


def pack_body(qkv_ref, proj_ref, fc1_ref, fc2_ref, near_ref, far_ref):
    depth = fc1_ref.shape[0]
    early = near_ref.shape[0] - depth
    near_ref[:depth] = jnp.concatenate([qkv_ref[0], qkv_ref[1], qkv_ref[2], proj_ref[...]], axis=1).astype(LOW)
    near_ref[depth:] = fc1_ref[:early].astype(LOW)
    far_ref[: depth - early] = fc1_ref[early:].astype(LOW)
    far_ref[depth - early :] = fc2_ref[...].astype(LOW)


def first_sum_body(keep_ref, got_ref, stays_ref, *goes_refs):
    stays_ref[...] = keep_ref[:4].astype(F32) + got_ref[:4].astype(F32)
    for index, goes in enumerate(goes_refs):
        at = 4 * (index + 1)
        goes[...] = (keep_ref[at : at + 4].astype(F32) + got_ref[at : at + 4].astype(F32)).astype(LOW)


def plane_sum_body(stays_ref, *refs):
    got, (rest, *goes) = refs[:3], refs[3:]
    for at in range(4):
        total = stays_ref[at : at + 1] + got[0][at : at + 1].astype(F32)
        total = total + (got[1][at : at + 1].astype(F32) + got[2][at : at + 1].astype(F32))
        if at == 0:
            rest[...] = total
        else:
            goes[at - 1][...] = total.astype(LOW)


def finish_body(patches, near_ref, far_ref, vec_ref, table_ref, *refs):
    near_got, far_got, (near_grad, far_grad, spare) = refs[:3], refs[3:6], refs[6:]
    squares = jnp.zeros((1, 1), F32)
    for stays, got, target in ((near_ref, near_got, near_grad), (far_ref, far_got, far_grad)):
        total = stays[0] + got[0][0].astype(F32) + (got[1][0].astype(F32) + got[2][0].astype(F32))
        total = total * (1.0 / patches)
        target[...] = total
        squares = squares + jnp.sum(jnp.sum(total * total, axis=1, keepdims=True), axis=0, keepdims=True)
    spare[0:12] = vec_ref[...] * (1.0 / patches)
    spare[12:24] = jnp.broadcast_to(squares, (12, C))
    spare[12:18, :REL] = table_ref[: NH // 2] * (1.0 / patches)
    spare[12:18, C // 2 : C // 2 + REL] = table_ref[NH // 2 :] * (1.0 / patches)


def three_parts(values):
    first = values.astype(LOW).astype(F32)
    second = (values - first).astype(LOW).astype(F32)
    return jnp.concatenate([first, second, values - first - second], axis=0)


def fetch(pairs, sems):
    copies = [pltpu.make_async_copy(source, target, sems.at[index]) for index, (source, target) in enumerate(pairs)]
    for copy in copies:
        copy.start()
    return copies


def deal_rows(source, deal, pad, image):
    for r in range(GRID):
        pad[image, 16 * r : 16 * r + GRID, :] = source[image, 0, r]
    return dot_nn(deal[...], pad[image])


def prep_body(
    table_hbm, lookup_hbm, vec_hbm, deal_hbm, tok_hbm, x_hbm, unit_hbm, n_ref, bias_ref,
    table, lookup, vec, deal, tok, x_all, unit_all, padded, pad, sems, out_sems
):
    copies = fetch(
        ((table_hbm, table), (lookup_hbm, lookup), (vec_hbm, vec), (deal_hbm, deal), (tok_hbm, tok)), sems
    )
    padded[...] = jnp.zeros_like(padded)
    pad[...] = jnp.zeros_like(pad)
    bias_ref[...] = jnp.zeros_like(bias_ref)
    copies[0].wait()
    padded[:NH, :REL] = table[...]
    parts = three_parts(padded[...])
    moved = [pltpu.roll(parts, shift, 1) if shift else parts for shift in SHIFTS]
    copies[1].wait()
    spread = dot_nn(jnp.concatenate(moved, axis=0).astype(LOW), lookup[...])
    for k in range(CELLS):
        rows = spread[48 * k : 48 * k + 48]
        bias_ref[pl.ds(k, NH, stride=WIN), :] = (rows[:16] + (rows[16:32] + rows[32:]))[:NH]
    for copy in copies[2:]:
        copy.wait()
    stores, made = [], []
    for image in range(MICRO):
        at = slice(image * IMG, (image + 1) * IMG)
        made.append(deal_rows(tok, deal, pad, image))
        x_all[at, :] = made[-1].astype(LOW)
        stores.append(pltpu.make_async_copy(x_all.at[at], x_hbm.at[at], out_sems.at[image, 0]))
        stores[-1].start()
    for image in range(MICRO):
        at = slice(image * IMG, (image + 1) * IMG)
        unit, _ = norm_parts(made[image])
        unit_all[:, at] = unit.astype(LOW).T
        stores.append(pltpu.make_async_copy(unit_all.at[:, at], unit_hbm.at[:, at], out_sems.at[image, 1]))
        stores[-1].start()
        n_ref[at, :] = (unit * vec[0:1] + vec[1:2]).astype(LOW)
    for store in stores:
        store.wait()


def prep_grad_body(deal_hbm, cot_hbm, g_ref, turned_ref, deal, cot, pad, sems):
    copies = fetch(((deal_hbm, deal), (cot_hbm, cot)), sems)
    pad[...] = jnp.zeros_like(pad)
    for copy in copies:
        copy.wait()
    for image in range(MICRO):
        at = slice(image * IMG, (image + 1) * IMG)
        rows = deal_rows(cot, deal, pad, image).astype(LOW)
        g_ref[at, :] = rows
        turned_ref[:, at] = rows.T


def table_body(sums_ref, lookup_ref, table_ref, padded):
    padded[...] = jnp.zeros_like(padded)
    slabs = []
    for k in range(CELLS):
        padded[:NH, :] = sums_ref[pl.ds(k, NH, stride=WIN), :]
        slabs.append(three_parts(padded[...]))
    made = dot_nt(jnp.concatenate(slabs, axis=0).astype(LOW), lookup_ref[...])
    total = jnp.zeros((16, 256), F32)
    for k, shift in enumerate(SHIFTS):
        rows = made[48 * k : 48 * k + 48]
        rows = rows[:16] + (rows[16:32] + rows[32:])
        total = total + (pltpu.roll(rows, 256 - shift, 1) if shift else rows)
    table_ref[...] = total[:NH, :REL]


def put_back(rows, back_ref, target, image):
    grid = dot_nn(back_ref[...], rows.astype(LOW)).astype(LOW)
    for r in range(GRID):
        target[image, 0, r] = grid[16 * r : 16 * r + GRID]


def spread_keys(part, heads_ref):
    wide = jnp.concatenate([part[:WIN], part[WIN:]], axis=1)
    return jnp.concatenate([wide] * GROUP, axis=0) * heads_ref[...]


def spread_rows(part):
    zero = jnp.zeros((WIN, LANES), part.dtype)
    top = jnp.concatenate([part[:WIN], zero], axis=1)
    return jnp.concatenate([top, jnp.concatenate([zero, part[WIN:]], axis=1)], axis=0)


def own_rows(product):
    return jnp.concatenate([product[:WIN, :LANES], product[WIN:, LANES:]], axis=0)


def own_keys(product, heads_ref):
    kept = product * heads_ref[...].astype(F32)
    total = kept[:WIN]
    for h in range(1, GROUP):
        total = total + kept[h * WIN : (h + 1) * WIN]
    return jnp.concatenate([total[:, :LANES], total[:, LANES:]], axis=0)


def attend_body(
    direct, table_ref, extent_ref, route_ref, n_ref, vec_ref, bias_ref, reach_ref, place_ref, heads_ref, *refs,
):
    near_refs, (packed_ref, soft_ref, attn_ref, wq_ref, wp_ref, parts) = refs[:PIECES], refs[PIECES:]
    for j in range(BLOCKS):
        at = table_ref[ME] ^ block_at(j) if direct else (j % 8) * 4 + j // 8
        row = at // 4 * PIECE if not direct else pl.multiple_of((at >> 2) * PIECE, PIECE)
        parts[at & 3, pl.ds(row, PIECE), :] = near_refs[j // 4][j % 4, :PIECE]
    for w in range(3):
        wq_ref[:, w * C : (w + 1) * C] = jnp.concatenate([parts[h, :, w * 96 : (w + 1) * 96] for h in range(4)], axis=1)
    wp_ref[...] = jnp.concatenate([parts[h, :, 288:] for h in range(4)], axis=1)

    @pl.loop(0, MICRO)
    def _(image):
        at_image = image_rows(image)
        made = dot_nn(n_ref[at_image, :], wq_ref[...])
        packed_ref[at_image, :C] = (made[:, :C] + vec_ref[2:3]).astype(LOW)
        packed_ref[at_image, C : 2 * C] = made[:, C : 2 * C].astype(LOW)
        packed_ref[at_image, 2 * C :] = (made[:, 2 * C :] + vec_ref[3:4]).astype(LOW)
        mask = row_mask(place_ref, table_ref, extent_ref, route_ref, image)
        high = extent_ref[table_ref[IMAGE], 0, image].astype(F32)
        wide = extent_ref[table_ref[IMAGE], 1, image].astype(F32)
        eye = identity()
        units = [(pair, g) for pair in range(2) for g in range(GROUPS)]
        at_pair = [pl.ds(pl.multiple_of(image * IMG + pair * 2 * WIN, 2 * WIN), 2 * WIN) for pair in range(2)]
        raws = []
        for pair, g in units:
            at = g * LANES
            queries = packed_ref[at_pair[pair], at : at + LANES]
            keys = packed_ref[at_pair[pair], C + at : C + at + LANES]
            raws.append(dot_nt(spread_keys(keys, heads_ref), spread_rows(queries)))
        softs = []
        for (pair, g), raw in zip(units, raws):
            allowed = (reach_ref[pair, 0] < high) & (reach_ref[pair, 1] < wide)
            raw = (raw * HD ** (-0.5) + bias_ref[g]).reshape(GROUP, WIN, 128)
            scores = jnp.where(allowed[None], raw, NEG_FILL)
            exponent = jnp.exp(scores - jnp.max(scores, axis=1, keepdims=True))
            soft = exponent * (1.0 / jnp.sum(exponent, axis=1, keepdims=True))
            soft = soft.reshape(GROUP * WIN, 128).astype(LOW)
            soft_ref[image, pair * GROUPS + g] = soft
            softs.append(soft)
        softs = [turned(soft, eye) for soft in softs]
        for (pair, g), soft in zip(units, softs):
            at = g * LANES
            values = packed_ref[at_pair[pair], 2 * C + at : 2 * C + at + LANES]
            result = own_rows(dot_nn(soft, spread_keys(values, heads_ref)))
            rows = slice(pair * 2 * WIN, (pair + 1) * 2 * WIN)
            attn_ref[at_pair[pair], at : at + LANES] = (result * mask[rows]).astype(LOW)


def middle_body(attn_ref, x_ref, wp_ref, vec_ref, middle_ref, n_ref, turned_ref):
    for image in range(MICRO):
        at = slice(image * IMG, (image + 1) * IMG)
        middle = x_ref[at, :].astype(F32) + dot_nt(attn_ref[at, :], wp_ref[...]) + vec_ref[4:5]
        middle_ref[at, :] = middle
        unit, _ = norm_parts(middle)
        normed = (unit * vec_ref[5:6] + vec_ref[6:7]).astype(LOW)
        n_ref[at, :] = normed
        turned_ref[:, at] = normed.T


def mlp_body(
    direct, table_ref, middle_ref, n_ref, g_ref, vec_ref, *refs,
):
    near_refs, far_refs, refs = refs[:PIECES], refs[PIECES : 2 * PIECES], refs[2 * PIECES :]
    (hidden_ref, grad_hidden_ref, grad_ref, sums_ref, w2_ref, w1, bias, bias_sum) = refs
    for j in range(BLOCKS):
        at = table_ref[ME] ^ block_at(j) if direct else (j % 8) * 4 + j // 8
        row = at // 4 * PIECE if not direct else pl.multiple_of((at >> 2) * PIECE, PIECE)
        col = at % 4 * C if not direct else pl.multiple_of((at & 3) * C, C)
        w1[pl.ds(row, EARLY), pl.ds(col, C)] = near_refs[j // 4][j % 4, PIECE:]
        w1[pl.ds(row + EARLY, PIECE - EARLY), pl.ds(col, C)] = far_refs[j // 4][j % 4, : PIECE - EARLY]
        w2_ref[pl.ds(row, PIECE), pl.ds(col, C)] = far_refs[j // 4][j % 4, PIECE - EARLY :]
    for r in range(4):
        bias[:, r * C : (r + 1) * C] = vec_ref[8 + r : 9 + r]
    sums_ref[...] = jnp.zeros_like(sums_ref)

    bias_sum[...] = jnp.zeros_like(bias_sum)
    for part in range(FF // WIDE):
        cols = slice(part * WIDE, (part + 1) * WIDE)
        for block in range(ROWS // TALL):
            at = slice(block * TALL, (block + 1) * TALL)
            pre_act = dot_nn(n_ref[at, :], w1[:, cols]) + bias[:, cols]
            grad_post = dot_nn(g_ref[at, :], w2_ref[:, cols])
            below, density = gelu_parts(pre_act)
            hidden_ref[at, cols] = (pre_act * below).astype(LOW)
            grad_pre = grad_post * (below + pre_act * density)
            grad_hidden_ref[at, cols] = grad_pre.astype(LOW)
            bias_sum[:, cols] += jnp.sum(grad_pre, axis=0, keepdims=True)
    for block in range(ROWS // TALL):
        at = slice(block * TALL, (block + 1) * TALL)
        back = dot_nt(grad_hidden_ref[at, :], w1[...])
        unit, inverse = norm_parts(middle_ref[at, :])
        g = g_ref[at, :].astype(F32)
        grad_middle = g + norm_back(back, unit, inverse, vec_ref[5:6])
        grad_ref[at, :] = grad_middle
        sums_ref[4:5] += jnp.sum(grad_middle, axis=0, keepdims=True)
        sums_ref[5:6] += jnp.sum(back * unit, axis=0, keepdims=True)
        sums_ref[6:7] += jnp.sum(back, axis=0, keepdims=True)
        sums_ref[7:8] += jnp.sum(g, axis=0, keepdims=True)
    for r in range(4):
        sums_ref[8 + r : 9 + r] = bias_sum[:, r * C : (r + 1) * C]


def place_of(direct, table_ref, t, h):
    if not direct:
        return h * 8 + t
    return table_ref[SLOT] ^ swap_bits(4 * t) ^ ((h & 1) * 16 + (h >> 1) * 4)


def mlp_weights_body(direct, table_ref, n_turned, g_turned, hidden_ref, grad_hidden_ref, keep_ref, send_ref, early_ref, made, first, second):
    for part in range(3):
        cols = slice(part * 2 * WIDE, (part + 1) * 2 * WIDE)
        first[:, cols] = dot_nn(n_turned[...], grad_hidden_ref[:, cols]).astype(LOW)
        second[:, cols] = dot_nn(g_turned[...], hidden_ref[:, cols]).astype(LOW)
    for h in range(4):
        cols = slice(h * C, (h + 1) * C)
        for t in range(8):
            at = place_of(direct, table_ref, t, h)
            early_ref[at] = first[t * PIECE : t * PIECE + EARLY, cols]
            made[at, : PIECE - EARLY] = first[t * PIECE + EARLY : (t + 1) * PIECE, cols]
            made[at, PIECE - EARLY :] = second[t * PIECE : (t + 1) * PIECE, cols]
    keep_ref[...] = made[: BLOCKS // 2]
    send_ref[...] = made[BLOCKS // 2 :]


def output_body(first, last, hidden_ref, w2_ref, middle_ref, vec_ref, back_ref, *refs):
    out_hbm, made, sems = refs[(first > 0) :]
    rows = []
    for image in range(first, last):
        at = slice(image * IMG, (image + 1) * IMG)
        rows.append((middle_ref[at, :] + dot_nt(hidden_ref[at, :], w2_ref[...]) + vec_ref[7:8]).astype(LOW))
    stores = []
    for index, low in enumerate(rows):
        put_back(low, back_ref, made, index)
        stores.append(pltpu.make_async_copy(made.at[index], out_hbm.at[first + index], sems.at[index]))
        stores[-1].start()
    for store in stores:
        store.wait()


def attend_back_body(
    table_ref, extent_ref, route_ref, grad_ref, packed_ref, soft_ref, wp_ref, place_ref, heads_ref,
    packed_grad_ref, grad_low_ref, bias_sum_ref, sums_ref,
):
    bias_sum_ref[...] = jnp.zeros_like(bias_sum_ref)
    sums_ref[...] = jnp.zeros_like(sums_ref)

    @pl.loop(0, MICRO, unroll=True)
    def _(image):
        at_image = image_rows(image)
        grad_low = grad_ref[at_image, :].astype(LOW)
        grad_low_ref[at_image, :] = grad_low
        mask = row_mask(place_ref, table_ref, extent_ref, route_ref, image)
        grad_attn = dot_nn(grad_low, wp_ref[...])
        grad_attn = (grad_attn * jnp.concatenate([mask] * 3, axis=1)).astype(LOW)
        eye = identity()
        units = [(pair, g) for pair in range(2) for g in range(GROUPS)]
        at_pair = [pl.ds(pl.multiple_of(image * IMG + pair * 2 * WIN, 2 * WIN), 2 * WIN) for pair in range(2)]
        incomings, grad_softs = [], []
        for pair, g in units:
            at = g * LANES
            values = packed_ref[at_pair[pair], 2 * C + at : 2 * C + at + LANES]
            incomings.append(spread_rows(grad_attn[pair * 2 * WIN : (pair + 1) * 2 * WIN, at : at + LANES]))
            grad_softs.append(dot_nt(spread_keys(values, heads_ref), incomings[-1]))
        grads = []
        for (pair, g), grad_soft in zip(units, grad_softs):
            soft = soft_ref[image, pair * GROUPS + g].astype(F32)
            joint = (soft * grad_soft).reshape(GROUP, WIN, 128)
            inner = jnp.sum(joint, axis=1, keepdims=True)
            grad_scores = (joint - soft.reshape(GROUP, WIN, 128) * inner).reshape(GROUP * WIN, 128)
            grads.append(grad_scores.astype(LOW))
            bias_sum_ref[g] += grads[-1].astype(F32)
        values_made = [dot_nn(soft_ref[image, pair * GROUPS + g], incoming) for (pair, g), incoming in zip(units, incomings)]
        turns = [turned(grad, eye) for grad in grads]
        keys_made, queries_made = [], []
        for (pair, g), grad, turn in zip(units, grads, turns):
            at = g * LANES
            queries = packed_ref[at_pair[pair], at : at + LANES]
            keys = packed_ref[at_pair[pair], C + at : C + at + LANES]
            keys_made.append(dot_nn(grad, spread_rows(queries)))
            queries_made.append(dot_nn(turn, spread_keys(keys, heads_ref)))
        for (pair, g), grad_values, grad_keys, grad_queries in zip(units, values_made, keys_made, queries_made):
            at = g * LANES
            rows = at_pair[pair]
            packed_grad_ref[rows, at : at + LANES] = (own_rows(grad_queries) * HD ** (-0.5)).astype(LOW)
            packed_grad_ref[rows, C + at : C + at + LANES] = (own_keys(grad_keys, heads_ref) * HD ** (-0.5)).astype(LOW)
            packed_grad_ref[rows, 2 * C + at : 2 * C + at + LANES] = own_keys(grad_values, heads_ref).astype(LOW)
        sums_ref[...] += jnp.sum(packed_grad_ref[at_image, :].astype(F32), axis=0, keepdims=True)


def attend_weights_body(
    direct, table_ref, unit_turned, grad_low_ref, packed_grad_ref, attn_ref, wq_ref, sums_ref, vec_ref, early_ref,
    keep_ref, send_ref, norm_ref, made,
):
    turned_vec = vec_ref[...].T
    gain, shift = turned_vec[:, 0:1], turned_vec[:, 1:2]
    parts = []
    gain_grad = jnp.zeros((C, 1), F32)
    shift_grad = jnp.zeros((C, 1), F32)
    for w in range(3):
        cols = slice(w * C, (w + 1) * C)
        product = dot_nn(unit_turned[...], packed_grad_ref[:, cols])
        weight, sums = wq_ref[:, cols].astype(F32), sums_ref[:, cols]
        parts.append((product * gain + shift * sums).astype(LOW))
        gain_grad = gain_grad + jnp.sum(product * weight, axis=1, keepdims=True)
        shift_grad = shift_grad + jnp.sum(weight * sums, axis=1, keepdims=True)
    norm_ref[0:1] = jnp.broadcast_to(gain_grad, (C, 128)).T[0:1]
    norm_ref[1:2] = jnp.broadcast_to(shift_grad, (C, 128)).T[0:1]
    parts.append(dot_nn(grad_low_ref[...].T, attn_ref[...]).astype(LOW))
    for h in range(4):
        block = jnp.concatenate([part[:, h * 96 : (h + 1) * 96] for part in parts], axis=1)
        for t in range(8):
            at = place_of(direct, table_ref, t, h)
            made[at, :PIECE] = block[t * PIECE : (t + 1) * PIECE]
            made[at, PIECE:] = early_ref[at]
    keep_ref[...] = made[: BLOCKS // 2]
    send_ref[...] = made[BLOCKS // 2 :]


def input_body(first, last, *refs):
    wq_hbm, packed_grad_hbm, x_hbm, grad_hbm = refs[:4]
    refs = refs[4 + (first > 0) :]
    vec_ref, back_ref, out_hbm, wq, packed_grad, x_all, grad_all, made, wq_sem, sems, out_sems = refs
    images = range(last - first)
    whole_copy = pltpu.make_async_copy(wq_hbm, wq, wq_sem)
    whole_copy.start()
    copies = []
    for image in images:
        source_at = slice((first + image) * IMG, (first + image + 1) * IMG)
        at = slice(image * IMG, (image + 1) * IMG)
        for index, (source, target) in enumerate(((packed_grad_hbm, packed_grad), (x_hbm, x_all), (grad_hbm, grad_all))):
            copies.append(pltpu.make_async_copy(source.at[source_at], target.at[at], sems.at[image, index]))
            copies[-1].start()
    whole_copy.wait()
    stores = []
    for image in images:
        at = slice(image * IMG, (image + 1) * IMG)
        for copy in copies[3 * image : 3 * image + 3]:
            copy.wait()
        back = dot_nt(packed_grad[at, :], wq[...])
        unit, inverse = norm_parts(x_all[at, :].astype(F32))
        rows = grad_all[at, :] + norm_back(back, unit, inverse, vec_ref[0:1])
        put_back(rows, back_ref, made, image)
        stores.append(pltpu.make_async_copy(made.at[image], out_hbm.at[first + image], out_sems.at[image]))
        stores[-1].start()
    for store in stores:
        store.wait()


def adam_update(weight, first, second, gradient, rate, decay):
    first_new = BETA_ONE * first + (1.0 - BETA_ONE) * gradient
    second_new = BETA_TWO * second + (1.0 - BETA_TWO) * gradient * gradient
    first_hat = first_new / (1.0 - BETA_ONE**STEP)
    second_hat = second_new / (1.0 - BETA_TWO**STEP)
    weight_new = weight * (1.0 - rate * decay) - rate * first_hat / (jnp.sqrt(second_hat) + ADAM_EPS)
    return (weight_new, first_new, second_new)


def adam_body(near_ref, far_ref, spare_ref, *refs):
    olds, news, turned, hidden_grad = refs[:18], refs[18:-2], refs[-2], refs[-1]
    depth = hidden_grad.shape[0]
    early = near_ref.shape[0] - depth
    hidden_grad[:early] = near_ref[depth:]
    hidden_grad[early:] = far_ref[: depth - early]
    turned[: NH // 2] = spare_ref[12:18, :REL]
    turned[NH // 2 :] = spare_ref[12:18, C // 2 : C // 2 + REL]
    vec, table = spare_ref[0:12], turned[...]
    total = spare_ref[18:19, 0:1]
    total = total + jnp.sum(jnp.sum(vec * vec, axis=1, keepdims=True), axis=0, keepdims=True)
    total = total + jnp.sum(jnp.sum(table * table, axis=1, keepdims=True), axis=0, keepdims=True)
    grad_norm = jnp.sqrt(total)
    factor = jnp.minimum(1.0, CLIP_NORM / (grad_norm + 1e-06))
    news[0][...] = grad_norm
    grads = [None, near_ref[:depth, 288:], hidden_grad[...], far_ref[depth - early :], vec, table]
    for index in range(6):
        weight, first, second = olds[index], olds[6 + index], olds[12 + index]
        rate, decay = (RATE_MATRIX, DECAY_MATRIX) if index < 4 else (RATE_VECTOR, 0.0)
        for w in range(3 if index == 0 else 1):
            pick = (w,) if index == 0 else (Ellipsis,)
            gradient = near_ref[:depth, w * 96 : (w + 1) * 96] if index == 0 else grads[index]
            made = adam_update(weight[pick], first[pick], second[pick], gradient * factor, rate, decay)
            for kind in range(3):
                news[1 + 3 * index + kind][pick] = made[kind]


def body(
    mesh_sizes, tokens_in, cotangent, route, extent, qkv_weight, proj_weight, fc1_weight, fc2_weight, vectors, rel_table,
    qkv_first, proj_first, fc1_first, fc2_first, vectors_first, table_first,
    qkv_second, proj_second, fc1_second, fc2_second, vectors_second, table_second,
):
    toks, heads = mesh_sizes
    devices = toks * heads
    direct = toks == 8 and heads == 4
    micro = tokens_in.shape[0]
    patches = micro * devices * GRID * GRID
    head_at = lax.axis_index("head")
    me = lax.axis_index("tok") * heads + head_at
    numbers = [me, swap_bits(me), head_at]
    extents, routes = extent.transpose(1, 2, 0), route.transpose(1, 2, 0)

    def tie(*arrays):
        return lax.optimization_barrier(arrays)

    def passed(rows, mask):
        return lax.ppermute(rows, BOTH, [(i, i ^ mask) for i in range(devices)])

    depth = fc1_weight.shape[0]
    early = depth * EARLY // PIECE
    near, far = pl.pallas_call(
        pack_body, out_shape=(sds((depth + early, C), LOW), sds((2 * depth - early, C), LOW)), compiler_params=whole(8), name="pack"
    )(*streamed(qkv_weight, proj_weight.T, fc1_weight, fc2_weight.T))

    def gather_plain(piece):
        spread = lax.all_gather(lax.all_gather(piece, "tok", axis=0), "head", axis=0)
        return spread.reshape(BLOCKS, PIECE, C)

    def plain_pieces(near, far):
        one = gather_plain(near[:depth])
        two = gather_plain(jnp.concatenate([near[depth:], far[: depth - early]], axis=0))
        three = gather_plain(far[depth - early :])
        near = jnp.concatenate([one, two[:, :EARLY]], axis=1)
        far = jnp.concatenate([two[:, EARLY:], three], axis=1)
        return [[array[at : at + 4] for at in range(0, BLOCKS, 4)] for array in (near, far)]

    def share_plain(blocks):
        blocks = blocks.reshape(devices, depth, C).astype(F32)
        part = lax.psum_scatter(blocks, "head", scatter_dimension=0, tiled=True)
        return lax.psum_scatter(part, "tok", scatter_dimension=0, tiled=True)[0]

    def plain_shares(near, far):
        one, three = share_plain(near[:, :PIECE]), share_plain(far[:, PIECE - EARLY :])
        two = share_plain(jnp.concatenate([near[:, PIECE:], far[:, : PIECE - EARLY]], axis=1))
        near = jnp.concatenate([one, two[:early]], axis=0) / patches
        return near, jnp.concatenate([two[early:], three], axis=0) / patches

    def join(*arrays):
        return jnp.concatenate(arrays, axis=0)

    def first_sum(keep, got):
        shape = (4,) + keep.shape[1:]
        stays, *goes = pl.pallas_call(
            first_sum_body, out_shape=[sds(shape, F32)] + [sds(shape, LOW)] * 3, compiler_params=whole(2), name="first_sum"
        )(keep, got)
        return stays, goes

    def plane_sum(stays, got):
        shape = (1,) + stays.shape[1:]
        rest, *goes = pl.pallas_call(
            plane_sum_body, out_shape=[sds(shape, F32)] + [sds(shape, LOW)] * 3, compiler_params=whole(2), name="plane_sum"
        )(stays, *got)
        return rest, goes

    def spread(rows, masks):
        return [passed(rows, mask) for mask in masks]

    def sent(parts, masks):
        return [passed(part, mask) for part, mask in zip(parts, masks)]

    back = jnp.asarray(DEAL.T, LOW)
    deal = jnp.asarray(DEAL, LOW)
    lookup = jnp.asarray(LOOKUP, LOW)
    place = jnp.asarray(PLACE)
    reach = jnp.asarray(REACH)
    heads_low = jnp.asarray(HEADS, LOW)
    whole_images = pltpu.VMEM((MICRO, 1, GRID, GRID, C), LOW)

    def prepare(tokens, values):
        x_rows, unit_turned, n_rows, bias = call(
            prep_body,
            [((ROWS, C), LOW), ((C, ROWS), LOW), ((ROWS, C), LOW), ((NH * WIN, 128), F32)],
            (values.T, lookup, vectors, deal, tokens),
            "prep",
            scratch=[
                pltpu.VMEM((NH, REL), F32), pltpu.VMEM((256, 128), LOW), pltpu.VMEM((12, C), F32), pltpu.VMEM((IMG, PAD), LOW),
                whole_images, pltpu.VMEM((ROWS, C), LOW), pltpu.VMEM((C, ROWS), LOW), pltpu.VMEM((16, 256), F32),
                pltpu.VMEM((MICRO, PAD, C), LOW), pltpu.SemaphoreType.DMA((5,)), pltpu.SemaphoreType.DMA((MICRO, 2)),
            ],
            flops=1e9,
            fetched=5,
            stored=2,
        )
        return x_rows, unit_turned, n_rows, bias.reshape(GROUPS, GROUP * WIN, 128)

    def prepare_grad(cotangents):
        return call(
            prep_grad_body,
            [((ROWS, C), LOW), ((C, ROWS), LOW)],
            (deal, cotangents),
            "prep_grad",
            limit=8,
            scratch=[pltpu.VMEM((IMG, PAD), LOW), whole_images, pltpu.VMEM((MICRO, PAD, C), LOW), pltpu.SemaphoreType.DMA((2,))],
            fetched=2,
        )

    if direct:
        near = near[None]
        near_got, far_got = spread(near, LINE), spread(far[None], LINE)
        near_all = join(near, *near_got)
        near_all = [near_all] + spread(near_all, PLANE)
        far_all = join(far[None], *far_got)
        far_all, tokens, rel_bias, *numbers = tie(far_all, tokens_in, rel_table, *numbers)
        table = jnp.stack(numbers).astype(jnp.int32)
        x_rows, unit_turned, n_rows, bias = prepare(tokens, rel_bias)
        bias, table, n_rows, *near_all = tie(bias, table, n_rows, *near_all)
        far_all, near_all[0] = tie(far_all, near_all[0])
        near_all = near_all + [passed(piece, CORE) for piece in near_all]
        far_got = [far_all] + spread(far_all, PLANE)
    else:
        table = jnp.stack(numbers).astype(jnp.int32)
        x_rows, unit_turned, n_rows, bias = prepare(tokens_in, rel_table)
        near_all, far_all = plain_pieces(near, far)

    packed, soft, attn, w_qkv, w_proj = call(
        functools.partial(attend_body, direct),
        [
            ((ROWS, 3 * C), LOW), ((MICRO, 2 * GROUPS, GROUP * WIN, 128), LOW), ((ROWS, C), LOW), ((C, 3 * C), LOW), ((C, C), LOW),
        ],
        (table, extents, routes, n_rows, vectors, bias, reach, place, heads_low, *near_all),
        "attend",
        limit=8,
        scratch=[pltpu.VMEM((4, C, C), LOW)],
        flops=8e9,
        scalars=3,
    )

    middle, n_two, n_turned = call(
        middle_body, [((ROWS, C), F32), ((ROWS, C), LOW), ((C, ROWS), LOW)], (attn, x_rows, w_proj, vectors), "middle", limit=4
    )

    late = cotangent
    if direct:
        middle, late, *far_got = tie(middle, late, *far_got)
        far_core = [passed(piece, CORE) for piece in far_got]
    g_rows, g_turned = prepare_grad(late)
    if direct:
        g_rows, *far_core = tie(g_rows, *far_core)
        far_all = far_got + far_core

    hidden, grad_hidden, grad_middle, sums_mlp, w_fc2 = call(
        functools.partial(mlp_body, direct),
        [((ROWS, FF), LOW), ((ROWS, FF), LOW), ((ROWS, C), F32), ((12, C), F32), ((C, FF), LOW)],
        (table, middle, n_two, g_rows, vectors, *near_all, *far_all),
        "mlp",
        limit=8,
        scratch=[pltpu.VMEM((C, FF), LOW), pltpu.VMEM((1, FF), F32), pltpu.VMEM((1, FF), F32)],
        flops=10e9,
        scalars=1,
    )

    half = BLOCKS // 2
    far_keep, far_send, early_grad = call(
        functools.partial(mlp_weights_body, direct),
        [((half, 2 * PIECE - EARLY, C), LOW)] * 2 + [((BLOCKS, EARLY, C), LOW)],
        (table, n_turned, g_turned, hidden, grad_hidden),
        "mlp_weights",
        limit=14,
        scratch=[
            pltpu.VMEM((BLOCKS, 2 * PIECE - EARLY, C), LOW), pltpu.VMEM((C, FF), LOW), pltpu.VMEM((C, FF), LOW),
        ],
        flops=4e9,
        scalars=1,
    )

    if direct:
        far_got = passed(far_send, CORE)

    def output_piece(first, last, hidden, block_out):
        far = pl.BlockSpec(memory_space=pltpu.HBM)
        before = [] if block_out is None else [pltpu.with_memory_space_constraint(block_out, pltpu.HBM)]
        return pl.pallas_call(
            functools.partial(output_body, first, last),
            in_specs=[HELD] * 5 + [far] * len(before),
            out_specs=far,
            out_shape=pltpu.HBM(tokens_in.shape, LOW),
            input_output_aliases={} if block_out is None else {5: 0},
            scratch_shapes=[pltpu.VMEM((last - first, 1, GRID, GRID, C), LOW), pltpu.SemaphoreType.DMA((last - first,))],
            compiler_params=whole(8),
            cost_estimate=pl.CostEstimate(flops=int(4e8 * (last - first)), bytes_accessed=2000000, transcendentals=0),
            name="output",
        )(hidden, w_fc2, middle, vectors, back, *before)

    early_images = 3 if direct else MICRO
    block_out = output_piece(0, early_images, hidden, None)

    if direct:
        block_out, far_got, grad_middle, hidden = tie(block_out, far_got, grad_middle, hidden)
        far_stays, far_goes = first_sum(far_keep, far_got)
        far_got = sent(far_goes, PLANE)

    packed_grad, grad_low, bias_sum, sums_attend = call(
        attend_back_body,
        [((ROWS, 3 * C), LOW), ((ROWS, C), LOW), ((GROUPS, GROUP * WIN, 128), F32), ((1, 3 * C), F32)],
        (table, extents, routes, grad_middle, packed, soft, w_proj, place, heads_low),
        "attend_back",
        limit=6,
        flops=8e9,
        scalars=3,
    )

    vec_square = jnp.concatenate([vectors, jnp.zeros((4, C), F32)], axis=0)
    near_keep, near_send, sums_input = call(
        functools.partial(attend_weights_body, direct),
        [((half, PIECE + EARLY, C), LOW)] * 2 + [((2, C), F32)],
        (table, unit_turned, grad_low, packed_grad, attn, w_qkv, sums_attend, vec_square, early_grad),
        "attend_weights",
        limit=8,
        scratch=[pltpu.VMEM((BLOCKS, PIECE + EARLY, C), LOW)],
        flops=2e9,
        scalars=1,
    )

    if direct:
        near_send, *far_got = tie(near_send, *far_got)
        near_send, hidden = tie(near_send, hidden)
        near_got = passed(near_send, CORE)
        block_out = output_piece(early_images, MICRO, hidden, block_out)
        near_got, block_out = tie(near_got, block_out)
        near_stays, near_goes = first_sum(near_keep, near_got)
        near_goes[0], bias_sum = tie(near_goes[0], bias_sum)
        near_got = sent(near_goes, PLANE)

    (table_grad,) = call(
        table_body,
        [((NH, REL), F32)],
        (bias_sum.reshape(NH * WIN, 128), lookup),
        "table_grad",
        limit=8,
        scratch=[pltpu.VMEM((16, 128), F32)],
        flops=1e8,
    )
    if direct:
        table_grad, *far_got = tie(table_grad, *far_got)
        far_stays, far_goes = plane_sum(far_stays, far_got)
        far_got = sent(far_goes, LINE)

    def input_piece(first, last, packed_grad, grad_block):
        count = last - first
        sources = [pltpu.with_memory_space_constraint(array, pltpu.HBM) for array in (w_qkv, packed_grad, x_rows, grad_middle)]
        sources += [] if grad_block is None else [pltpu.with_memory_space_constraint(grad_block, pltpu.HBM)]
        far = pl.BlockSpec(memory_space=pltpu.HBM)
        return pl.pallas_call(
            functools.partial(input_body, first, last),
            in_specs=[far] * len(sources) + [HELD] * 2,
            out_specs=far,
            out_shape=pltpu.HBM(tokens_in.shape, LOW),
            input_output_aliases={} if grad_block is None else {4: 0},
            scratch_shapes=[
                pltpu.VMEM((C, 3 * C), LOW), pltpu.VMEM((count * IMG, 3 * C), LOW), pltpu.VMEM((count * IMG, C), LOW),
                pltpu.VMEM((count * IMG, C), F32), pltpu.VMEM((count, 1, GRID, GRID, C), LOW),
                pltpu.SemaphoreType.DMA, pltpu.SemaphoreType.DMA((count, 3)), pltpu.SemaphoreType.DMA((count,)),
            ],
            compiler_params=whole(16),
            cost_estimate=pl.CostEstimate(flops=int(4e8 * count), bytes_accessed=2000000, transcendentals=0),
            name="input_grad",
        )(*sources, vectors, back)

    vec_grad = jnp.concatenate([sums_input, sums_attend[:, :C], sums_attend[:, 2 * C :], sums_mlp[4:]], axis=0)
    if direct:
        vec_grad, table_grad, far_got[0], *near_got = tie(vec_grad, table_grad, far_got[0], *near_got)
        near_stays, near_goes = plane_sum(near_stays, near_got)
        near_goes[0], packed_grad = tie(near_goes[0], packed_grad)
        near_got = sent(near_goes, LINE)
        grad_block = input_piece(0, 2, packed_grad, None)
        grad_block, *near_got = tie(grad_block, *near_got)
        near_grad, far_grad, spare = pl.pallas_call(
            functools.partial(finish_body, patches),
            out_shape=[sds((depth + early, C), F32), sds((2 * depth - early, C), F32), sds((24, C), F32)],
            compiler_params=whole(2),
            name="finish",
        )(near_stays, far_stays, vec_grad, table_grad, *near_got, *far_got)
        spare = spare + passed(spare, CORE)
        for masks, first, last in ((PLANE, 2, 4), (LINE, 4, 5)):
            spare, packed_grad = tie(spare, packed_grad)
            one, two, three = spread(spare, masks)
            grad_block = input_piece(first, last, packed_grad, grad_block)
            grad_block, one, two, three = tie(grad_block, one, two, three)
            spare = (spare + one) + (two + three)
    else:
        grad_block = input_piece(0, MICRO, packed_grad, None)
        near_grad, far_grad = plain_shares(join(near_keep, near_send), join(far_keep, far_send))
        squares = jnp.sum(near_grad * near_grad) + jnp.sum(far_grad * far_grad)
        vec_grad, table_grad, squares = lax.psum((vec_grad, table_grad, squares), BOTH)
        gap = jnp.zeros((6, C // 2 - REL), F32)
        table_grad = jnp.concatenate([table_grad[:6] / patches, gap, table_grad[6:] / patches, gap], axis=1)
        spare = jnp.concatenate([vec_grad / patches, table_grad, jnp.broadcast_to(squares, (6, C))], axis=0)

    olds = (
        qkv_weight, proj_weight.T, fc1_weight, fc2_weight.T, vectors, rel_table.T,
        qkv_first, proj_first.T, fc1_first, fc2_first.T, vectors_first, table_first.T,
        qkv_second, proj_second.T, fc1_second, fc2_second.T, vectors_second, table_second.T,
    )
    shapes = [sds((1, 1), F32)] + [sds(olds[index].shape, F32) for index in range(6) for _ in range(3)]
    news = pl.pallas_call(
        adam_body,
        out_shape=shapes,
        scratch_shapes=[pltpu.VMEM((NH, REL), F32), pltpu.VMEM((depth, C), F32)],
        compiler_params=whole(8),
        name="adam",
    )(near_grad, far_grad, spare, *olds)
    turned = [new.T if index // 3 in (1, 3, 5) else new for index, new in enumerate(news[1:])]
    return (block_out, grad_block, news[0][0, 0], *turned)


def solution(mesh):
    sizes = (mesh.shape["tok"], mesh.shape["head"])
    weights = (P(None, "tok", "head"), P("head", "tok"), P("tok", "head"), P("head", "tok"), P(), P())
    images = P(None, ("tok", "head"), None, None, None)
    return jax.shard_map(
        lambda *args: body(sizes, *args),
        mesh=mesh,
        in_specs=(images, images, P(None, "tok", None), P(None, "tok", None)) + weights * 3,
        out_specs=(images, images, P()) + tuple(spec for spec in weights for _ in range(3)),
        check_vma=False,
    )
```

```python
import functools
import math

import jax
import jax.numpy as jnp
import numpy as np
from jax import lax
from jax.experimental import pallas as pl
from jax.experimental.pallas import tpu as pltpu
from jax.sharding import PartitionSpec as P

C = 384
NH = 12
HD = 32
FF = 1536
WS = 7
SHIFT = 3
STEP = 10
GRID = 14
CELLS = WS * WS
REL = (2 * WS - 1) ** 2
MICRO = 5

WIN = 64
IMG = 4 * WIN
PAD = 16 * GRID
ROWS = MICRO * IMG
GROUP = 4
GROUPS = NH // GROUP
LANES = GROUP * HD
BLOCKS = 32
PIECE = 48
EARLY = 16
TALL, WIDE = 320, 256

EPS_NORM = 1e-05
BETA_ONE = 0.9
BETA_TWO = 0.999
ADAM_EPS = 1e-08
RATE_MATRIX = 0.08
RATE_VECTOR = 1.0
DECAY_MATRIX = 0.05
CLIP_NORM = 0.05
NEG_FILL = -1e30
HIGH = lax.Precision.HIGHEST
LOW = jnp.bfloat16
F32 = jnp.float32
NEVER = 99.0
BOTH = ("tok", "head")
MASKS = (16, 8, 2, 4, 1)
CORE, PLANE, LINE = 1, (2, 4, 6), (16, 8, 24)
PIECES = 8
ME, SLOT, IMAGE = 0, 1, 2


def swap_bits(position):
    return sum((position & mask) // mask << bit for bit, mask in enumerate(MASKS))


def block_at(place):
    return sum(((place >> bit) & 1) * mask for bit, mask in enumerate(MASKS))


def window_tables():
    cell = np.arange(WIN)
    real = cell < CELLS
    rolled_row = np.stack([WS * (w // 2) + cell // WS for w in range(4)])
    rolled_col = np.stack([WS * (w % 2) + cell % WS for w in range(4)])
    source_row = (rolled_row + SHIFT) % GRID
    source_col = (rolled_col + SHIFT) % GRID

    def band(position):
        return np.where(position < GRID - WS, 0, np.where(position < GRID - SHIFT, 1, 2))

    label_row = (rolled_row + SHIFT) % GRID
    label_col = (rolled_col + SHIFT) % GRID
    region = 3 * band(label_row) + band(label_col)
    label_row = (label_row + SHIFT) % GRID
    label_col = (label_col + SHIFT) % GRID
    deal = np.zeros((IMG, PAD), np.float32)
    for w in range(4):
        for c in range(CELLS):
            deal[w * WIN + c, 16 * source_row[w, c] + source_col[w, c]] = 1.0
    place = np.full((2, IMG, 128), NEVER, np.float32)
    place[0] = np.where(real[None], source_row, NEVER).reshape(IMG, 1)
    place[1] = np.where(real[None], source_col, NEVER).reshape(IMG, 1)
    reach = np.full((2, 2, WIN, 128), NEVER, np.float32)
    for pair in range(2):
        for side in range(2):
            w = 2 * pair + side
            same = (region[w][:, None] == region[w][None, :]) & real[:, None] & real[None, :]
            for kind, source in enumerate((label_row, label_col)):
                far = np.where(same, np.maximum(source[w][:, None], source[w][None, :]), NEVER)
                far = np.where(np.eye(WIN, dtype=bool) & real[:, None], -1.0, far)
                reach[pair, kind, :, side * WIN : (side + 1) * WIN] = far
    offset = (2 * WS - 1) * (cell // WS) + cell % WS
    shifts = [int(value) for value in offset[:CELLS]]
    wanted = np.where(real, offset + REL // 2, -1)
    lookup = (np.arange(256)[:, None] == np.concatenate([wanted, wanted])[None, :]).astype(np.float32)
    heads = (np.arange(LANES)[None, :] // HD == np.arange(GROUP)[:, None]).astype(np.float32)
    heads = np.repeat(np.concatenate([heads, heads], axis=1), WIN, axis=0)
    return deal, place, reach, lookup, heads, shifts


DEAL, PLACE, REACH, LOOKUP, HEADS, SHIFTS = window_tables()


def dot_nn(a, b):
    return lax.dot_general(a, b, (((1,), (0,)), ((), ())), preferred_element_type=F32)


def dot_nt(a, b):
    return lax.dot_general(a, b, (((1,), (1,)), ((), ())), preferred_element_type=F32)


def dot_tn(a, b):
    return lax.dot_general(a, b, (((0,), (0,)), ((), ())), preferred_element_type=F32)


def turned(a, eye):
    return dot_nt(eye, a).astype(LOW)


def identity():
    row = lax.broadcasted_iota(jnp.int32, (128, 128), 0)
    return jnp.where(row == lax.broadcasted_iota(jnp.int32, (128, 128), 1), 1.0, 0.0).astype(LOW)


def norm_parts(rows):
    average = jnp.mean(rows, axis=-1, keepdims=True)
    centered = rows - average
    inverse = lax.rsqrt(jnp.mean(centered * centered, axis=-1, keepdims=True) + EPS_NORM)
    return centered * inverse, inverse


def norm_back(gradient, normed, inverse, gain):
    scaled = gradient * gain
    return inverse * (
        scaled
        - jnp.mean(scaled, axis=-1, keepdims=True)
        - normed * jnp.mean(scaled * normed, axis=-1, keepdims=True)
    )


def gelu_parts(pre_act):
    below = 0.5 + 0.5 * lax.erf(pre_act * 2.0 ** (-0.5))
    return below, jnp.exp(-0.5 * pre_act * pre_act) * (2.0 * math.pi) ** (-0.5)


SCALARS = pl.BlockSpec(memory_space=pltpu.SMEM)
HELD = pl.BlockSpec(memory_space=pltpu.VMEM)


def call(body, outs, inputs, name, limit=16, scratch=(), flops=1e9, scalars=0, fetched=0, stored=0):
    inputs = list(inputs)
    remote = slice(scalars, scalars + fetched)
    inputs[remote] = [pltpu.with_memory_space_constraint(array, pltpu.HBM) for array in inputs[remote]]
    far = pl.BlockSpec(memory_space=pltpu.HBM)
    return pl.pallas_call(
        body,
        in_specs=[SCALARS] * scalars + [far] * fetched + [HELD] * (len(inputs) - scalars - fetched),
        out_specs=[far] * stored + [HELD] * (len(outs) - stored),
        out_shape=[
            pltpu.HBM(shape, dtype) if index < stored else jax.ShapeDtypeStruct(shape, dtype)
            for index, (shape, dtype) in enumerate(outs)
        ],
        scratch_shapes=list(scratch),
        compiler_params=whole(limit),
        cost_estimate=pl.CostEstimate(flops=int(flops), bytes_accessed=4000000, transcendentals=0),
        name=name,
    )(*inputs)


def image_rows(image):
    return pl.ds(pl.multiple_of(image * IMG, IMG), IMG)


def whole(limit):
    return pltpu.CompilerParams(vmem_limit_bytes=limit * 1024 * 1024)


def sds(shape, dtype):
    return jax.ShapeDtypeStruct(shape, dtype)


def streamed(*arrays):
    return [pltpu.with_memory_space_constraint(array, pltpu.HBM) for array in arrays]


def row_mask(place_ref, table_ref, extent_ref, route_ref, image):
    parts = []
    own = table_ref[IMAGE]
    for w in range(4):
        rows = slice(w * WIN, (w + 1) * WIN)
        high = jnp.where(route_ref[own, w, image] >= 0, extent_ref[own, 0, image], -1).astype(F32)
        wide = extent_ref[own, 1, image].astype(F32)
        inside = (place_ref[0, rows] < high) & (place_ref[1, rows] < wide)
        parts.append(jnp.where(inside, 1.0, 0.0))
    return jnp.concatenate(parts, axis=0)


def pack_body(qkv_ref, proj_ref, fc1_ref, fc2_ref, near_ref, far_ref):
    depth = fc1_ref.shape[0]
    early = near_ref.shape[0] - depth
    near_ref[:depth] = jnp.concatenate([qkv_ref[0], qkv_ref[1], qkv_ref[2], proj_ref[...]], axis=1).astype(LOW)
    near_ref[depth:] = fc1_ref[:early].astype(LOW)
    far_ref[: depth - early] = fc1_ref[early:].astype(LOW)
    far_ref[depth - early :] = fc2_ref[...].astype(LOW)


def first_sum_body(keep_ref, got_ref, stays_ref, *goes_refs):
    stays_ref[...] = keep_ref[:4].astype(F32) + got_ref[:4].astype(F32)
    for index, goes in enumerate(goes_refs):
        at = 4 * (index + 1)
        goes[...] = (keep_ref[at : at + 4].astype(F32) + got_ref[at : at + 4].astype(F32)).astype(LOW)


def plane_sum_body(stays_ref, *refs):
    got, (rest, *goes) = refs[:3], refs[3:]
    for at in range(4):
        total = stays_ref[at : at + 1] + got[0][at : at + 1].astype(F32)
        total = total + (got[1][at : at + 1].astype(F32) + got[2][at : at + 1].astype(F32))
        if at == 0:
            rest[...] = total
        else:
            goes[at - 1][...] = total.astype(LOW)


def finish_body(patches, near_ref, far_ref, vec_ref, table_ref, *refs):
    near_got, far_got, (near_grad, far_grad, spare) = refs[:3], refs[3:6], refs[6:]
    squares = jnp.zeros((1, 1), F32)
    for stays, got, target in ((near_ref, near_got, near_grad), (far_ref, far_got, far_grad)):
        total = stays[0] + got[0][0].astype(F32) + (got[1][0].astype(F32) + got[2][0].astype(F32))
        total = total * (1.0 / patches)
        target[...] = total
        squares = squares + jnp.sum(jnp.sum(total * total, axis=1, keepdims=True), axis=0, keepdims=True)
    spare[0:12] = vec_ref[...] * (1.0 / patches)
    spare[12:24] = jnp.broadcast_to(squares, (12, C))
    spare[12:18, :REL] = table_ref[: NH // 2] * (1.0 / patches)
    spare[12:18, C // 2 : C // 2 + REL] = table_ref[NH // 2 :] * (1.0 / patches)


def three_parts(values):
    first = values.astype(LOW).astype(F32)
    second = (values - first).astype(LOW).astype(F32)
    return jnp.concatenate([first, second, values - first - second], axis=0)


def fetch(pairs, sems):
    copies = [pltpu.make_async_copy(source, target, sems.at[index]) for index, (source, target) in enumerate(pairs)]
    for copy in copies:
        copy.start()
    return copies


def deal_rows(source, deal, pad, image):
    for r in range(GRID):
        pad[image, 16 * r : 16 * r + GRID, :] = source[image, 0, r]
    return dot_nn(deal[...], pad[image])


def prep_body(
    table_hbm, lookup_hbm, vec_hbm, deal_hbm, tok_hbm, x_hbm, unit_hbm, n_ref, bias_ref,
    table, lookup, vec, deal, tok, x_all, unit_all, padded, pad, sems, out_sems
):
    copies = fetch(
        ((table_hbm, table), (lookup_hbm, lookup), (vec_hbm, vec), (deal_hbm, deal), (tok_hbm, tok)), sems
    )
    padded[...] = jnp.zeros_like(padded)
    pad[...] = jnp.zeros_like(pad)
    bias_ref[...] = jnp.zeros_like(bias_ref)
    copies[0].wait()
    padded[:NH, :REL] = table[...]
    parts = three_parts(padded[...])
    moved = [pltpu.roll(parts, shift, 1) if shift else parts for shift in SHIFTS]
    copies[1].wait()
    spread = dot_nn(jnp.concatenate(moved, axis=0).astype(LOW), lookup[...])
    for k in range(CELLS):
        rows = spread[48 * k : 48 * k + 48]
        bias_ref[pl.ds(k, NH, stride=WIN), :] = (rows[:16] + (rows[16:32] + rows[32:]))[:NH]
    for copy in copies[2:]:
        copy.wait()
    stores, made = [], []
    for image in range(MICRO):
        at = slice(image * IMG, (image + 1) * IMG)
        made.append(deal_rows(tok, deal, pad, image))
        x_all[at, :] = made[-1].astype(LOW)
        stores.append(pltpu.make_async_copy(x_all.at[at], x_hbm.at[at], out_sems.at[image, 0]))
        stores[-1].start()
    for image in range(MICRO):
        at = slice(image * IMG, (image + 1) * IMG)
        unit, _ = norm_parts(made[image])
        unit_all[:, at] = unit.astype(LOW).T
        stores.append(pltpu.make_async_copy(unit_all.at[:, at], unit_hbm.at[:, at], out_sems.at[image, 1]))
        stores[-1].start()
        n_ref[at, :] = (unit * vec[0:1] + vec[1:2]).astype(LOW)
    for store in stores:
        store.wait()


def prep_grad_body(deal_hbm, cot_hbm, g_ref, turned_ref, deal, cot, pad, sems):
    copies = fetch(((deal_hbm, deal), (cot_hbm, cot)), sems)
    pad[...] = jnp.zeros_like(pad)
    for copy in copies:
        copy.wait()
    for image in range(MICRO):
        at = slice(image * IMG, (image + 1) * IMG)
        rows = deal_rows(cot, deal, pad, image).astype(LOW)
        g_ref[at, :] = rows
        turned_ref[:, at] = rows.T


def table_body(sums_ref, lookup_ref, table_ref, padded):
    padded[...] = jnp.zeros_like(padded)
    slabs = []
    for k in range(CELLS):
        padded[:NH, :] = sums_ref[pl.ds(k, NH, stride=WIN), :]
        slabs.append(three_parts(padded[...]))
    made = dot_nt(jnp.concatenate(slabs, axis=0).astype(LOW), lookup_ref[...])
    total = jnp.zeros((16, 256), F32)
    for k, shift in enumerate(SHIFTS):
        rows = made[48 * k : 48 * k + 48]
        rows = rows[:16] + (rows[16:32] + rows[32:])
        total = total + (pltpu.roll(rows, 256 - shift, 1) if shift else rows)
    table_ref[...] = total[:NH, :REL]


def put_back(rows, back_ref, target, image):
    grid = dot_nn(back_ref[...], rows.astype(LOW)).astype(LOW)
    for r in range(GRID):
        target[image, 0, r] = grid[16 * r : 16 * r + GRID]


def spread_keys(part, heads_ref):
    wide = jnp.concatenate([part[:WIN], part[WIN:]], axis=1)
    return jnp.concatenate([wide] * GROUP, axis=0) * heads_ref[...]


def spread_rows(part):
    zero = jnp.zeros((WIN, LANES), part.dtype)
    top = jnp.concatenate([part[:WIN], zero], axis=1)
    return jnp.concatenate([top, jnp.concatenate([zero, part[WIN:]], axis=1)], axis=0)


def own_rows(product):
    return jnp.concatenate([product[:WIN, :LANES], product[WIN:, LANES:]], axis=0)


def own_keys(product, heads_ref):
    kept = product * heads_ref[...].astype(F32)
    total = kept[:WIN]
    for h in range(1, GROUP):
        total = total + kept[h * WIN : (h + 1) * WIN]
    return jnp.concatenate([total[:, :LANES], total[:, LANES:]], axis=0)


def attend_body(
    direct, table_ref, extent_ref, route_ref, n_ref, vec_ref, bias_ref, reach_ref, place_ref, heads_ref, *refs,
):
    near_refs, (packed_ref, soft_ref, attn_ref, wq_ref, wp_ref, parts) = refs[:PIECES], refs[PIECES:]
    for j in range(BLOCKS):
        at = table_ref[ME] ^ block_at(j) if direct else (j % 8) * 4 + j // 8
        row = at // 4 * PIECE if not direct else pl.multiple_of((at >> 2) * PIECE, PIECE)
        parts[at & 3, pl.ds(row, PIECE), :] = near_refs[j // 4][j % 4, :PIECE]
    for w in range(3):
        wq_ref[:, w * C : (w + 1) * C] = jnp.concatenate([parts[h, :, w * 96 : (w + 1) * 96] for h in range(4)], axis=1)
    wp_ref[...] = jnp.concatenate([parts[h, :, 288:] for h in range(4)], axis=1)

    @pl.loop(0, MICRO, unroll=True)
    def _(image):
        at_image = image_rows(image)
        made = dot_nn(n_ref[at_image, :], wq_ref[...])
        packed_ref[at_image, :C] = (made[:, :C] + vec_ref[2:3]).astype(LOW)
        packed_ref[at_image, C : 2 * C] = made[:, C : 2 * C].astype(LOW)
        packed_ref[at_image, 2 * C :] = (made[:, 2 * C :] + vec_ref[3:4]).astype(LOW)
        mask = row_mask(place_ref, table_ref, extent_ref, route_ref, image)
        high = extent_ref[table_ref[IMAGE], 0, image].astype(F32)
        wide = extent_ref[table_ref[IMAGE], 1, image].astype(F32)
        eye = identity()
        units = [(pair, g) for pair in range(2) for g in range(GROUPS)]
        at_pair = [pl.ds(pl.multiple_of(image * IMG + pair * 2 * WIN, 2 * WIN), 2 * WIN) for pair in range(2)]
        raws = []
        for pair, g in units:
            at = g * LANES
            queries = packed_ref[at_pair[pair], at : at + LANES]
            keys = packed_ref[at_pair[pair], C + at : C + at + LANES]
            raws.append(dot_nt(spread_keys(keys, heads_ref), spread_rows(queries)))
        softs = []
        for (pair, g), raw in zip(units, raws):
            allowed = (reach_ref[pair, 0] < high) & (reach_ref[pair, 1] < wide)
            raw = (raw * HD ** (-0.5) + bias_ref[g]).reshape(GROUP, WIN, 128)
            scores = jnp.where(allowed[None], raw, NEG_FILL)
            exponent = jnp.exp(scores - jnp.max(scores, axis=1, keepdims=True))
            soft = exponent * (1.0 / jnp.sum(exponent, axis=1, keepdims=True))
            soft = soft.reshape(GROUP * WIN, 128).astype(LOW)
            soft_ref[image, pair * GROUPS + g] = soft
            softs.append(soft)
        softs = [turned(soft, eye) for soft in softs]
        for (pair, g), soft in zip(units, softs):
            at = g * LANES
            values = packed_ref[at_pair[pair], 2 * C + at : 2 * C + at + LANES]
            result = own_rows(dot_nn(soft, spread_keys(values, heads_ref)))
            rows = slice(pair * 2 * WIN, (pair + 1) * 2 * WIN)
            attn_ref[at_pair[pair], at : at + LANES] = (result * mask[rows]).astype(LOW)


def middle_body(attn_ref, x_ref, wp_ref, vec_ref, middle_ref, n_ref, turned_ref):
    for image in range(MICRO):
        at = slice(image * IMG, (image + 1) * IMG)
        middle = x_ref[at, :].astype(F32) + dot_nt(attn_ref[at, :], wp_ref[...]) + vec_ref[4:5]
        middle_ref[at, :] = middle
        unit, _ = norm_parts(middle)
        normed = (unit * vec_ref[5:6] + vec_ref[6:7]).astype(LOW)
        n_ref[at, :] = normed
        turned_ref[:, at] = normed.T


def mlp_body(
    direct, table_ref, middle_ref, n_ref, g_ref, vec_ref, *refs,
):
    near_refs, far_refs, refs = refs[:PIECES], refs[PIECES : 2 * PIECES], refs[2 * PIECES :]
    (hidden_ref, grad_hidden_ref, grad_ref, sums_ref, w2_ref, w1, bias, bias_sum) = refs
    for j in range(BLOCKS):
        at = table_ref[ME] ^ block_at(j) if direct else (j % 8) * 4 + j // 8
        row = at // 4 * PIECE if not direct else pl.multiple_of((at >> 2) * PIECE, PIECE)
        col = at % 4 * C if not direct else pl.multiple_of((at & 3) * C, C)
        w1[pl.ds(row, EARLY), pl.ds(col, C)] = near_refs[j // 4][j % 4, PIECE:]
        w1[pl.ds(row + EARLY, PIECE - EARLY), pl.ds(col, C)] = far_refs[j // 4][j % 4, : PIECE - EARLY]
        w2_ref[pl.ds(row, PIECE), pl.ds(col, C)] = far_refs[j // 4][j % 4, PIECE - EARLY :]
    for r in range(4):
        bias[:, r * C : (r + 1) * C] = vec_ref[8 + r : 9 + r]
    sums_ref[...] = jnp.zeros_like(sums_ref)

    bias_sum[...] = jnp.zeros_like(bias_sum)
    for part in range(FF // WIDE):
        cols = slice(part * WIDE, (part + 1) * WIDE)
        for block in range(ROWS // TALL):
            at = slice(block * TALL, (block + 1) * TALL)
            pre_act = dot_nn(n_ref[at, :], w1[:, cols]) + bias[:, cols]
            grad_post = dot_nn(g_ref[at, :], w2_ref[:, cols])
            below, density = gelu_parts(pre_act)
            hidden_ref[at, cols] = (pre_act * below).astype(LOW)
            grad_pre = grad_post * (below + pre_act * density)
            grad_hidden_ref[at, cols] = grad_pre.astype(LOW)
            bias_sum[:, cols] += jnp.sum(grad_pre, axis=0, keepdims=True)
    for block in range(ROWS // TALL):
        at = slice(block * TALL, (block + 1) * TALL)
        back = dot_nt(grad_hidden_ref[at, :], w1[...])
        unit, inverse = norm_parts(middle_ref[at, :])
        g = g_ref[at, :].astype(F32)
        grad_middle = g + norm_back(back, unit, inverse, vec_ref[5:6])
        grad_ref[at, :] = grad_middle
        sums_ref[4:5] += jnp.sum(grad_middle, axis=0, keepdims=True)
        sums_ref[5:6] += jnp.sum(back * unit, axis=0, keepdims=True)
        sums_ref[6:7] += jnp.sum(back, axis=0, keepdims=True)
        sums_ref[7:8] += jnp.sum(g, axis=0, keepdims=True)
    for r in range(4):
        sums_ref[8 + r : 9 + r] = bias_sum[:, r * C : (r + 1) * C]


def place_of(direct, table_ref, t, h):
    if not direct:
        return h * 8 + t
    return table_ref[SLOT] ^ swap_bits(4 * t) ^ ((h & 1) * 16 + (h >> 1) * 4)


def mlp_weights_body(direct, table_ref, n_turned, g_turned, hidden_ref, grad_hidden_ref, keep_ref, send_ref, early_ref, made, first, second):
    for part in range(3):
        cols = slice(part * 2 * WIDE, (part + 1) * 2 * WIDE)
        first[:, cols] = dot_nn(n_turned[...], grad_hidden_ref[:, cols]).astype(LOW)
        second[:, cols] = dot_nn(g_turned[...], hidden_ref[:, cols]).astype(LOW)
    for h in range(4):
        cols = slice(h * C, (h + 1) * C)
        for t in range(8):
            at = place_of(direct, table_ref, t, h)
            early_ref[at] = first[t * PIECE : t * PIECE + EARLY, cols]
            made[at, : PIECE - EARLY] = first[t * PIECE + EARLY : (t + 1) * PIECE, cols]
            made[at, PIECE - EARLY :] = second[t * PIECE : (t + 1) * PIECE, cols]
    keep_ref[...] = made[: BLOCKS // 2]
    send_ref[...] = made[BLOCKS // 2 :]


def output_body(first, last, hidden_ref, w2_ref, middle_ref, vec_ref, back_ref, *refs):
    out_hbm, made, sems = refs[(first > 0) :]
    rows = []
    for image in range(first, last):
        at = slice(image * IMG, (image + 1) * IMG)
        rows.append((middle_ref[at, :] + dot_nt(hidden_ref[at, :], w2_ref[...]) + vec_ref[7:8]).astype(LOW))
    stores = []
    for index, low in enumerate(rows):
        put_back(low, back_ref, made, index)
        stores.append(pltpu.make_async_copy(made.at[index], out_hbm.at[first + index], sems.at[index]))
        stores[-1].start()
    for store in stores:
        store.wait()


def attend_back_body(
    table_ref, extent_ref, route_ref, grad_ref, packed_ref, soft_ref, wp_ref, place_ref, heads_ref,
    packed_grad_ref, grad_low_ref, bias_sum_ref, sums_ref,
):
    bias_sum_ref[...] = jnp.zeros_like(bias_sum_ref)
    sums_ref[...] = jnp.zeros_like(sums_ref)

    @pl.loop(0, MICRO, unroll=True)
    def _(image):
        at_image = image_rows(image)
        grad_low = grad_ref[at_image, :].astype(LOW)
        grad_low_ref[at_image, :] = grad_low
        mask = row_mask(place_ref, table_ref, extent_ref, route_ref, image)
        grad_attn = dot_nn(grad_low, wp_ref[...])
        grad_attn = (grad_attn * jnp.concatenate([mask] * 3, axis=1)).astype(LOW)
        eye = identity()
        units = [(pair, g) for pair in range(2) for g in range(GROUPS)]
        at_pair = [pl.ds(pl.multiple_of(image * IMG + pair * 2 * WIN, 2 * WIN), 2 * WIN) for pair in range(2)]
        incomings, grad_softs = [], []
        for pair, g in units:
            at = g * LANES
            values = packed_ref[at_pair[pair], 2 * C + at : 2 * C + at + LANES]
            incomings.append(spread_rows(grad_attn[pair * 2 * WIN : (pair + 1) * 2 * WIN, at : at + LANES]))
            grad_softs.append(dot_nt(spread_keys(values, heads_ref), incomings[-1]))
        grads = []
        for (pair, g), grad_soft in zip(units, grad_softs):
            soft = soft_ref[image, pair * GROUPS + g].astype(F32)
            joint = (soft * grad_soft).reshape(GROUP, WIN, 128)
            inner = jnp.sum(joint, axis=1, keepdims=True)
            grad_scores = (joint - soft.reshape(GROUP, WIN, 128) * inner).reshape(GROUP * WIN, 128)
            grads.append(grad_scores.astype(LOW))
            bias_sum_ref[g] += grads[-1].astype(F32)
        values_made = [dot_nn(soft_ref[image, pair * GROUPS + g], incoming) for (pair, g), incoming in zip(units, incomings)]
        turns = [turned(grad, eye) for grad in grads]
        keys_made, queries_made = [], []
        for (pair, g), grad, turn in zip(units, grads, turns):
            at = g * LANES
            queries = packed_ref[at_pair[pair], at : at + LANES]
            keys = packed_ref[at_pair[pair], C + at : C + at + LANES]
            keys_made.append(dot_nn(grad, spread_rows(queries)))
            queries_made.append(dot_nn(turn, spread_keys(keys, heads_ref)))
        for (pair, g), grad_values, grad_keys, grad_queries in zip(units, values_made, keys_made, queries_made):
            at = g * LANES
            rows = at_pair[pair]
            packed_grad_ref[rows, at : at + LANES] = (own_rows(grad_queries) * HD ** (-0.5)).astype(LOW)
            packed_grad_ref[rows, C + at : C + at + LANES] = (own_keys(grad_keys, heads_ref) * HD ** (-0.5)).astype(LOW)
            packed_grad_ref[rows, 2 * C + at : 2 * C + at + LANES] = own_keys(grad_values, heads_ref).astype(LOW)
        sums_ref[...] += jnp.sum(packed_grad_ref[at_image, :].astype(F32), axis=0, keepdims=True)


def attend_weights_body(
    direct, table_ref, unit_turned, grad_low_ref, packed_grad_ref, attn_ref, wq_ref, sums_ref, vec_ref, early_ref,
    keep_ref, send_ref, norm_ref, made,
):
    turned_vec = vec_ref[...].T
    gain, shift = turned_vec[:, 0:1], turned_vec[:, 1:2]
    parts = []
    gain_grad = jnp.zeros((C, 1), F32)
    shift_grad = jnp.zeros((C, 1), F32)
    for w in range(3):
        cols = slice(w * C, (w + 1) * C)
        product = dot_nn(unit_turned[...], packed_grad_ref[:, cols])
        weight, sums = wq_ref[:, cols].astype(F32), sums_ref[:, cols]
        parts.append((product * gain + shift * sums).astype(LOW))
        gain_grad = gain_grad + jnp.sum(product * weight, axis=1, keepdims=True)
        shift_grad = shift_grad + jnp.sum(weight * sums, axis=1, keepdims=True)
    norm_ref[0:1] = jnp.broadcast_to(gain_grad, (C, 128)).T[0:1]
    norm_ref[1:2] = jnp.broadcast_to(shift_grad, (C, 128)).T[0:1]
    parts.append(dot_nn(grad_low_ref[...].T, attn_ref[...]).astype(LOW))
    for h in range(4):
        block = jnp.concatenate([part[:, h * 96 : (h + 1) * 96] for part in parts], axis=1)
        for t in range(8):
            at = place_of(direct, table_ref, t, h)
            made[at, :PIECE] = block[t * PIECE : (t + 1) * PIECE]
            made[at, PIECE:] = early_ref[at]
    keep_ref[...] = made[: BLOCKS // 2]
    send_ref[...] = made[BLOCKS // 2 :]


def input_body(first, last, *refs):
    wq_hbm, packed_grad_hbm, x_hbm, grad_hbm = refs[:4]
    refs = refs[4 + (first > 0) :]
    vec_ref, back_ref, out_hbm, wq, packed_grad, x_all, grad_all, made, wq_sem, sems, out_sems = refs
    images = range(last - first)
    whole_copy = pltpu.make_async_copy(wq_hbm, wq, wq_sem)
    whole_copy.start()
    copies = []
    for image in images:
        source_at = slice((first + image) * IMG, (first + image + 1) * IMG)
        at = slice(image * IMG, (image + 1) * IMG)
        for index, (source, target) in enumerate(((packed_grad_hbm, packed_grad), (x_hbm, x_all), (grad_hbm, grad_all))):
            copies.append(pltpu.make_async_copy(source.at[source_at], target.at[at], sems.at[image, index]))
            copies[-1].start()
    whole_copy.wait()
    stores = []
    for image in images:
        at = slice(image * IMG, (image + 1) * IMG)
        for copy in copies[3 * image : 3 * image + 3]:
            copy.wait()
        back = dot_nt(packed_grad[at, :], wq[...])
        unit, inverse = norm_parts(x_all[at, :].astype(F32))
        rows = grad_all[at, :] + norm_back(back, unit, inverse, vec_ref[0:1])
        put_back(rows, back_ref, made, image)
        stores.append(pltpu.make_async_copy(made.at[image], out_hbm.at[first + image], out_sems.at[image]))
        stores[-1].start()
    for store in stores:
        store.wait()


def adam_update(weight, first, second, gradient, rate, decay):
    first_new = BETA_ONE * first + (1.0 - BETA_ONE) * gradient
    second_new = BETA_TWO * second + (1.0 - BETA_TWO) * gradient * gradient
    first_hat = first_new / (1.0 - BETA_ONE**STEP)
    second_hat = second_new / (1.0 - BETA_TWO**STEP)
    weight_new = weight * (1.0 - rate * decay) - rate * first_hat / (jnp.sqrt(second_hat) + ADAM_EPS)
    return (weight_new, first_new, second_new)


def adam_body(near_ref, far_ref, spare_ref, *refs):
    olds, news, turned, hidden_grad = refs[:18], refs[18:-2], refs[-2], refs[-1]
    depth = hidden_grad.shape[0]
    early = near_ref.shape[0] - depth
    hidden_grad[:early] = near_ref[depth:]
    hidden_grad[early:] = far_ref[: depth - early]
    turned[: NH // 2] = spare_ref[12:18, :REL]
    turned[NH // 2 :] = spare_ref[12:18, C // 2 : C // 2 + REL]
    vec, table = spare_ref[0:12], turned[...]
    total = spare_ref[18:19, 0:1]
    total = total + jnp.sum(jnp.sum(vec * vec, axis=1, keepdims=True), axis=0, keepdims=True)
    total = total + jnp.sum(jnp.sum(table * table, axis=1, keepdims=True), axis=0, keepdims=True)
    grad_norm = jnp.sqrt(total)
    factor = jnp.minimum(1.0, CLIP_NORM / (grad_norm + 1e-06))
    news[0][...] = grad_norm
    grads = [None, near_ref[:depth, 288:], hidden_grad[...], far_ref[depth - early :], vec, table]
    for index in range(6):
        weight, first, second = olds[index], olds[6 + index], olds[12 + index]
        rate, decay = (RATE_MATRIX, DECAY_MATRIX) if index < 4 else (RATE_VECTOR, 0.0)
        for w in range(3 if index == 0 else 1):
            pick = (w,) if index == 0 else (Ellipsis,)
            gradient = near_ref[:depth, w * 96 : (w + 1) * 96] if index == 0 else grads[index]
            made = adam_update(weight[pick], first[pick], second[pick], gradient * factor, rate, decay)
            for kind in range(3):
                news[1 + 3 * index + kind][pick] = made[kind]


def body(
    mesh_sizes, tokens_in, cotangent, route, extent, qkv_weight, proj_weight, fc1_weight, fc2_weight, vectors, rel_table,
    qkv_first, proj_first, fc1_first, fc2_first, vectors_first, table_first,
    qkv_second, proj_second, fc1_second, fc2_second, vectors_second, table_second,
):
    toks, heads = mesh_sizes
    devices = toks * heads
    direct = toks == 8 and heads == 4
    micro = tokens_in.shape[0]
    patches = micro * devices * GRID * GRID
    head_at = lax.axis_index("head")
    me = lax.axis_index("tok") * heads + head_at
    numbers = [me, swap_bits(me), head_at]
    extents, routes = extent.transpose(1, 2, 0), route.transpose(1, 2, 0)

    def tie(*arrays):
        return lax.optimization_barrier(arrays)

    def passed(rows, mask):
        return lax.ppermute(rows, BOTH, [(i, i ^ mask) for i in range(devices)])

    depth = fc1_weight.shape[0]
    early = depth * EARLY // PIECE
    near, far = pl.pallas_call(
        pack_body, out_shape=(sds((depth + early, C), LOW), sds((2 * depth - early, C), LOW)), compiler_params=whole(8), name="pack"
    )(*streamed(qkv_weight, proj_weight.T, fc1_weight, fc2_weight.T))

    def gather_plain(piece):
        spread = lax.all_gather(lax.all_gather(piece, "tok", axis=0), "head", axis=0)
        return spread.reshape(BLOCKS, PIECE, C)

    def plain_pieces(near, far):
        one = gather_plain(near[:depth])
        two = gather_plain(jnp.concatenate([near[depth:], far[: depth - early]], axis=0))
        three = gather_plain(far[depth - early :])
        near = jnp.concatenate([one, two[:, :EARLY]], axis=1)
        far = jnp.concatenate([two[:, EARLY:], three], axis=1)
        return [[array[at : at + 4] for at in range(0, BLOCKS, 4)] for array in (near, far)]

    def share_plain(blocks):
        blocks = blocks.reshape(devices, depth, C).astype(F32)
        part = lax.psum_scatter(blocks, "head", scatter_dimension=0, tiled=True)
        return lax.psum_scatter(part, "tok", scatter_dimension=0, tiled=True)[0]

    def plain_shares(near, far):
        one, three = share_plain(near[:, :PIECE]), share_plain(far[:, PIECE - EARLY :])
        two = share_plain(jnp.concatenate([near[:, PIECE:], far[:, : PIECE - EARLY]], axis=1))
        near = jnp.concatenate([one, two[:early]], axis=0) / patches
        return near, jnp.concatenate([two[early:], three], axis=0) / patches

    def join(*arrays):
        return jnp.concatenate(arrays, axis=0)

    def first_sum(keep, got):
        shape = (4,) + keep.shape[1:]
        stays, *goes = pl.pallas_call(
            first_sum_body, out_shape=[sds(shape, F32)] + [sds(shape, LOW)] * 3, compiler_params=whole(2), name="first_sum"
        )(keep, got)
        return stays, goes

    def plane_sum(stays, got):
        shape = (1,) + stays.shape[1:]
        rest, *goes = pl.pallas_call(
            plane_sum_body, out_shape=[sds(shape, F32)] + [sds(shape, LOW)] * 3, compiler_params=whole(2), name="plane_sum"
        )(stays, *got)
        return rest, goes

    def spread(rows, masks):
        return [passed(rows, mask) for mask in masks]

    def sent(parts, masks):
        return [passed(part, mask) for part, mask in zip(parts, masks)]

    back = jnp.asarray(DEAL.T, LOW)
    deal = jnp.asarray(DEAL, LOW)
    lookup = jnp.asarray(LOOKUP, LOW)
    place = jnp.asarray(PLACE)
    reach = jnp.asarray(REACH)
    heads_low = jnp.asarray(HEADS, LOW)
    whole_images = pltpu.VMEM((MICRO, 1, GRID, GRID, C), LOW)

    def prepare(tokens, values):
        x_rows, unit_turned, n_rows, bias = call(
            prep_body,
            [((ROWS, C), LOW), ((C, ROWS), LOW), ((ROWS, C), LOW), ((NH * WIN, 128), F32)],
            (values.T, lookup, vectors, deal, tokens),
            "prep",
            scratch=[
                pltpu.VMEM((NH, REL), F32), pltpu.VMEM((256, 128), LOW), pltpu.VMEM((12, C), F32), pltpu.VMEM((IMG, PAD), LOW),
                whole_images, pltpu.VMEM((ROWS, C), LOW), pltpu.VMEM((C, ROWS), LOW), pltpu.VMEM((16, 256), F32),
                pltpu.VMEM((MICRO, PAD, C), LOW), pltpu.SemaphoreType.DMA((5,)), pltpu.SemaphoreType.DMA((MICRO, 2)),
            ],
            flops=1e9,
            fetched=5,
            stored=2,
        )
        return x_rows, unit_turned, n_rows, bias.reshape(GROUPS, GROUP * WIN, 128)

    def prepare_grad(cotangents):
        return call(
            prep_grad_body,
            [((ROWS, C), LOW), ((C, ROWS), LOW)],
            (deal, cotangents),
            "prep_grad",
            limit=8,
            scratch=[pltpu.VMEM((IMG, PAD), LOW), whole_images, pltpu.VMEM((MICRO, PAD, C), LOW), pltpu.SemaphoreType.DMA((2,))],
            fetched=2,
        )

    if direct:
        near = near[None]
        near_got, far_got = spread(near, LINE), spread(far[None], LINE)
        near_all = join(near, *near_got)
        near_all = [near_all] + spread(near_all, PLANE)
        far_all = join(far[None], *far_got)
        far_all, tokens, rel_bias, *numbers = tie(far_all, tokens_in, rel_table, *numbers)
        table = jnp.stack(numbers).astype(jnp.int32)
        x_rows, unit_turned, n_rows, bias = prepare(tokens, rel_bias)
        bias, table, n_rows, *near_all = tie(bias, table, n_rows, *near_all)
        far_all, near_all[0] = tie(far_all, near_all[0])
        near_all = near_all + [passed(piece, CORE) for piece in near_all]
        far_got = [far_all] + spread(far_all, PLANE)
    else:
        table = jnp.stack(numbers).astype(jnp.int32)
        x_rows, unit_turned, n_rows, bias = prepare(tokens_in, rel_table)
        near_all, far_all = plain_pieces(near, far)

    packed, soft, attn, w_qkv, w_proj = call(
        functools.partial(attend_body, direct),
        [
            ((ROWS, 3 * C), LOW), ((MICRO, 2 * GROUPS, GROUP * WIN, 128), LOW), ((ROWS, C), LOW), ((C, 3 * C), LOW), ((C, C), LOW),
        ],
        (table, extents, routes, n_rows, vectors, bias, reach, place, heads_low, *near_all),
        "attend",
        limit=8,
        scratch=[pltpu.VMEM((4, C, C), LOW)],
        flops=8e9,
        scalars=3,
    )

    middle, n_two, n_turned = call(
        middle_body, [((ROWS, C), F32), ((ROWS, C), LOW), ((C, ROWS), LOW)], (attn, x_rows, w_proj, vectors), "middle", limit=4
    )

    late = cotangent
    if direct:
        middle, late, *far_got = tie(middle, late, *far_got)
        far_core = [passed(piece, CORE) for piece in far_got]
    g_rows, g_turned = prepare_grad(late)
    if direct:
        g_rows, *far_core = tie(g_rows, *far_core)
        far_all = far_got + far_core

    hidden, grad_hidden, grad_middle, sums_mlp, w_fc2 = call(
        functools.partial(mlp_body, direct),
        [((ROWS, FF), LOW), ((ROWS, FF), LOW), ((ROWS, C), F32), ((12, C), F32), ((C, FF), LOW)],
        (table, middle, n_two, g_rows, vectors, *near_all, *far_all),
        "mlp",
        limit=8,
        scratch=[pltpu.VMEM((C, FF), LOW), pltpu.VMEM((1, FF), F32), pltpu.VMEM((1, FF), F32)],
        flops=10e9,
        scalars=1,
    )

    half = BLOCKS // 2
    far_keep, far_send, early_grad = call(
        functools.partial(mlp_weights_body, direct),
        [((half, 2 * PIECE - EARLY, C), LOW)] * 2 + [((BLOCKS, EARLY, C), LOW)],
        (table, n_turned, g_turned, hidden, grad_hidden),
        "mlp_weights",
        limit=14,
        scratch=[
            pltpu.VMEM((BLOCKS, 2 * PIECE - EARLY, C), LOW), pltpu.VMEM((C, FF), LOW), pltpu.VMEM((C, FF), LOW),
        ],
        flops=4e9,
        scalars=1,
    )

    if direct:
        far_got = passed(far_send, CORE)

    def output_piece(first, last, hidden, block_out):
        far = pl.BlockSpec(memory_space=pltpu.HBM)
        before = [] if block_out is None else [pltpu.with_memory_space_constraint(block_out, pltpu.HBM)]
        return pl.pallas_call(
            functools.partial(output_body, first, last),
            in_specs=[HELD] * 5 + [far] * len(before),
            out_specs=far,
            out_shape=pltpu.HBM(tokens_in.shape, LOW),
            input_output_aliases={} if block_out is None else {5: 0},
            scratch_shapes=[pltpu.VMEM((last - first, 1, GRID, GRID, C), LOW), pltpu.SemaphoreType.DMA((last - first,))],
            compiler_params=whole(8),
            cost_estimate=pl.CostEstimate(flops=int(4e8 * (last - first)), bytes_accessed=2000000, transcendentals=0),
            name="output",
        )(hidden, w_fc2, middle, vectors, back, *before)

    early_images = 3 if direct else MICRO
    block_out = output_piece(0, early_images, hidden, None)

    if direct:
        block_out, far_got, grad_middle, hidden = tie(block_out, far_got, grad_middle, hidden)
        far_stays, far_goes = first_sum(far_keep, far_got)
        far_got = sent(far_goes, PLANE)

    packed_grad, grad_low, bias_sum, sums_attend = call(
        attend_back_body,
        [((ROWS, 3 * C), LOW), ((ROWS, C), LOW), ((GROUPS, GROUP * WIN, 128), F32), ((1, 3 * C), F32)],
        (table, extents, routes, grad_middle, packed, soft, w_proj, place, heads_low),
        "attend_back",
        limit=6,
        flops=8e9,
        scalars=3,
    )

    vec_square = jnp.concatenate([vectors, jnp.zeros((4, C), F32)], axis=0)
    near_keep, near_send, sums_input = call(
        functools.partial(attend_weights_body, direct),
        [((half, PIECE + EARLY, C), LOW)] * 2 + [((2, C), F32)],
        (table, unit_turned, grad_low, packed_grad, attn, w_qkv, sums_attend, vec_square, early_grad),
        "attend_weights",
        limit=8,
        scratch=[pltpu.VMEM((BLOCKS, PIECE + EARLY, C), LOW)],
        flops=2e9,
        scalars=1,
    )

    if direct:
        near_send, *far_got = tie(near_send, *far_got)
        near_send, hidden = tie(near_send, hidden)
        near_got = passed(near_send, CORE)
        block_out = output_piece(early_images, MICRO, hidden, block_out)
        near_got, block_out = tie(near_got, block_out)
        near_stays, near_goes = first_sum(near_keep, near_got)
        near_goes[0], bias_sum = tie(near_goes[0], bias_sum)
        near_got = sent(near_goes, PLANE)

    (table_grad,) = call(
        table_body,
        [((NH, REL), F32)],
        (bias_sum.reshape(NH * WIN, 128), lookup),
        "table_grad",
        limit=8,
        scratch=[pltpu.VMEM((16, 128), F32)],
        flops=1e8,
    )
    if direct:
        table_grad, *far_got = tie(table_grad, *far_got)
        far_stays, far_goes = plane_sum(far_stays, far_got)
        far_got = sent(far_goes, LINE)

    def input_piece(first, last, packed_grad, grad_block):
        count = last - first
        sources = [pltpu.with_memory_space_constraint(array, pltpu.HBM) for array in (w_qkv, packed_grad, x_rows, grad_middle)]
        sources += [] if grad_block is None else [pltpu.with_memory_space_constraint(grad_block, pltpu.HBM)]
        far = pl.BlockSpec(memory_space=pltpu.HBM)
        return pl.pallas_call(
            functools.partial(input_body, first, last),
            in_specs=[far] * len(sources) + [HELD] * 2,
            out_specs=far,
            out_shape=pltpu.HBM(tokens_in.shape, LOW),
            input_output_aliases={} if grad_block is None else {4: 0},
            scratch_shapes=[
                pltpu.VMEM((C, 3 * C), LOW), pltpu.VMEM((count * IMG, 3 * C), LOW), pltpu.VMEM((count * IMG, C), LOW),
                pltpu.VMEM((count * IMG, C), F32), pltpu.VMEM((count, 1, GRID, GRID, C), LOW),
                pltpu.SemaphoreType.DMA, pltpu.SemaphoreType.DMA((count, 3)), pltpu.SemaphoreType.DMA((count,)),
            ],
            compiler_params=whole(16),
            cost_estimate=pl.CostEstimate(flops=int(4e8 * count), bytes_accessed=2000000, transcendentals=0),
            name="input_grad",
        )(*sources, vectors, back)

    vec_grad = jnp.concatenate([sums_input, sums_attend[:, :C], sums_attend[:, 2 * C :], sums_mlp[4:]], axis=0)
    if direct:
        vec_grad, table_grad, far_got[0], *near_got = tie(vec_grad, table_grad, far_got[0], *near_got)
        near_stays, near_goes = plane_sum(near_stays, near_got)
        near_goes[0], packed_grad = tie(near_goes[0], packed_grad)
        near_got = sent(near_goes, LINE)
        grad_block = input_piece(0, 2, packed_grad, None)
        grad_block, *near_got = tie(grad_block, *near_got)
        near_grad, far_grad, spare = pl.pallas_call(
            functools.partial(finish_body, patches),
            out_shape=[sds((depth + early, C), F32), sds((2 * depth - early, C), F32), sds((24, C), F32)],
            compiler_params=whole(2),
            name="finish",
        )(near_stays, far_stays, vec_grad, table_grad, *near_got, *far_got)
        spare = spare + passed(spare, CORE)
        for masks, first, last in ((PLANE, 2, 4), (LINE, 4, 5)):
            spare, packed_grad = tie(spare, packed_grad)
            one, two, three = spread(spare, masks)
            grad_block = input_piece(first, last, packed_grad, grad_block)
            grad_block, one, two, three = tie(grad_block, one, two, three)
            spare = (spare + one) + (two + three)
    else:
        grad_block = input_piece(0, MICRO, packed_grad, None)
        near_grad, far_grad = plain_shares(join(near_keep, near_send), join(far_keep, far_send))
        squares = jnp.sum(near_grad * near_grad) + jnp.sum(far_grad * far_grad)
        vec_grad, table_grad, squares = lax.psum((vec_grad, table_grad, squares), BOTH)
        gap = jnp.zeros((6, C // 2 - REL), F32)
        table_grad = jnp.concatenate([table_grad[:6] / patches, gap, table_grad[6:] / patches, gap], axis=1)
        spare = jnp.concatenate([vec_grad / patches, table_grad, jnp.broadcast_to(squares, (6, C))], axis=0)

    olds = (
        qkv_weight, proj_weight.T, fc1_weight, fc2_weight.T, vectors, rel_table.T,
        qkv_first, proj_first.T, fc1_first, fc2_first.T, vectors_first, table_first.T,
        qkv_second, proj_second.T, fc1_second, fc2_second.T, vectors_second, table_second.T,
    )
    shapes = [sds((1, 1), F32)] + [sds(olds[index].shape, F32) for index in range(6) for _ in range(3)]
    news = pl.pallas_call(
        adam_body,
        out_shape=shapes,
        scratch_shapes=[pltpu.VMEM((NH, REL), F32), pltpu.VMEM((depth, C), F32)],
        compiler_params=whole(8),
        name="adam",
    )(near_grad, far_grad, spare, *olds)
    turned = [new.T if index // 3 in (1, 3, 5) else new for index, new in enumerate(news[1:])]
    return (block_out, grad_block, news[0][0, 0], *turned)


def solution(mesh):
    sizes = (mesh.shape["tok"], mesh.shape["head"])
    weights = (P(None, "tok", "head"), P("head", "tok"), P("tok", "head"), P("head", "tok"), P(), P())
    images = P(None, ("tok", "head"), None, None, None)
    return jax.shard_map(
        lambda *args: body(sizes, *args),
        mesh=mesh,
        in_specs=(images, images, P(None, "tok", None), P(None, "tok", None)) + weights * 3,
        out_specs=(images, images, P()) + tuple(spec for spec in weights for _ in range(3)),
        check_vma=False,
    )
```
